256 devices in a mesh: prow: 32 (over x, z), pcol: 8 (over y, core).
Axes of the slice: x: 4, y: 4, z: 8, core: 2. Of those that a mesh axis runs over, the one named last changes fastest.
Arguments:
- matrix: float32 [24, 512, 3, 4096], P(None, 'prow', None, 'pcol'), may hold values from -6 to 6
- pivots: int32 [2, 512], replicated, may hold values from 0 to 12287, as said below
- lower_inv: float32 [2, 512, 512], replicated
- upper_inv: float32 [2, 512, 512], replicated
Outputs:
- factored: float32 [24, 512, 3, 4096], P(None, 'prow', None, 'pcol')
The draws below stay inside these ranges and needn't reach their ends.
Inputs may be any that keep to these rules, and one draw needn't show every extreme that they name: pivots[k, i] is at least k * 512 + i; every panel has one entry equal to 12287, and the first panel's first row keeps its place.
All inputs are finite; a program needn't handle non-finite values.
Results may differ from the reference program's by a relative error of at most 0.00011.
Values sent between devices are 32-bit elements; how exact they have to be, the bound alone decides.
A program may use at most 64 MiB of HBM per device.

```python
import math
import jax
import jax.numpy as jnp
from jax import lax

M = 12288
NB = 512
PANELS = 2
ROWBLK = 24
COLSPAN = 4096
COLBLK = 3


def draw_pivots(key, part):
    bits_key = jax.random.fold_in(key, 21)
    pick_key = jax.random.fold_in(key, 22)
    starts = jnp.arange(PANELS, dtype=jnp.int32)[:, None] * NB + jnp.arange(NB, dtype=jnp.int32)[None, :]
    random_bits = jax.random.randint(bits_key, (PANELS, NB), 0, 2 ** 30, dtype=jnp.int32)
    chosen = starts + random_bits % (M - starts)
    picked = jax.random.randint(pick_key, (PANELS, 1), 1, NB, dtype=jnp.int32)
    positions = jnp.arange(NB, dtype=jnp.int32)[None, :]
    chosen = jnp.where(positions == picked, M - 1, chosen)
    first_spot = (jnp.arange(PANELS, dtype=jnp.int32)[:, None] == 0) & (positions == 0)
    chosen = jnp.where(first_spot, 0, chosen)
    return chosen.astype(jnp.int32)


def draw_lower_inv(key, part):
    entry_key = jax.random.fold_in(key, 31)
    entries = jax.random.normal(entry_key, (PANELS, NB, NB), jnp.float32)
    row_ids = jnp.arange(NB)[:, None]
    col_ids = jnp.arange(NB)[None, :]
    below = jnp.where(row_ids > col_ids, entries * (0.7 / math.sqrt(NB)), 0.0)
    return (below + jnp.where(row_ids == col_ids, 1.0, 0.0)).astype(jnp.float32)


def draw_upper_inv(key, part):
    entry_key = jax.random.fold_in(key, 41)
    diag_key = jax.random.fold_in(key, 42)
    entries = jax.random.normal(entry_key, (PANELS, NB, NB), jnp.float32)
    diag_vals = jnp.exp(jax.random.uniform(diag_key, (PANELS, NB, NB), jnp.float32, math.log(0.5), math.log(2.0)))
    row_ids = jnp.arange(NB)[:, None]
    col_ids = jnp.arange(NB)[None, :]
    above = jnp.where(row_ids < col_ids, entries * (0.7 / math.sqrt(NB)), 0.0)
    diagonal_part = jnp.where(row_ids == col_ids, diag_vals, 0.0)
    return ((above + diagonal_part) / math.sqrt(NB)).astype(jnp.float32)


def level_of(key, extent, split, least, largest):
    factor_of = 1.0
    for dim, blocks in split:
        draws = jax.random.uniform(jax.random.fold_in(jax.random.fold_in(key, 6), dim), (blocks,), jnp.float32, least / len(split), largest / len(split))
        factor_of = factor_of * jnp.repeat(jnp.exp(draws), extent[dim] // blocks).reshape((-1,) + (1,) * (len(extent) - 1 - dim))
    return factor_of


def bell_draw(rng, dims, width, reach, split=(), held_as=jnp.bfloat16):
    level = level_of(rng, dims, split, -0.22, 0.18) if split else 1.0
    array = jax.random.normal(rng, dims, jnp.float32) * width * level
    return jnp.minimum(jnp.maximum(array, -reach), reach).astype(held_as)


def setup_inputs(seed: int = 0) -> dict:
    seeds = jax.random.split(jax.random.key(seed), 5)
    matrix = bell_draw(seeds[0], (ROWBLK, NB, COLBLK, COLSPAN), 1.0, 6.0, ((1, 32), (3, 8)), jnp.float32)
    pivots = draw_pivots(jax.random.fold_in(seeds[4], 71), 0)
    lower_inv = draw_lower_inv(jax.random.fold_in(seeds[4], 71), 0)
    upper_inv = draw_upper_inv(jax.random.fold_in(seeds[4], 71), 0)
    return {"matrix": matrix, "pivots": pivots, "lower_inv": lower_inv, "upper_inv": upper_inv}


def permutation(pivot_row, offset):
    def swap_one(position, ordering):
        target = pivot_row[position].astype(jnp.int32)
        root = (offset + position)
        first_row = ordering[root]
        second_row = ordering[target]
        return ordering.at[root].set(second_row).at[target].set(first_row)
    return lax.fori_loop(0, NB, swap_one, jnp.arange(M, dtype=jnp.int32))


def reference(matrix, pivots, lower_inv, upper_inv):
    current = matrix.reshape(M, M)
    for panel_index in range(PANELS):
        offset = panel_index * NB
        ending = offset + NB
        ordering = permutation(pivots[panel_index], offset)
        current = current[ordering]
        upper_block = jnp.dot(lower_inv[panel_index], current[offset:ending, ending:], precision=lax.Precision.HIGHEST, preferred_element_type=jnp.float32)
        lower_block = jnp.dot(current[ending:, offset:ending], upper_inv[panel_index], precision=lax.Precision.HIGHEST, preferred_element_type=jnp.float32)
        trailing = current[ending:, ending:] - jnp.dot(lower_block, upper_block, precision=lax.Precision.HIGHEST, preferred_element_type=jnp.float32)
        current = current.at[offset:ending, ending:].set(upper_block)
        current = current.at[ending:, offset:ending].set(lower_block)
        current = current.at[ending:, ending:].set(trailing)
    return current.reshape(ROWBLK, NB, COLBLK, COLSPAN)
```

```python
import functools

import jax
import jax.numpy as jnp
from jax import lax
from jax.experimental import pallas as pl
from jax.experimental.pallas import tpu as pltpu
from jax.sharding import Mesh
from jax.sharding import PartitionSpec as P

PROW = ("x", "z")
MESH = pl.DeviceIdType.MESH
NX, NZ = 4, 8
CAP = 56


def in_order(parts, dim):
    shape = list(parts.shape[1:])
    shape[dim] *= parts.shape[0]
    return jnp.moveaxis(parts, 0, dim).reshape(shape)


def all_blocks(x, axes, order):
    parts = x
    for k in order:
        parts = lax.all_gather(parts, axes[k])
    done = order[::-1]
    back = [done.index(k) for k in range(len(axes))]
    parts = parts.transpose(*back, *range(len(axes), parts.ndim))
    return parts.reshape(-1, *x.shape)


def gathered_by_axis(x, axes, order, dim):
    return in_order(all_blocks(x, axes, order), dim)


def sum_by_axis(x, axes, dim):
    for axis in axes:
        x = lax.psum_scatter(x, axis, scatter_dimension=dim, tiled=True)
    return x


def broadcast(x, axis, root):
    return lax.dynamic_index_in_dim(lax.all_gather(x, axis), root, 0, keepdims=False)


def permutation(pivot_row, offset, panel_width, full_order):
    steps = jnp.arange(panel_width, dtype=jnp.int32)
    anchors = offset + steps
    earlier = steps[None, :] < steps[:, None]
    hits_anchor = (pivot_row[None, :] == anchors[:, None]) & earlier
    chain_from = jnp.max(jnp.where(hits_anchor, steps[None, :], -1), axis=1)
    pointer = jnp.where(chain_from >= 0, chain_from, steps)
    for level in range(max(1, panel_width.bit_length())):
        pointer = pointer[pointer]
    before_value = offset + pointer
    same_target = (pivot_row[None, :] == pivot_row[:, None]) & earlier
    last_before = jnp.max(jnp.where(same_target, steps[None, :], -1), axis=1)
    anchor_value = jnp.where(
        last_before >= 0, before_value[jnp.clip(last_before, 0, panel_width - 1)], pivot_row
    )
    later = steps[None, :] > steps[:, None]
    has_later = jnp.any((pivot_row[None, :] == pivot_row[:, None]) & later, axis=1)
    outside = jnp.logical_not(has_later) & (pivot_row >= offset + panel_width)
    spots = jnp.where(outside, pivot_row, full_order)
    ordering = jnp.arange(full_order, dtype=jnp.int32).at[spots].set(before_value, mode="drop")
    return lax.dynamic_update_slice_in_dim(ordering, anchor_value, offset, 0)


def product(left, right):
    return jnp.dot(left, right, precision=lax.Precision.HIGHEST, preferred_element_type=jnp.float32)


def general(matrix, pivots, lower_inv, upper_inv):
    row_blocks, row_part, col_blocks, col_part = matrix.shape
    panel_width = lower_inv.shape[1]
    panel_count = pivots.shape[0]
    full_order = row_blocks * panel_width
    row_devices = lax.axis_size(PROW)
    col_devices = lax.axis_size("pcol")
    row_index = lax.axis_index(PROW)
    col_index = lax.axis_index("pcol")
    local_rows = row_blocks * row_part
    local_cols = col_blocks * col_part
    share_width = local_cols // row_devices
    current = matrix.reshape(local_rows, local_cols)
    global_rows = (
        jnp.arange(row_blocks, dtype=jnp.int32)[:, None] * panel_width
        + row_index * row_part
        + jnp.arange(row_part, dtype=jnp.int32)[None, :]
    ).reshape(local_rows)
    col_span = col_devices * col_part
    global_cols = (
        jnp.arange(col_blocks, dtype=jnp.int32)[:, None] * col_span
        + col_index * col_part
        + jnp.arange(col_part, dtype=jnp.int32)[None, :]
    ).reshape(local_cols)
    for panel_index in range(panel_count):
        offset = panel_index * panel_width
        ending = offset + panel_width
        ordering = permutation(pivots[panel_index], offset, panel_width, full_order)
        source = ordering[global_rows]
        old_top = current[panel_index * row_part : (panel_index + 1) * row_part]
        old_panel = gathered_by_axis(old_top, PROW, (0, 1), 0)
        wanted = ordering[offset + jnp.arange(panel_width, dtype=jnp.int32)]
        holder = wanted % panel_width // row_part
        local_spot = wanted // panel_width * row_part + wanted % row_part
        picked = jnp.where((holder == row_index)[:, None], current[local_spot], 0.0)
        column_share = sum_by_axis(picked, PROW, 1)
        share_cols = lax.dynamic_slice_in_dim(global_cols, row_index * share_width, share_width)
        solved = product(lower_inv[panel_index], column_share)
        merged = jnp.where((share_cols >= ending)[None, :], solved, column_share)
        top_rows = gathered_by_axis(merged, PROW, (0, 1), 1)
        in_panel = global_rows // panel_width == panel_index
        displaced = (source != global_rows) & jnp.logical_not(in_panel)
        from_old = old_panel[jnp.clip(source - offset, 0, panel_width - 1)]
        current = jnp.where(displaced[:, None], from_old, current)
        own_rows = lax.dynamic_slice_in_dim(top_rows, row_index * row_part, row_part, 0)
        current = lax.dynamic_update_slice_in_dim(current, own_rows, panel_index * row_part, 0)
        trailing_row = global_rows >= ending
        trailing_col = global_cols >= ending
        lower_full = product(current[:, :col_part], upper_inv[panel_index])
        lower_here = jnp.where(trailing_row[:, None], lower_full, 0.0)
        lower_rows = broadcast(lower_here, "pcol", panel_index)
        upper_part = jnp.where(trailing_col[None, :], top_rows, 0.0)
        current = current - product(lower_rows, upper_part)
        own_panel = col_index == panel_index
        new_cols = jnp.where(own_panel & trailing_row[:, None], lower_rows, current[:, :col_part])
        current = jnp.concatenate([new_cols, current[:, col_part:]], axis=1)
    return current.reshape(row_blocks, row_part, col_blocks, col_part)


def to_column(row):
    n = row.shape[1]
    eye = lax.broadcasted_iota(jnp.int32, (n, n), 0) == lax.broadcasted_iota(jnp.int32, (n, n), 1)
    return jnp.max(jnp.where(eye, row, -1.0), axis=1, keepdims=True)


def lookup(keys, values, wanted):
    return jnp.max(jnp.where(keys == wanted, values, -1.0), axis=0, keepdims=True)


def plan_kernel(width, order, piv_row_ref, piv_col_ref, slot_ref, pick_ref, source_ref, count_ref):
    me = lax.axis_index("x") * NZ + lax.axis_index("z")
    part = width // (NX * NZ)
    j = lax.broadcasted_iota(jnp.int32, (width, width), 0).astype(jnp.float32)
    i = lax.broadcasted_iota(jnp.int32, (width, width), 1).astype(jnp.float32)
    i_row = i[:1]
    sources, spots, befores = [], [], []
    for k in range(2):
        offset = float(k * width)
        p_row = piv_row_ref[k : k + 1, :].astype(jnp.float32)
        p_col = piv_col_ref[:, k : k + 1].astype(jnp.float32)
        chain = jnp.max(jnp.where((p_col == offset + i) & (j < i), j, -1.0), axis=0, keepdims=True)
        start = jnp.where(chain >= 0.0, chain, i_row)

        def again(state):
            return state[1] > 0.0

        def jump(state):
            pointer = state[0]
            found = lookup(j[:, :1], to_column(pointer), pointer)
            return found, jnp.max(jnp.abs(found - pointer))

        pointer, _ = lax.while_loop(again, jump, (start, jnp.float32(1.0)))
        before = offset + pointer
        before_col = to_column(before)
        same = p_col == p_row
        last = jnp.max(jnp.where(same & (j < i), j, -1.0), axis=0, keepdims=True)
        later = jnp.max(jnp.where(same & (j > i), 1.0, 0.0), axis=0, keepdims=True)
        anchor = jnp.where(last >= 0.0, lookup(j[:, :1], before_col, last), p_row)
        spot = jnp.where((later == 0.0) & (p_row >= offset + width), p_row, -5.0)
        if k == 1:
            moved = lookup(spots[0], befores[0], anchor)
            anchor = jnp.where(moved >= 0.0, moved, anchor)
        sources.append(anchor)
        spots.append(jnp.max(jnp.where(i == j, spot, -5.0), axis=1, keepdims=True))
        befores.append(before_col)

    holders, places = [], []
    for k in range(2):
        src = sources[k].astype(jnp.int32)
        within = jnp.bitwise_and(src, width - 1)
        holders.append((within // part).astype(jnp.float32))
        places.append(((src // width) * part + jnp.bitwise_and(src, part - 1)).astype(jnp.float32))
    h_col = [to_column(h) for h in holders]
    ranks = []
    for k in range(2):
        rank = jnp.sum(jnp.where((h_col[k] == holders[k]) & (j < i), 1.0, 0.0), axis=0, keepdims=True)
        if k == 1:
            rank = rank + jnp.sum(jnp.where(h_col[0] == holders[1], 1.0, 0.0), axis=0, keepdims=True)
        ranks.append(rank)
    most = jnp.maximum(jnp.max(ranks[0]), jnp.max(ranks[1])) + 1.0
    count_ref[...] = jnp.full(count_ref.shape, most, jnp.float32).astype(jnp.int32)
    cap = pick_ref.shape[0]
    k_col = lax.broadcasted_iota(jnp.int32, (cap, width), 0).astype(jnp.float32)
    pick = jnp.full((cap, 1), -1.0, jnp.float32)
    for k in range(2):
        slot_ref[k : k + 1, :] = (holders[k] * float(cap) + jnp.minimum(ranks[k], cap - 1.0)).astype(jnp.int32)
        mine = jnp.where(holders[k] == me.astype(jnp.float32), ranks[k], -1.0)
        pick = jnp.maximum(pick, jnp.max(jnp.where(k_col == mine, places[k], -1.0), axis=1, keepdims=True))
    pick_ref[...] = pick.astype(jnp.int32)
    rows = source_ref.shape[1]
    spot_row = lax.broadcasted_iota(jnp.int32, (1, rows), 1)
    g = ((spot_row // part) * width + me * part + jnp.bitwise_and(spot_row, part - 1)).astype(jnp.float32)
    first = lookup(spots[1], befores[1], g)
    g1 = jnp.where(first >= 0.0, first, g)
    second = lookup(spots[0], befores[0], g1)
    g0 = jnp.where(second >= 0.0, second, g1)
    source_ref[...] = jnp.where(g0 == g, -1.0, g0).astype(jnp.int32)


def make_plan(pivots, width, order, rows):
    vmem = pl.BlockSpec(memory_space=pltpu.VMEM)
    return pl.pallas_call(
        functools.partial(plan_kernel, width, order),
        out_shape=(
            jax.ShapeDtypeStruct((2, width), jnp.int32),
            jax.ShapeDtypeStruct((CAP, 1), jnp.int32),
            jax.ShapeDtypeStruct((1, rows), jnp.int32),
            jax.ShapeDtypeStruct((8, 128), jnp.int32),
        ),
        in_specs=[vmem, vmem],
        out_specs=(vmem, vmem, vmem, vmem),
        name="row_plan",
    )(pivots, pivots.T)


class Piece:
    def __init__(self, buf, cols, first, x, z, col, send_sem, recv_sem):
        self.buf, self.cols, self.first, self.x, self.z, self.col = buf, cols, first, x, z, col
        self.send_sem, self.recv_sem = send_sem, recv_sem
        self.rows = buf.shape[1]
        self.started = []
        self.na, self.nb = (NX, NZ) if first == "x" else (NZ, NX)
        self.a, self.b = (x, z) if first == "x" else (z, x)

    def place(self, da, db):
        return lax.rem(self.a + da + self.na, self.na), lax.rem(self.b + db + self.nb, self.nb)

    def block(self, da, db):
        a, b = self.place(da, db)
        return a * NZ + b if self.first == "x" else b * NZ + a

    def device(self, da, db):
        a, b = self.place(da, db)
        return (a, b, self.col) if self.first == "x" else (b, a, self.col)

    def copy(self, da, db, to, half, k):
        block = self.block(da, db)
        middle = self.rows // 16 * 8
        low, high = ((0, self.rows), (0, middle), (middle, self.rows))[0 if half is None else half + 1]
        view = self.buf.at[block, low:high, self.cols[0] : self.cols[1]]
        return pltpu.make_async_remote_copy(
            src_ref=view,
            dst_ref=view,
            send_sem=self.send_sem.at[block, k],
            recv_sem=self.recv_sem.at[block, half or 0],
            device_id=self.device(*to),
            device_id_type=MESH,
        )

    def send(self, da, db, to, half, k):
        copy = self.copy(da, db, to, half, k)
        copy.start()
        self.started.append(copy)

    def receive(self, da, db, half):
        self.copy(da, db, (0, 1), half, 0).wait_recv()

    def along_first(self, d):
        for s in (1, -1):
            if d + 1 <= self.na // 2:
                half = None if d + 1 < self.na // 2 else (1 - s) // 2
                self.send(-s * d, 0, (s, 0), half, (1 - s) // 2)

    def along_second(self, da, d):
        for s in (1, -1):
            if d + 1 <= self.nb // 2:
                half = None if d + 1 < self.nb // 2 else (1 - s) // 2
                self.send(da, -s * d, (0, s), half, (1 - s) // 2 + (2 if d == 0 else 0))

    def first_step(self, d):
        if d == 0:
            self.along_first(0)
            self.along_second(0, 0)
        elif d < self.na // 2:
            for s in (1, -1):
                self.receive(-s * d, 0, None)
            self.along_first(d)
            for s in (1, -1):
                self.along_second(-s * d, 0)
        else:
            self.receive(d, 0, 0)
            self.receive(d, 0, 1)
            self.along_second(d, 0)

    def second_step(self, da, d):
        if d < self.nb // 2:
            for s in (1, -1):
                self.receive(da, -s * d, None)
            self.along_second(da, d)
        else:
            self.receive(da, d, 0)
            self.receive(da, d, 1)

    def steps(self):
        work = [(d, functools.partial(self.first_step, d)) for d in range(self.na // 2 + 1)]
        for d in range(1, self.nb // 2 + 1):
            for ad in range(self.na // 2 + 1):
                for da in [0] if ad == 0 else [ad] if ad == self.na // 2 else [-ad, ad]:
                    work.append((ad + d + 0.5, functools.partial(self.second_step, da, d)))
        return work

    def finish(self):
        for copy in self.started:
            copy.wait_send()


def greet(devices):
    barrier = pltpu.get_barrier_semaphore()
    for device in devices:
        pl.semaphore_signal(barrier, inc=1, device_id=device, device_id_type=MESH)
    pl.semaphore_wait(barrier, len(devices))


def run_pieces(pieces, lag):
    work = []
    for number, piece in enumerate(pieces):
        for place, (when, step) in enumerate(piece.steps()):
            work.append((when + lag[number], number, place, step))
    work.sort(key=lambda entry: entry[:3])
    for entry in work:
        entry[3]()
    for piece in pieces:
        piece.finish()


def split_three(value):
    high = value.astype(jnp.bfloat16)
    rest = value - high.astype(jnp.float32)
    middle = rest.astype(jnp.bfloat16)
    low = (rest - middle.astype(jnp.float32)).astype(jnp.bfloat16)
    return high, middle, low


def gather_kernel(matrix_ref, pick_ref, old_ref, new_ref, *sems):
    x, z, col = lax.axis_index("x"), lax.axis_index("z"), lax.axis_index("pcol")
    me = x * NZ + z
    rows, columns = matrix_ref.shape
    old_ref[pl.ds(me, 1)] = matrix_ref[0 : old_ref.shape[1], :][None]
    hot = pick_ref[...] == lax.broadcasted_iota(jnp.int32, (CAP, rows), 1)
    hot = jnp.where(hot, 1.0, 0.0).astype(jnp.bfloat16)
    for c in range(0, columns, 512):
        total = jnp.zeros((CAP, 512), jnp.float32)
        for term in split_three(matrix_ref[:, c : c + 512]):
            total = total + jnp.dot(hot, term, preferred_element_type=jnp.float32)
        new_ref[pl.ds(me, 1), :, c : c + 512] = total[None]
    greet(
        [
            (lax.rem(x + 1, NX), z, col),
            (lax.rem(x + NX - 1, NX), z, col),
            (x, lax.rem(z + 1, NZ), col),
            (x, lax.rem(z + NZ - 1, NZ), col),
        ]
    )
    pieces = []
    for number, buf in enumerate((new_ref, old_ref)):
        for part, (first, cols) in enumerate((("x", (0, 640)), ("z", (640, 1536)))):
            s = 4 * number + 2 * part
            pieces.append(Piece(buf, cols, first, x, z, col, sems[s], sems[s + 1]))
    run_pieces(pieces, [0.0, 0.0, 0.1, 0.1])


def gather_rows(matrix, pick):
    rows, columns = matrix.shape
    vmem = pl.BlockSpec(memory_space=pltpu.VMEM)
    sems = [pltpu.SemaphoreType.DMA((NX * NZ, 4)), pltpu.SemaphoreType.DMA((NX * NZ, 2))]
    return pl.pallas_call(
        gather_kernel,
        out_shape=(
            jax.ShapeDtypeStruct((NX * NZ, 32, columns), jnp.float32),
            jax.ShapeDtypeStruct((NX * NZ, CAP, columns), jnp.float32),
        ),
        in_specs=[vmem, vmem],
        out_specs=(vmem, vmem),
        scratch_shapes=sems * 4,
        compiler_params=pltpu.CompilerParams(
            collective_id=0, has_side_effects=True, vmem_limit_bytes=60 * 2**20
        ),
        name="gather_rows",
    )(matrix, pick)


def spread_kernel(root, chunks, own_ref, out_ref, send_sem, recv_sem, mate_send, mate_recv):
    x, z, col = lax.axis_index("x"), lax.axis_index("z"), lax.axis_index("pcol")
    y, core = col // 2, lax.rem(col, 2)
    mate = y * 2 + 1 - core
    up, down = lax.rem(y + 1, 4) * 2 + core, lax.rem(y + 3, 4) * 2 + core
    away = lax.rem(y - root // 2 + 4, 4)
    step = own_ref.shape[0] // chunks

    @pl.when(col == root)
    def _():
        out_ref[...] = own_ref[...]

    greet([(x, z, mate), (x, z, up), (x, z, down)])

    def copy(c, device, sems, k):
        view = out_ref.at[c * step : (c + 1) * step]
        return pltpu.make_async_remote_copy(
            src_ref=view, dst_ref=view, send_sem=sems[0].at[k], recv_sem=sems[1].at[c],
            device_id=(x, z, device), device_id_type=MESH,
        )

    ring, pair = (send_sem, recv_sem), (mate_send, mate_recv)

    @pl.when(core == root % 2)
    def _():
        for c in range(chunks):
            forward = up if c % 2 == 0 else down
            far = 3 if c % 2 == 0 else 1

            @pl.when(away != 0)
            def _():
                copy(c, forward, ring, c).wait_recv()

            @pl.when(away != far)
            def _():
                copy(c, forward, ring, c).start()

            copy(c, mate, pair, c).start()
        for c in range(chunks):
            forward = up if c % 2 == 0 else down
            far = 3 if c % 2 == 0 else 1

            @pl.when(away != far)
            def _():
                copy(c, forward, ring, c).wait_send()

            copy(c, mate, pair, c).wait_send()

    @pl.when(core != root % 2)
    def _():
        for c in range(chunks):
            copy(c, mate, pair, c).wait_recv()


def spread(own, root, chunks, number):
    vmem = pl.BlockSpec(memory_space=pltpu.VMEM)
    return pl.pallas_call(
        functools.partial(spread_kernel, root, chunks),
        out_shape=jax.ShapeDtypeStruct(own.shape, jnp.float32),
        in_specs=[vmem],
        out_specs=vmem,
        scratch_shapes=[pltpu.SemaphoreType.DMA((chunks,))] * 4,
        compiler_params=pltpu.CompilerParams(
            collective_id=number, has_side_effects=True, vmem_limit_bytes=40 * 2**20
        ),
        name=f"spread_lower_{root}",
    )(own)


def times(left, right):
    return jnp.dot(left, right, precision=lax.Precision.HIGH, preferred_element_type=jnp.float32)


def balanced(matrix, slots, pick, source, lower_inv, upper_inv):
    row_blocks, row_part, col_blocks, col_part = matrix.shape
    width = lower_inv.shape[1]
    me = lax.axis_index(PROW)
    col = lax.axis_index("pcol")
    top = 2 * row_part
    local = matrix.reshape(row_blocks * row_part, col_blocks * col_part)
    old, new = gather_rows(local, pick)
    panels = new.reshape(-1, local.shape[1])[slots.reshape(-1)]
    source = source[0]
    old_spot = (source % width) // row_part * top + source // width * row_part + source % row_part
    moved = old.reshape(-1, local.shape[1])[jnp.maximum(old_spot[top:], 0)]
    kept = jnp.where((source[top:] >= 0)[:, None], moved, local[top:])
    top0 = panels[:width]
    below = jnp.concatenate([panels[width:], kept], axis=0)
    lower0 = spread(times(below[:, :col_part], upper_inv[0]), 0, 12, 1)
    solved0 = times(lower_inv[0], top0)
    chunk0 = jnp.arange(local.shape[1])[None, :] < col_part
    upper0 = jnp.where(chunk0 & (col == 0), 0.0, solved0)
    below = below - times(lower0, upper0)
    lower1 = spread(times(below[width:, :col_part], upper_inv[1]), 1, 11, 2)
    solved1 = times(lower_inv[1], below[:width])
    upper1 = jnp.where(chunk0 & (col <= 1), 0.0, solved1)
    trailing = below[width:] - times(lower1, upper1)
    first = jnp.where(chunk0 & (col == 0), top0, solved0)
    second = jnp.where(chunk0 & (col <= 1), below[:width], solved1)
    head = jnp.where(col == 0, lower0[width:], jnp.where(col == 1, lower1, trailing[:, :col_part]))
    head1 = jnp.where(col == 0, lower0[:width], second[:, :col_part])
    own0 = lax.dynamic_slice_in_dim(first, me * row_part, row_part, 0)
    own1 = jnp.concatenate(
        [
            lax.dynamic_slice_in_dim(head1, me * row_part, row_part, 0),
            lax.dynamic_slice_in_dim(second, me * row_part, row_part, 0)[:, col_part:],
        ],
        axis=1,
    )
    trailing = jnp.concatenate([head, trailing[:, col_part:]], axis=1)
    out = jnp.concatenate([own0, own1, trailing], axis=0)
    return out.reshape(matrix.shape)


def local(matrix, pivots, lower_inv, upper_inv):
    row_blocks, row_part = matrix.shape[:2]
    width = lower_inv.shape[1]
    slots, pick, source, most = make_plan(pivots, width, row_blocks * width, row_blocks * row_part)
    return lax.cond(
        most[0, 0] <= CAP,
        lambda m, s, k, r, a, b: balanced(m, s, k, r, a, b),
        lambda m, s, k, r, a, b: general(m, pivots, a, b),
        matrix, slots, pick, source, lower_inv, upper_inv,
    )


def solution(mesh):
    finer = Mesh(mesh.devices.reshape(NX, NZ, mesh.shape["pcol"]), ("x", "z", "pcol"))
    in_specs = (P(None, PROW, None, "pcol"), P(), P(), P())
    out_specs = P(None, PROW, None, "pcol")
    return jax.shard_map(local, mesh=finer, in_specs=in_specs, out_specs=out_specs, check_vma=False)
```

```python
import functools

import jax
import jax.numpy as jnp
from jax import lax
from jax.experimental import pallas as pl
from jax.experimental.pallas import tpu as pltpu
from jax.sharding import Mesh
from jax.sharding import PartitionSpec as P

PROW = ("x", "z")
MESH = pl.DeviceIdType.MESH
NX, NZ = 4, 8


def in_order(parts, dim):
    shape = list(parts.shape[1:])
    shape[dim] *= parts.shape[0]
    return jnp.moveaxis(parts, 0, dim).reshape(shape)


def all_blocks(x, axes, order):
    parts = x
    for k in order:
        parts = lax.all_gather(parts, axes[k])
    done = order[::-1]
    back = [done.index(k) for k in range(len(axes))]
    parts = parts.transpose(*back, *range(len(axes), parts.ndim))
    return parts.reshape(-1, *x.shape)


def gathered_by_axis(x, axes, order, dim):
    return in_order(all_blocks(x, axes, order), dim)


def sum_by_axis(x, axes, dim):
    for axis in axes:
        x = lax.psum_scatter(x, axis, scatter_dimension=dim, tiled=True)
    return x


def broadcast(x, axis, root):
    return lax.dynamic_index_in_dim(lax.all_gather(x, axis), root, 0, keepdims=False)


def permutation(pivot_row, offset, panel_width, full_order):
    steps = jnp.arange(panel_width, dtype=jnp.int32)
    anchors = offset + steps
    earlier = steps[None, :] < steps[:, None]
    hits_anchor = (pivot_row[None, :] == anchors[:, None]) & earlier
    chain_from = jnp.max(jnp.where(hits_anchor, steps[None, :], -1), axis=1)
    pointer = jnp.where(chain_from >= 0, chain_from, steps)
    for level in range(max(1, panel_width.bit_length())):
        pointer = pointer[pointer]
    before_value = offset + pointer
    same_target = (pivot_row[None, :] == pivot_row[:, None]) & earlier
    last_before = jnp.max(jnp.where(same_target, steps[None, :], -1), axis=1)
    anchor_value = jnp.where(
        last_before >= 0, before_value[jnp.clip(last_before, 0, panel_width - 1)], pivot_row
    )
    later = steps[None, :] > steps[:, None]
    has_later = jnp.any((pivot_row[None, :] == pivot_row[:, None]) & later, axis=1)
    outside = jnp.logical_not(has_later) & (pivot_row >= offset + panel_width)
    spots = jnp.where(outside, pivot_row, full_order)
    ordering = jnp.arange(full_order, dtype=jnp.int32).at[spots].set(before_value, mode="drop")
    return lax.dynamic_update_slice_in_dim(ordering, anchor_value, offset, 0)


def product(left, right):
    return jnp.dot(left, right, precision=lax.Precision.HIGHEST, preferred_element_type=jnp.float32)


def general(matrix, pivots, lower_inv, upper_inv):
    row_blocks, row_part, col_blocks, col_part = matrix.shape
    panel_width = lower_inv.shape[1]
    panel_count = pivots.shape[0]
    full_order = row_blocks * panel_width
    row_devices = lax.axis_size(PROW)
    col_devices = lax.axis_size("pcol")
    row_index = lax.axis_index(PROW)
    col_index = lax.axis_index("pcol")
    local_rows = row_blocks * row_part
    local_cols = col_blocks * col_part
    share_width = local_cols // row_devices
    current = matrix.reshape(local_rows, local_cols)
    global_rows = (
        jnp.arange(row_blocks, dtype=jnp.int32)[:, None] * panel_width
        + row_index * row_part
        + jnp.arange(row_part, dtype=jnp.int32)[None, :]
    ).reshape(local_rows)
    col_span = col_devices * col_part
    global_cols = (
        jnp.arange(col_blocks, dtype=jnp.int32)[:, None] * col_span
        + col_index * col_part
        + jnp.arange(col_part, dtype=jnp.int32)[None, :]
    ).reshape(local_cols)
    for panel_index in range(panel_count):
        offset = panel_index * panel_width
        ending = offset + panel_width
        ordering = permutation(pivots[panel_index], offset, panel_width, full_order)
        source = ordering[global_rows]
        old_top = current[panel_index * row_part : (panel_index + 1) * row_part]
        old_panel = gathered_by_axis(old_top, PROW, (0, 1), 0)
        wanted = ordering[offset + jnp.arange(panel_width, dtype=jnp.int32)]
        holder = wanted % panel_width // row_part
        local_spot = wanted // panel_width * row_part + wanted % row_part
        picked = jnp.where((holder == row_index)[:, None], current[local_spot], 0.0)
        column_share = sum_by_axis(picked, PROW, 1)
        share_cols = lax.dynamic_slice_in_dim(global_cols, row_index * share_width, share_width)
        solved = product(lower_inv[panel_index], column_share)
        merged = jnp.where((share_cols >= ending)[None, :], solved, column_share)
        top_rows = gathered_by_axis(merged, PROW, (0, 1), 1)
        in_panel = global_rows // panel_width == panel_index
        displaced = (source != global_rows) & jnp.logical_not(in_panel)
        from_old = old_panel[jnp.clip(source - offset, 0, panel_width - 1)]
        current = jnp.where(displaced[:, None], from_old, current)
        own_rows = lax.dynamic_slice_in_dim(top_rows, row_index * row_part, row_part, 0)
        current = lax.dynamic_update_slice_in_dim(current, own_rows, panel_index * row_part, 0)
        trailing_row = global_rows >= ending
        trailing_col = global_cols >= ending
        lower_full = product(current[:, :col_part], upper_inv[panel_index])
        lower_here = jnp.where(trailing_row[:, None], lower_full, 0.0)
        lower_rows = broadcast(lower_here, "pcol", panel_index)
        upper_part = jnp.where(trailing_col[None, :], top_rows, 0.0)
        current = current - product(lower_rows, upper_part)
        own_panel = col_index == panel_index
        new_cols = jnp.where(own_panel & trailing_row[:, None], lower_rows, current[:, :col_part])
        current = jnp.concatenate([new_cols, current[:, col_part:]], axis=1)
    return current.reshape(row_blocks, row_part, col_blocks, col_part)


CLASS_ROWS = 8
MOVED_ROWS = 16


def to_column(row):
    n = row.shape[1]
    eye = lax.broadcasted_iota(jnp.int32, (n, n), 0) == lax.broadcasted_iota(jnp.int32, (n, n), 1)
    return jnp.max(jnp.where(eye, row, -1.0), axis=1, keepdims=True)


def lookup(keys, values, wanted):
    return jnp.max(jnp.where(keys == wanted, values, -1.0), axis=0, keepdims=True)


def find(size, keys, values):
    found = jnp.full((size, 1), -1.0, jnp.float32)
    for key, value in zip(keys, values):
        number = lax.broadcasted_iota(jnp.int32, (size, key.shape[1]), 0).astype(jnp.float32)
        found = jnp.maximum(found, jnp.max(jnp.where(number == key, value, -1.0), axis=1, keepdims=True))
    return found.astype(jnp.int32)


def ranks_of(keys, columns, j, i):
    ranks, smaller = [], []
    for k in range(2):
        rank = jnp.sum(jnp.where((columns[k] == keys[k]) & (j < i), 1.0, 0.0), axis=0, keepdims=True)
        if k == 1:
            rank = rank + jnp.sum(jnp.where(columns[0] == keys[1], 1.0, 0.0), axis=0, keepdims=True)
        ranks.append(rank)
        smaller.append(
            sum(jnp.sum(jnp.where(column < keys[k], 1.0, 0.0), axis=0, keepdims=True) for column in columns)
        )
    return ranks, smaller


def plan_kernel(width, piv_row_ref, piv_col_ref, pick_ref, fold_ref, perm_ref, pack_ref, place_ref, most_ref):
    me = (lax.axis_index("x") * NZ + lax.axis_index("z")).astype(jnp.float32)
    my_x, my_z = lax.axis_index("x").astype(jnp.float32), lax.axis_index("z").astype(jnp.float32)
    part = width // (NX * NZ)
    j = lax.broadcasted_iota(jnp.int32, (width, width), 0).astype(jnp.float32)
    i = lax.broadcasted_iota(jnp.int32, (width, width), 1).astype(jnp.float32)
    i_row = i[:1]
    sources, spots, spot_cols, befores, before_cols = [], [], [], [], []
    for k in range(2):
        offset = float(k * width)
        p_row = piv_row_ref[k : k + 1, :].astype(jnp.float32)
        p_col = piv_col_ref[:, k : k + 1].astype(jnp.float32)
        chain = jnp.max(jnp.where((p_col == offset + i) & (j < i), j, -1.0), axis=0, keepdims=True)
        start = jnp.where(chain >= 0.0, chain, i_row)

        def again(state):
            return state[1] > 0.0

        def jump(state):
            pointer = state[0]
            found = lookup(j[:, :1], to_column(pointer), pointer)
            return found, jnp.max(jnp.abs(found - pointer))

        pointer, _ = lax.while_loop(again, jump, (start, jnp.float32(1.0)))
        before = offset + pointer
        before_col = to_column(before)
        same = p_col == p_row
        last = jnp.max(jnp.where(same & (j < i), j, -1.0), axis=0, keepdims=True)
        later = jnp.max(jnp.where(same & (j > i), 1.0, 0.0), axis=0, keepdims=True)
        anchor = jnp.where(last >= 0.0, lookup(j[:, :1], before_col, last), p_row)
        spot = jnp.where((later == 0.0) & (p_row >= offset + width), p_row, -5.0)
        if k == 1:
            moved = lookup(spot_cols[0], before_cols[0], anchor)
            anchor = jnp.where(moved >= 0.0, moved, anchor)
        sources.append(anchor)
        spots.append(spot)
        spot_cols.append(jnp.max(jnp.where(i == j, spot, -5.0), axis=1, keepdims=True))
        befores.append(before)
        before_cols.append(before_col)

    def divided(value, by):
        return jnp.floor(value * (1.0 / by))

    def holder_and_place(source):
        block = divided(source, width)
        within = source - block * width
        holder = divided(within, part)
        return holder, block * part + within - holder * part

    holders, places = zip(*[holder_and_place(source) for source in sources])
    ranks, smaller = ranks_of(holders, [to_column(h) for h in holders], j, i)
    most = jnp.zeros((1, 1), jnp.float32)
    picks, folds, pick_keys, fold_keys = [], [], [], []
    for k in range(2):
        number = smaller[k] + ranks[k]
        at = divided(number, NZ)
        kind = number - at * NZ
        slot = at - divided(smaller[k] - kind + (NZ - 1.0), NZ)
        most = jnp.maximum(most, jnp.max(slot, axis=1, keepdims=True) - (CLASS_ROWS - 1.0))
        good = slot < CLASS_ROWS
        pick_keys.append(jnp.where((holders[k] == me) & good, kind * CLASS_ROWS + slot, -1.0))
        picks.append(places[k])
        fold_keys.append(jnp.where((kind == my_z) & good, at, -1.0))
        folds.append(holders[k] * CLASS_ROWS + slot)
        perm_ref[k * width : (k + 1) * width, :] = to_column(kind * (2 * width // NZ) + at).astype(jnp.int32)
    pick_ref[...] = find(pick_ref.shape[0], pick_keys, picks)
    fold_ref[...] = find(fold_ref.shape[0], fold_keys, folds)

    landed = lookup(spot_cols[0], before_cols[0], befores[1])
    origins = [befores[0], jnp.where(landed >= 0.0, landed, befores[1])]
    taken = lookup(spot_cols[1], spot_cols[1], spots[0])
    targets = [
        jnp.where((spots[0] >= 2.0 * width) & (taken < 0.0), spots[0], -1.0),
        jnp.where(spots[1] >= 2.0 * width, spots[1], -1.0),
    ]
    owners, rows = zip(*[holder_and_place(origin) for origin in origins])
    ends, spot_rows = zip(*[holder_and_place(jnp.maximum(target, 0.0)) for target in targets])
    owner_x = [divided(owner, NZ) for owner in owners]
    owner_z = [owner - x * NZ for owner, x in zip(owners, owner_x)]
    keys = [
        jnp.where(targets[k] >= 0.0, owner_z[k] * (NX * NZ) + ends[k], 2000.0 + i_row + 600.0 * k) for k in range(2)
    ]
    ranks, _ = ranks_of(keys, [to_column(key) for key in keys], j, i)
    pack_keys, packs, place_keys, place_values = [], [], [], []
    for k in range(2):
        most = jnp.maximum(most, jnp.max(ranks[k], axis=1, keepdims=True) - (MOVED_ROWS - 1.0))
        good = (targets[k] >= 0.0) & (ranks[k] < MOVED_ROWS)
        end_x = divided(ends[k], NZ)
        end_z = ends[k] - end_x * NZ
        pack_keys.append(
            jnp.where(good & (owner_z[k] == my_z) & (end_x == my_x), end_z * MOVED_ROWS + ranks[k], -1.0)
        )
        packs.append(owner_x[k] * (2 * part) + rows[k])
        place_keys.append(jnp.where(good & (ends[k] == me), spot_rows[k], -1.0))
        place_values.append(owner_z[k] * MOVED_ROWS + ranks[k])
    pack_ref[...] = find(pack_ref.shape[0], pack_keys, packs)
    place_ref[...] = find(place_ref.shape[0], place_keys, place_values)
    most_ref[...] = jnp.broadcast_to(most, most_ref.shape).astype(jnp.int32)


def make_plan(pivots, width, rows):
    vmem = pl.BlockSpec(memory_space=pltpu.VMEM)
    sizes = [NZ * CLASS_ROWS, 2 * width // NZ, 2 * width, NZ * MOVED_ROWS, rows]
    shapes = [(n, 1) for n in sizes] + [(8, 128)]
    return pl.pallas_call(
        functools.partial(plan_kernel, width),
        out_shape=[jax.ShapeDtypeStruct(shape, jnp.int32) for shape in shapes],
        in_specs=[vmem, vmem],
        out_specs=[vmem] * len(shapes),
        name="row_plan",
    )(pivots, pivots.T)


class Piece:
    def __init__(self, buf, size, low, high, first, x, z, col, send_sem, recv_sem):
        self.buf, self.size, self.low, self.high, self.first = buf, size, low, high, first
        self.x, self.z, self.col = x, z, col
        self.send_sem, self.recv_sem = send_sem, recv_sem
        self.started = []
        self.na, self.nb = (NX, NZ) if first == "x" else (NZ, NX)
        self.a, self.b = (x, z) if first == "x" else (z, x)

    def place(self, da, db):
        a, b = lax.rem(self.a + da + self.na, self.na), lax.rem(self.b + db + self.nb, self.nb)
        return (a, b) if self.first == "x" else (b, a)

    def copy(self, da, db, to, half, k):
        bx, bz = self.place(da, db)
        middle = (self.low + self.high) // 16 * 8
        low, high = ((self.low, self.high), (self.low, middle), (middle, self.high))[0 if half is None else half + 1]
        view = self.buf.at[bx, pl.ds(pl.multiple_of(bz * self.size + low, 8), high - low)]
        return pltpu.make_async_remote_copy(
            src_ref=view,
            dst_ref=view,
            send_sem=self.send_sem.at[bx * NZ + bz, k],
            recv_sem=self.recv_sem.at[bx * NZ + bz, half or 0],
            device_id=self.place(*to) + (self.col,),
            device_id_type=MESH,
        )

    def send(self, da, db, to, half, k):
        copy = self.copy(da, db, to, half, k)
        copy.start()
        self.started.append(copy)

    def receive(self, da, db, half):
        self.copy(da, db, (0, 1), half, 0).wait_recv()

    def along_first(self, d):
        for s in (1, -1):
            if d + 1 <= self.na // 2:
                half = None if d + 1 < self.na // 2 else (1 - s) // 2
                self.send(-s * d, 0, (s, 0), half, (1 - s) // 2)

    def along_second(self, da, d):
        for s in (1, -1):
            if d + 1 <= self.nb // 2:
                half = None if d + 1 < self.nb // 2 else (1 - s) // 2
                self.send(da, -s * d, (0, s), half, (1 - s) // 2 + (2 if d == 0 else 0))

    def first_step(self, d):
        if d == 0:
            self.along_first(0)
            self.along_second(0, 0)
        elif d < self.na // 2:
            for s in (1, -1):
                self.receive(-s * d, 0, None)
            self.along_first(d)
            for s in (1, -1):
                self.along_second(-s * d, 0)
        else:
            self.receive(d, 0, 0)
            self.receive(d, 0, 1)
            self.along_second(d, 0)

    def second_step(self, da, d):
        if d < self.nb // 2:
            for s in (1, -1):
                self.receive(da, -s * d, None)
            self.along_second(da, d)
        else:
            self.receive(da, d, 0)
            self.receive(da, d, 1)

    def steps(self):
        work = [(d, functools.partial(self.first_step, d)) for d in range(self.na // 2 + 1)]
        for d in range(1, self.nb // 2 + 1):
            for ad in range(self.na // 2 + 1):
                for da in [0] if ad == 0 else [ad] if ad == self.na // 2 else [-ad, ad]:
                    work.append((ad + d + 0.5, functools.partial(self.second_step, da, d)))
        return work


class Spread:
    def __init__(self, buf, chunks, root, x, z, col, sems):
        self.buf, self.chunks, self.root, self.x, self.z, self.col, self.sems = buf, chunks, root, x, z, col, sems
        y, self.core = col // 2, lax.rem(col, 2)
        self.mate = y * 2 + 1 - self.core
        self.up = lax.rem(y + 1, 4) * 2 + self.core
        self.down = lax.rem(y + 3, 4) * 2 + self.core
        self.away = lax.rem(y - root // 2 + 4, 4)

    def copy(self, c, device, pair):
        step = self.buf.shape[0] // self.chunks
        view = self.buf.at[c * step : (c + 1) * step]
        return pltpu.make_async_remote_copy(
            src_ref=view,
            dst_ref=view,
            send_sem=self.sems.at[pair, c],
            recv_sem=self.sems.at[pair + 1, c],
            device_id=(self.x, self.z, device),
            device_id_type=MESH,
        )

    def order(self, hops):
        timed = [((c // 2 + (hops if c % 2 == 0 else 4 - hops)) if hops else c, c) for c in range(self.chunks)]
        return [c for _, c in sorted(timed)]

    def pass_on(self, hops):
        for c in self.order(hops):
            forward, far = (self.up, 3) if c % 2 == 0 else (self.down, 1)
            if hops:
                self.copy(c, forward, 0).wait_recv()
            if hops != far:
                self.copy(c, forward, 0).start()
            self.copy(c, self.mate, 2).start()

    def close(self, hops):
        for c in range(self.chunks):
            if hops != (3 if c % 2 == 0 else 1):
                self.copy(c, self.up, 0).wait_send()
            self.copy(c, self.mate, 2).wait_send()

    def each(self, action, hops_from):
        for hops in range(hops_from, 4):
            pl.when((self.core == self.root % 2) & (self.away == hops))(functools.partial(action, hops))

    def begin(self):
        pl.when(self.col == self.root)(functools.partial(self.pass_on, 0))

    def middle(self):
        self.each(self.pass_on, 1)

        @pl.when(self.core != self.root % 2)
        def _():
            for c in range(self.chunks):
                self.copy(c, self.mate, 2).wait_recv()

    def finish(self):
        self.each(self.close, 0)


def dot(left, right):
    return jnp.dot(left, right, preferred_element_type=jnp.float32)


def split(value):
    high = value.astype(jnp.bfloat16)
    return high, (value - high.astype(jnp.float32)).astype(jnp.bfloat16)


def split_three(value):
    high, rest = split(value)
    low = value - high.astype(jnp.float32) - rest.astype(jnp.float32)
    return high, rest, low.astype(jnp.bfloat16)


def exact(hot, value):
    return sum(dot(hot, term) for term in split_three(value))


def times(left, right):
    return dot(left[0], right[0]) + (dot(left[0], right[1]) + dot(left[1], right[0]))


def hot_of(column, lanes):
    number = lax.broadcasted_iota(jnp.int32, (column.shape[0], lanes), 1)
    return jnp.where(column == number, 1.0, 0.0).astype(jnp.bfloat16)


def blocks(total, step, body):
    def one(n, carry):
        body(pl.multiple_of(n * step, step))
        return carry

    lax.fori_loop(0, total // step, one, 0)


def panels_kernel(
    m_ref, pick_ref, fold_ref, perm_ref, pack_ref, place_ref, linv_ref, uinv_ref, out_ref,
    old, pack_box, place_box, outbox, inbox, g, hot, linv, uinv, t, u, rest, lower0, lower1, low0, low1, solved,
    box_sem, move_sem, old_sem, ring_send, ring_recv, spread_sem0, spread_sem1,
):
    x, z, col = lax.axis_index("x"), lax.axis_index("z"), lax.axis_index("pcol")
    me = x * NZ + z
    count = NX * NZ
    width = linv_ref.shape[1]
    part = width // count
    top = 2 * part
    rows, columns = m_ref.shape
    chunks = columns // width
    size = 2 * width // NZ
    tail = rows - top
    spread0 = Spread(lower0, 6, 0, x, z, col, spread_sem0)
    spread1 = Spread(lower1, 4, 1, x, z, col, spread_sem1)
    started = []

    others = [lax.rem(me + n, count) for n in range(1, count)]
    barrier = pltpu.get_barrier_semaphore()
    greeted = [(o // NZ, lax.rem(o, NZ), col) for o in others]
    greeted += [(x, z, spread0.mate), (x, z, spread0.up), (x, z, spread0.down)]
    for device in greeted:
        pl.semaphore_signal(barrier, inc=1, device_id=device, device_id_type=MESH)

    old[pl.ds(x, 1)] = m_ref[0:top, :][None]
    pick_hot = hot_of(pick_ref[...], rows)
    tile = width // NX
    for c in range(chunks):
        picked = exact(pick_hot, m_ref[:, c * width : (c + 1) * width])
        for xs in range(NX):
            outbox[xs * NZ : (xs + 1) * NZ, :, c * tile : (c + 1) * tile] = picked[
                :, xs * tile : (xs + 1) * tile
            ].reshape(NZ, -1, tile)
    inbox[pl.ds(me, 1)] = outbox[pl.ds(me, 1)]
    pl.semaphore_wait(barrier, len(greeted))

    def send(src, dst, send_sem, recv_sem, device):
        copy = pltpu.make_async_remote_copy(
            src_ref=src, dst_ref=dst, send_sem=send_sem, recv_sem=recv_sem, device_id=device, device_id_type=MESH
        )
        copy.start()
        started.append(copy)

    for o in others:
        send(outbox.at[o], inbox.at[me], box_sem.at[0, o], box_sem.at[1, me], (o // NZ, lax.rem(o, NZ), col))
    for d in range(1, NX):
        to = lax.rem(x + d, NX)
        send(old.at[x], old.at[x], old_sem.at[0, to], old_sem.at[1, x], (to, z, col))

    def arrive(view, sem):
        pltpu.make_async_remote_copy(
            src_ref=view, dst_ref=view, send_sem=sem, recv_sem=sem, device_id=(lax.rem(x + 1, NX), z, col),
            device_id_type=MESH,
        ).wait_recv()

    for d in range(1, NX):
        xs = lax.rem(x + d, NX)
        arrive(old.at[xs], old_sem.at[1, xs])
    pack_hot = hot_of(pack_ref[...], NX * top)
    for c in range(0, columns, width):
        packed = exact(pack_hot, old[:, :, c : c + width].reshape(NX * top, width))
        pack_box[:, :, c : c + width] = packed.reshape(NZ, -1, width)
    place_box[pl.ds(z, 1)] = pack_box[pl.ds(z, 1)]
    for o in others:
        arrive(inbox.at[o], box_sem.at[1, o])
    fold_hot = hot_of(fold_ref[...], count * CLASS_ROWS)
    for c in range(chunks):
        mine = exact(fold_hot, inbox[:, :, c * tile : (c + 1) * tile].reshape(count * CLASS_ROWS, tile))
        g[c, pl.ds(x, 1), pl.ds(pl.multiple_of(z * size, size), size), :] = mine[None]

    pieces, work = [], []
    for c in range(chunks):
        for number, (first, low, high) in enumerate((("x", 0, 32), ("z", 32, size))):
            s = 2 * c + number
            pieces.append(Piece(g.at[c], size, low, high, first, x, z, col, ring_send.at[s], ring_recv.at[s]))
    steps = [sorted(pieces[2 * c].steps() + pieces[2 * c + 1].steps(), key=lambda entry: entry[0]) for c in range(chunks)]
    queue = [[step for _, step in stage] for stage in steps]
    for stage in queue:
        stage.pop(0)()
        stage.pop(0)()
        if stage is queue[0]:
            for d in range(1, NZ):
                to = lax.rem(z + d, NZ)
                send(pack_box.at[to], place_box.at[z], move_sem.at[0, to], move_sem.at[1, z], (x, to, col))

    def prepare():
        for k in range(2):
            linv[k, 0], linv[k, 1] = split(linv_ref[k])
            uinv[k, 0], uinv[k, 1] = split(uinv_ref[k])

        def perm(r):
            hot[pl.ds(r, 128)] = hot_of(perm_ref[pl.ds(r, 128), :], 2 * width)

        blocks(2 * width, 128, perm)

    def place_moved():
        for d in range(1, NZ):
            zs = lax.rem(z + d, NZ)
            arrive(place_box.at[zs], move_sem.at[1, zs])
        column = place_ref[...]
        place_hot = hot_of(column[top:], NZ * MOVED_ROWS)
        for c in range(0, columns, width):
            moved = exact(place_hot, place_box[:, :, c : c + width].reshape(NZ * MOVED_ROWS, width))
            rest[width:, c : c + width] = jnp.where(column[top:] >= 0, moved, m_ref[top:, c : c + width])

    def permute(c):
        whole = jnp.concatenate([g[c, n] for n in range(NX)], axis=1)
        high, middle = split(whole)

        def body(r):
            left = hot[pl.ds(r, 128)]
            first, second = dot(left, high), dot(left, middle)
            t[0, pl.ds(r, 128)] = first.astype(jnp.bfloat16)
            t[1, pl.ds(r, 128)] = second.astype(jnp.bfloat16)

            @pl.when(r >= width)
            def _():
                rest[pl.ds(r - width, 128), c * width : (c + 1) * width] = first + second

        blocks(2 * width, 128, body)

    def own(ref):
        return ref[pl.ds(pl.multiple_of(me * part, part), part)]

    def solve0(c):
        right = t[0, 0:width], t[1, 0:width]
        cols = slice(c * width, (c + 1) * width)

        def body(r):
            value = times((linv[0, 0, pl.ds(r, 128)], linv[0, 1, pl.ds(r, 128)]), right)
            u[0, 0, pl.ds(r, 128), cols], u[0, 1, pl.ds(r, 128), cols] = split(value)
            solved[pl.ds(r, 128)] = value

        blocks(width, 128, body)
        out_ref[0:part, cols] = own(solved)
        if c == 0:

            @pl.when(col == 0)
            def _():
                out_ref[0:part, cols] = own(t.at[0]).astype(jnp.float32) + own(t.at[1]).astype(jnp.float32)
                u[0, :, :, cols] = jnp.zeros((2, width, width), jnp.bfloat16)

    def find_lower0():
        @pl.when(col == 0)
        def _():
            right = uinv[0, 0], uinv[0, 1]

            def body(r):
                lower0[pl.ds(r, 96)] = times(split(rest[pl.ds(r, 96), 0:width]), right)

            blocks(width + tail, 96, body)

    def split_lower(source, target):
        def body(r):
            target[0, pl.ds(r, 32)], target[1, pl.ds(r, 32)] = split(source[pl.ds(r, 32)])

        blocks(source.shape[0], 32, body)

    def reduce0(c):
        cols = slice(c * width, (c + 1) * width)
        right = u[0, 0, :, cols], u[0, 1, :, cols]

        def body(r):
            rest[pl.ds(r, 96), cols] -= times((low0[0, pl.ds(r, 96)], low0[1, pl.ds(r, 96)]), right)

        blocks(width + tail, 96, body)

    def find_lower1():
        @pl.when(col == 1)
        def _():
            right = uinv[1, 0], uinv[1, 1]

            def body(r):
                lower1[pl.ds(r, 32)] = times(split(rest[pl.ds(width + r, 32), 0:width]), right)

            blocks(tail, 32, body)

    def solve1(c):
        cols = slice(c * width, (c + 1) * width)
        right = split(rest[0:width, cols])

        def body(r):
            value = times((linv[1, 0, pl.ds(r, 128)], linv[1, 1, pl.ds(r, 128)]), right)
            u[1, 0, pl.ds(r, 128), cols], u[1, 1, pl.ds(r, 128), cols] = split(value)
            solved[pl.ds(r, 128)] = value

        blocks(width, 128, body)
        out_ref[part:top, cols] = own(solved)
        if c == 0:

            @pl.when(col <= 1)
            def _():
                mine = jnp.where(col == 0, own(lower0), rest[pl.ds(pl.multiple_of(me * part, part), part), cols])
                out_ref[part:top, cols] = mine
                u[1, :, :, cols] = jnp.zeros((2, width, width), jnp.bfloat16)

    def reduce1(c):
        cols = slice(c * width, (c + 1) * width)
        right = u[1, 0, :, cols], u[1, 1, :, cols]

        def body(r):
            value = rest[pl.ds(width + r, 32), cols] - times((low1[0, pl.ds(r, 32)], low1[1, pl.ds(r, 32)]), right)
            if c == 0:
                value = jnp.where(col == 0, lower0[pl.ds(width + r, 32)], jnp.where(col == 1, lower1[pl.ds(r, 32)], value))
            out_ref[pl.ds(top + r, 32), cols] = value

        blocks(tail, 32, body)

    def run(stage, amount=None):
        for _ in range(len(queue[stage]) if amount is None else min(amount, len(queue[stage]))):
            queue[stage].pop(0)()

    def stage_mix(stage, actions):
        total = len(queue[stage])
        for number, action in enumerate(actions):
            run(stage, (number + 1) * total // (len(actions) + 1) - (total - len(queue[stage])))
            action()
        run(stage)

    P_ = functools.partial
    stage_mix(0, [prepare, place_moved])
    stage_mix(1, [P_(permute, 0), find_lower0, spread0.begin, P_(solve0, 0)])
    stage_mix(2, [spread0.middle, P_(split_lower, lower0, low0), P_(reduce0, 0), find_lower1, spread1.begin,
                  P_(permute, 1), P_(solve0, 1), P_(reduce0, 1), P_(solve1, 0), P_(solve1, 1)])
    permute(2)
    solve0(2)
    reduce0(2)
    solve1(2)
    spread1.middle()
    split_lower(lower1, low1)
    for c in range(chunks):
        reduce1(c)
    for copy in started:
        copy.wait_send()
    for piece in pieces:
        for copy in piece.started:
            copy.wait_send()
    spread0.finish()
    spread1.finish()


def two_panels(matrix, plan, lower_inv, upper_inv):
    rows, columns = matrix.shape
    width = lower_inv.shape[1]
    count, top, size, tile = NX * NZ, 2 * width // (NX * NZ), 2 * width // NZ, width // NX
    chunks, tail = columns // width, rows - top
    vmem = pl.BlockSpec(memory_space=pltpu.VMEM)
    f32, bf16, dma = jnp.float32, jnp.bfloat16, pltpu.SemaphoreType.DMA
    return pl.pallas_call(
        panels_kernel,
        out_shape=jax.ShapeDtypeStruct((rows, columns), f32),
        in_specs=[vmem] * 8,
        out_specs=vmem,
        scratch_shapes=[
            pltpu.VMEM((NX, top, columns), f32),
            pltpu.VMEM((NZ, MOVED_ROWS, columns), f32),
            pltpu.VMEM((NZ, MOVED_ROWS, columns), f32),
            pltpu.VMEM((count, CLASS_ROWS, columns // NX), f32),
            pltpu.VMEM((count, CLASS_ROWS, columns // NX), f32),
            pltpu.VMEM((chunks, NX, 2 * width, tile), f32),
            pltpu.VMEM((2 * width, 2 * width), bf16),
            pltpu.VMEM((2, 2, width, width), bf16),
            pltpu.VMEM((2, 2, width, width), bf16),
            pltpu.VMEM((2, 2 * width, width), bf16),
            pltpu.VMEM((2, 2, width, columns), bf16),
            pltpu.VMEM((width + tail, columns), f32),
            pltpu.VMEM((width + tail, width), f32),
            pltpu.VMEM((tail, width), f32),
            pltpu.VMEM((2, width + tail, width), bf16),
            pltpu.VMEM((2, tail, width), bf16),
            pltpu.VMEM((width, width), f32),
            dma((2, count)),
            dma((2, NZ)),
            dma((2, NX)),
            dma((2 * chunks, count, 4)),
            dma((2 * chunks, count, 2)),
            dma((4, 6)),
            dma((4, 4)),
        ],
        compiler_params=pltpu.CompilerParams(
            collective_id=0, has_side_effects=True, vmem_limit_bytes=62 * 2**20
        ),
        name="two_panels",
    )(matrix, *plan, lower_inv, upper_inv)


def local(matrix, pivots, lower_inv, upper_inv):
    row_blocks, row_part, col_blocks, col_part = matrix.shape
    width = lower_inv.shape[1]
    *plan, most = make_plan(pivots, width, row_blocks * row_part)
    return lax.cond(
        most[0, 0] <= 0,
        lambda m, p, a, b, q: two_panels(m.reshape(row_blocks * row_part, -1), q, a, b).reshape(m.shape),
        lambda m, p, a, b, q: general(m, p, a, b),
        matrix, pivots, lower_inv, upper_inv, plan,
    )


def solution(mesh):
    finer = Mesh(mesh.devices.reshape(NX, NZ, mesh.shape["pcol"]), ("x", "z", "pcol"))
    in_specs = (P(None, PROW, None, "pcol"), P(), P(), P())
    out_specs = P(None, PROW, None, "pcol")
    return jax.shard_map(local, mesh=finer, in_specs=in_specs, out_specs=out_specs, check_vma=False)
```

```python
import functools

import jax
import jax.numpy as jnp
from jax import lax
from jax.experimental import pallas as pl
from jax.experimental.pallas import tpu as pltpu
from jax.sharding import Mesh
from jax.sharding import PartitionSpec as P

PROW = ("x", "z")
MESH = pl.DeviceIdType.MESH
NX, NZ = 4, 8


def in_order(parts, dim):
    shape = list(parts.shape[1:])
    shape[dim] *= parts.shape[0]
    return jnp.moveaxis(parts, 0, dim).reshape(shape)


def all_blocks(x, axes, order):
    parts = x
    for k in order:
        parts = lax.all_gather(parts, axes[k])
    done = order[::-1]
    back = [done.index(k) for k in range(len(axes))]
    parts = parts.transpose(*back, *range(len(axes), parts.ndim))
    return parts.reshape(-1, *x.shape)


def gathered_by_axis(x, axes, order, dim):
    return in_order(all_blocks(x, axes, order), dim)


def sum_by_axis(x, axes, dim):
    for axis in axes:
        x = lax.psum_scatter(x, axis, scatter_dimension=dim, tiled=True)
    return x


def broadcast(x, axis, root):
    return lax.dynamic_index_in_dim(lax.all_gather(x, axis), root, 0, keepdims=False)


def permutation(pivot_row, offset, panel_width, full_order):
    steps = jnp.arange(panel_width, dtype=jnp.int32)
    anchors = offset + steps
    earlier = steps[None, :] < steps[:, None]
    hits_anchor = (pivot_row[None, :] == anchors[:, None]) & earlier
    chain_from = jnp.max(jnp.where(hits_anchor, steps[None, :], -1), axis=1)
    pointer = jnp.where(chain_from >= 0, chain_from, steps)
    for level in range(max(1, panel_width.bit_length())):
        pointer = pointer[pointer]
    before_value = offset + pointer
    same_target = (pivot_row[None, :] == pivot_row[:, None]) & earlier
    last_before = jnp.max(jnp.where(same_target, steps[None, :], -1), axis=1)
    anchor_value = jnp.where(
        last_before >= 0, before_value[jnp.clip(last_before, 0, panel_width - 1)], pivot_row
    )
    later = steps[None, :] > steps[:, None]
    has_later = jnp.any((pivot_row[None, :] == pivot_row[:, None]) & later, axis=1)
    outside = jnp.logical_not(has_later) & (pivot_row >= offset + panel_width)
    spots = jnp.where(outside, pivot_row, full_order)
    ordering = jnp.arange(full_order, dtype=jnp.int32).at[spots].set(before_value, mode="drop")
    return lax.dynamic_update_slice_in_dim(ordering, anchor_value, offset, 0)


def product(left, right):
    return jnp.dot(left, right, precision=lax.Precision.HIGHEST, preferred_element_type=jnp.float32)


def general(matrix, pivots, lower_inv, upper_inv):
    row_blocks, row_part, col_blocks, col_part = matrix.shape
    panel_width = lower_inv.shape[1]
    panel_count = pivots.shape[0]
    full_order = row_blocks * panel_width
    row_devices = lax.axis_size(PROW)
    col_devices = lax.axis_size("pcol")
    row_index = lax.axis_index(PROW)
    col_index = lax.axis_index("pcol")
    local_rows = row_blocks * row_part
    local_cols = col_blocks * col_part
    share_width = local_cols // row_devices
    current = matrix.reshape(local_rows, local_cols)
    global_rows = (
        jnp.arange(row_blocks, dtype=jnp.int32)[:, None] * panel_width
        + row_index * row_part
        + jnp.arange(row_part, dtype=jnp.int32)[None, :]
    ).reshape(local_rows)
    col_span = col_devices * col_part
    global_cols = (
        jnp.arange(col_blocks, dtype=jnp.int32)[:, None] * col_span
        + col_index * col_part
        + jnp.arange(col_part, dtype=jnp.int32)[None, :]
    ).reshape(local_cols)

    def panel(panel_index, current):
        offset = panel_index * panel_width
        ending = offset + panel_width
        ordering = permutation(pivots[panel_index], offset, panel_width, full_order)
        source = ordering[global_rows]
        old_top = lax.dynamic_slice_in_dim(current, panel_index * row_part, row_part, 0)
        old_panel = gathered_by_axis(old_top, PROW, (0, 1), 0)
        wanted = ordering[offset + jnp.arange(panel_width, dtype=jnp.int32)]
        holder = wanted % panel_width // row_part
        local_spot = wanted // panel_width * row_part + wanted % row_part
        picked = jnp.where((holder == row_index)[:, None], current[local_spot], 0.0)
        column_share = sum_by_axis(picked, PROW, 1)
        share_cols = lax.dynamic_slice_in_dim(global_cols, row_index * share_width, share_width)
        solved = product(lower_inv[panel_index], column_share)
        merged = jnp.where((share_cols >= ending)[None, :], solved, column_share)
        top_rows = gathered_by_axis(merged, PROW, (0, 1), 1)
        in_panel = global_rows // panel_width == panel_index
        displaced = (source != global_rows) & jnp.logical_not(in_panel)
        from_old = old_panel[jnp.clip(source - offset, 0, panel_width - 1)]
        current = jnp.where(displaced[:, None], from_old, current)
        own_rows = lax.dynamic_slice_in_dim(top_rows, row_index * row_part, row_part, 0)
        current = lax.dynamic_update_slice_in_dim(current, own_rows, panel_index * row_part, 0)
        trailing_row = global_rows >= ending
        trailing_col = global_cols >= ending
        lower_full = product(current[:, :col_part], upper_inv[panel_index])
        lower_here = jnp.where(trailing_row[:, None], lower_full, 0.0)
        lower_rows = broadcast(lower_here, "pcol", panel_index)
        upper_part = jnp.where(trailing_col[None, :], top_rows, 0.0)
        current = current - product(lower_rows, upper_part)
        own_panel = col_index == panel_index
        new_cols = jnp.where(own_panel & trailing_row[:, None], lower_rows, current[:, :col_part])
        return jnp.concatenate([new_cols, current[:, col_part:]], axis=1)

    current = lax.fori_loop(0, panel_count, panel, current)
    return current.reshape(row_blocks, row_part, col_blocks, col_part)


CLASS_ROWS = 8
MOVED_ROWS = 16


def to_column(row):
    n = row.shape[1]
    eye = lax.broadcasted_iota(jnp.int32, (n, n), 0) == lax.broadcasted_iota(jnp.int32, (n, n), 1)
    return jnp.max(jnp.where(eye, row, -1.0), axis=1, keepdims=True)


def lookup(keys, values, wanted):
    return jnp.max(jnp.where(keys == wanted, values, -1.0), axis=0, keepdims=True)


def find(size, keys, values):
    found = jnp.full((size, 1), -1.0, jnp.float32)
    for key, value in zip(keys, values):
        number = lax.broadcasted_iota(jnp.int32, (size, key.shape[1]), 0).astype(jnp.float32)
        found = jnp.maximum(found, jnp.max(jnp.where(number == key, value, -1.0), axis=1, keepdims=True))
    return found.astype(jnp.int32)


def ranks_of(keys, columns, j, i):
    ranks, smaller = [], []
    for k in range(2):
        rank = jnp.sum(jnp.where((columns[k] == keys[k]) & (j < i), 1.0, 0.0), axis=0, keepdims=True)
        if k == 1:
            rank = rank + jnp.sum(jnp.where(columns[0] == keys[1], 1.0, 0.0), axis=0, keepdims=True)
        ranks.append(rank)
        smaller.append(
            sum(jnp.sum(jnp.where(column < keys[k], 1.0, 0.0), axis=0, keepdims=True) for column in columns)
        )
    return ranks, smaller


def plan_kernel(width, piv_row_ref, pick_ref, fold_ref, perm_ref, pack_ref, place_ref, most_ref):
    me = (lax.axis_index("x") * NZ + lax.axis_index("z")).astype(jnp.float32)
    my_x, my_z = lax.axis_index("x").astype(jnp.float32), lax.axis_index("z").astype(jnp.float32)
    part = width // (NX * NZ)
    j = lax.broadcasted_iota(jnp.int32, (width, width), 0).astype(jnp.float32)
    i = lax.broadcasted_iota(jnp.int32, (width, width), 1).astype(jnp.float32)
    i_row = i[:1]
    sources, spots, spot_cols, befores, before_cols = [], [], [], [], []
    for k in range(2):
        offset = float(k * width)
        p_row = piv_row_ref[k : k + 1, :].astype(jnp.float32)
        p_col = to_column(p_row)
        chain = jnp.max(jnp.where((p_col == offset + i) & (j < i), j, -1.0), axis=0, keepdims=True)
        start = jnp.where(chain >= 0.0, chain, i_row)

        def again(state):
            return state[1] > 0.0

        def jump(state):
            pointer = state[0]
            found = lookup(j[:, :1], to_column(pointer), pointer)
            return found, jnp.max(jnp.abs(found - pointer))

        pointer, _ = lax.while_loop(again, jump, (start, jnp.float32(1.0)))
        before = offset + pointer
        before_col = to_column(before)
        same = p_col == p_row
        last = jnp.max(jnp.where(same & (j < i), j, -1.0), axis=0, keepdims=True)
        later = jnp.max(jnp.where(same & (j > i), 1.0, 0.0), axis=0, keepdims=True)
        anchor = jnp.where(last >= 0.0, lookup(j[:, :1], before_col, last), p_row)
        spot = jnp.where((later == 0.0) & (p_row >= offset + width), p_row, -5.0)
        if k == 1:
            moved = lookup(spot_cols[0], before_cols[0], anchor)
            anchor = jnp.where(moved >= 0.0, moved, anchor)
        sources.append(anchor)
        spots.append(spot)
        spot_cols.append(jnp.max(jnp.where(i == j, spot, -5.0), axis=1, keepdims=True))
        befores.append(before)
        before_cols.append(before_col)

    def divided(value, by):
        return jnp.floor(value * (1.0 / by))

    def holder_and_place(source):
        block = divided(source, width)
        within = source - block * width
        holder = divided(within, part)
        return holder, block * part + within - holder * part

    holders, places = zip(*[holder_and_place(source) for source in sources])
    ranks, smaller = ranks_of(holders, [to_column(h) for h in holders], j, i)
    most = jnp.zeros((1, 1), jnp.float32)
    picks, folds, pick_keys, fold_keys = [], [], [], []
    for k in range(2):
        number = smaller[k] + ranks[k]
        at = divided(number, NZ)
        kind = number - at * NZ
        slot = at - divided(smaller[k] - kind + (NZ - 1.0), NZ)
        most = jnp.maximum(most, jnp.max(slot, axis=1, keepdims=True) - (CLASS_ROWS - 1.0))
        good = slot < CLASS_ROWS
        pick_keys.append(jnp.where((holders[k] == me) & good, kind * CLASS_ROWS + slot, -1.0))
        picks.append(places[k])
        fold_keys.append(jnp.where((kind == my_z) & good, at, -1.0))
        folds.append(holders[k] * CLASS_ROWS + slot)
        perm_ref[k * width : (k + 1) * width, :] = to_column(kind * (2 * width // NZ) + at).astype(jnp.int32)
    pick_ref[...] = find(pick_ref.shape[0], pick_keys, picks)
    fold_ref[...] = find(fold_ref.shape[0], fold_keys, folds)

    landed = lookup(spot_cols[0], before_cols[0], befores[1])
    origins = [befores[0], jnp.where(landed >= 0.0, landed, befores[1])]
    taken = lookup(spot_cols[1], spot_cols[1], spots[0])
    targets = [
        jnp.where((spots[0] >= 2.0 * width) & (taken < 0.0), spots[0], -1.0),
        jnp.where(spots[1] >= 2.0 * width, spots[1], -1.0),
    ]
    owners, rows = zip(*[holder_and_place(origin) for origin in origins])
    ends, spot_rows = zip(*[holder_and_place(jnp.maximum(target, 0.0)) for target in targets])
    owner_x = [divided(owner, NZ) for owner in owners]
    owner_z = [owner - x * NZ for owner, x in zip(owners, owner_x)]
    keys = [
        jnp.where(targets[k] >= 0.0, owner_z[k] * (NX * NZ) + ends[k], 2000.0 + i_row + 600.0 * k) for k in range(2)
    ]
    ranks, _ = ranks_of(keys, [to_column(key) for key in keys], j, i)
    pack_keys, packs, place_keys, place_values = [], [], [], []
    for k in range(2):
        most = jnp.maximum(most, jnp.max(ranks[k], axis=1, keepdims=True) - (MOVED_ROWS - 1.0))
        good = (targets[k] >= 0.0) & (ranks[k] < MOVED_ROWS)
        end_x = divided(ends[k], NZ)
        end_z = ends[k] - end_x * NZ
        pack_keys.append(
            jnp.where(good & (owner_z[k] == my_z) & (end_x == my_x), end_z * MOVED_ROWS + ranks[k], -1.0)
        )
        packs.append(owner_x[k] * (2 * part) + rows[k])
        place_keys.append(jnp.where(good & (ends[k] == me), spot_rows[k], -1.0))
        place_values.append(owner_z[k] * MOVED_ROWS + ranks[k])
    pack_ref[...] = find(pack_ref.shape[0], pack_keys, packs)
    place_ref[...] = find(place_ref.shape[0], place_keys, place_values)
    most_ref[...] = jnp.broadcast_to(most, most_ref.shape).astype(jnp.int32)


def make_plan(pivots, width, rows):
    vmem = pl.BlockSpec(memory_space=pltpu.VMEM)
    sizes = [NZ * CLASS_ROWS, 2 * width // NZ, 2 * width, NZ * MOVED_ROWS, rows]
    shapes = [(n, 1) for n in sizes] + [(8, 128)]
    return pl.pallas_call(
        functools.partial(plan_kernel, width),
        out_shape=[jax.ShapeDtypeStruct(shape, jnp.int32) for shape in shapes],
        in_specs=[vmem],
        out_specs=[vmem] * len(shapes),
        name="row_plan",
    )(pivots)


class Piece:
    def __init__(self, buf, low, high, first, x, z, col, send_sem, recv_sem):
        self.buf, self.low, self.high, self.first = buf, low, high, first
        self.x, self.z, self.col = x, z, col
        self.send_sem, self.recv_sem = send_sem, recv_sem
        self.started = []
        self.na, self.nb = (NX, NZ) if first == "x" else (NZ, NX)
        self.a, self.b = (x, z) if first == "x" else (z, x)

    def place(self, da, db):
        a, b = lax.rem(self.a + da + self.na, self.na), lax.rem(self.b + db + self.nb, self.nb)
        return (a, b) if self.first == "x" else (b, a)

    def copy(self, da, db, to, half, k):
        bx, bz = self.place(da, db)
        middle = (self.low + self.high) // 16 * 8
        low, high = ((self.low, self.high), (self.low, middle), (middle, self.high))[0 if half is None else half + 1]
        view = self.buf.at[bx, bz, low:high]
        return pltpu.make_async_remote_copy(
            src_ref=view,
            dst_ref=view,
            send_sem=self.send_sem.at[bx * NZ + bz, k],
            recv_sem=self.recv_sem.at[bx * NZ + bz, half or 0],
            device_id=self.place(*to) + (self.col,),
            device_id_type=MESH,
        )

    def send(self, da, db, to, half, k):
        copy = self.copy(da, db, to, half, k)
        copy.start()
        self.started.append(copy)

    def receive(self, da, db, half):
        self.copy(da, db, (0, 1), half, 0).wait_recv()

    def along_first(self, d):
        for s in (1, -1):
            if d + 1 <= self.na // 2:
                half = None if d + 1 < self.na // 2 else (1 - s) // 2
                self.send(-s * d, 0, (s, 0), half, (1 - s) // 2)

    def along_second(self, da, d):
        for s in (1, -1):
            if d + 1 <= self.nb // 2:
                half = None if d + 1 < self.nb // 2 else (1 - s) // 2
                self.send(da, -s * d, (0, s), half, (1 - s) // 2 + (2 if d == 0 else 0))

    def first_step(self, d):
        if d == 0:
            self.along_first(0)
            self.along_second(0, 0)
        elif d < self.na // 2:
            for s in (1, -1):
                self.receive(-s * d, 0, None)
            self.along_first(d)
            for s in (1, -1):
                self.along_second(-s * d, 0)
        else:
            self.receive(d, 0, 0)
            self.receive(d, 0, 1)
            self.along_second(d, 0)

    def second_step(self, da, d):
        if d < self.nb // 2:
            for s in (1, -1):
                self.receive(da, -s * d, None)
            self.along_second(da, d)
        else:
            self.receive(da, d, 0)
            self.receive(da, d, 1)

    def steps(self):
        work = [(d, functools.partial(self.first_step, d)) for d in range(self.na // 2 + 1)]
        for d in range(1, self.nb // 2 + 1):
            for ad in range(self.na // 2 + 1):
                for da in [0] if ad == 0 else [ad] if ad == self.na // 2 else [-ad, ad]:
                    work.append((ad + d + 0.5, functools.partial(self.second_step, da, d)))
        return work


class Spread:
    def __init__(self, buf, root, x, z, col, sems):
        self.buf, self.root, self.x, self.z, self.col, self.sems = buf, root, x, z, col, sems
        y, self.core = col // 2, lax.rem(col, 2)
        self.mate = y * 2 + 1 - self.core
        self.up = lax.rem(y + 1, 4) * 2 + self.core
        self.down = lax.rem(y + 3, 4) * 2 + self.core
        self.away = lax.rem(y - root // 2 + 4, 4)

    def copy(self, half, device, k, pair):
        rows = self.buf.shape[0] // 2
        view = self.buf.at[half * rows : (half + 1) * rows]
        return pltpu.make_async_remote_copy(
            src_ref=view,
            dst_ref=view,
            send_sem=self.sems.at[0, half, k],
            recv_sem=self.sems.at[1, half, pair],
            device_id=(self.x, self.z, device),
            device_id_type=MESH,
        )

    def sends(self, hops):
        up = [self.copy(half, self.up, 0, 0) for half in ((0, 1) if hops == 0 else (0,) if hops == 1 else ())]
        down = [self.copy(half, self.down, 1, 0) for half in ((1, 0) if hops == 0 else (1,) if hops == 3 else ())]
        return up, down

    def pass_on(self, half):
        self.copy(half, self.up, 0, 0).wait_recv()
        self.copy(half, self.mate, 2, 1).start()

    def at(self, hops, action):
        pl.when((self.core == self.root % 2) & (self.away == hops))(action)

    def begin(self):
        @pl.when(self.col == self.root)
        def _():
            up, down = self.sends(0)
            for n in range(2):
                up[n].start()
                down[n].start()
                self.copy(n, self.mate, 2, 1).start()

    def relay(self):
        for hops, half in ((1, 0), (3, 1)):

            def action(hops=hops, half=half):
                self.copy(half, self.up, 0, 0).wait_recv()
                for copy in sum(self.sends(hops), []):
                    copy.start()
                self.copy(half, self.mate, 2, 1).start()

            self.at(hops, action)

    def finish(self):
        self.at(1, functools.partial(self.pass_on, 1))
        self.at(3, functools.partial(self.pass_on, 0))

        def both():
            self.pass_on(0)
            self.pass_on(1)

        self.at(2, both)

        @pl.when(self.core != self.root % 2)
        def _():
            for half in range(2):
                self.copy(half, self.mate, 2, 1).wait_recv()

    def close(self):
        for hops in range(4):

            def action(hops=hops):
                for copy in sum(self.sends(hops), []):
                    copy.wait_send()
                for half in range(2):
                    self.copy(half, self.mate, 2, 1).wait_send()

            self.at(hops, action)


def dot(left, right):
    return jnp.dot(left, right, preferred_element_type=jnp.float32)


def split(value):
    high = value.astype(jnp.bfloat16)
    return high, (value - high.astype(jnp.float32)).astype(jnp.bfloat16)


def split_three(value):
    high, rest = split(value)
    low = value - high.astype(jnp.float32) - rest.astype(jnp.float32)
    return high, rest, low.astype(jnp.bfloat16)


def exact(hot, value):
    return sum(dot(hot, term) for term in split_three(value))


def times(left, right):
    return dot(left[0], right[0]) + (dot(left[0], right[1]) + dot(left[1], right[0]))


def hot_of(column, lanes):
    number = lax.broadcasted_iota(jnp.int32, (column.shape[0], lanes), 1)
    return jnp.where(column == number, 1.0, 0.0).astype(jnp.bfloat16)


def blocks(total, step, body):
    def one(n, carry):
        body(pl.multiple_of(n * step, step))
        return carry

    lax.fori_loop(0, total // step, one, 0)


ROWS, BODY, TAIL = 256, 288, 176
LAG, X_ROWS = 3.5, 48


def panels_kernel(
    m_ref, pick_ref, fold_ref, perm_ref, pack_ref, place_ref, linv_ref, uinv_ref, out_ref,
    old, pack_box, place_box, outbox, inbox, g, hot, linv, uinv, t, u, rest, lower0, lower1, low0, low1, solved,
    box_sem, move_sem, old_sem, ring_send, ring_recv, spread_sem0, spread_sem1,
):
    x, z, col = lax.axis_index("x"), lax.axis_index("z"), lax.axis_index("pcol")
    me = x * NZ + z
    count = NX * NZ
    width = linv_ref.shape[1]
    part = width // count
    top = 2 * part
    row_blocks, chunks = m_ref.shape[:2]
    rows, columns = row_blocks * part, chunks * width
    size = 2 * width // NZ
    tail = rows - top
    spread0 = Spread(lower0, 0, x, z, col, spread_sem0)
    spread1 = Spread(lower1, 1, x, z, col, spread_sem1)
    started = []

    others = [lax.rem(me + n, count) for n in range(1, count)]
    barrier = pltpu.get_barrier_semaphore()
    greeted = [(o // NZ, lax.rem(o, NZ), col) for o in others]
    greeted += [(x, z, spread0.mate), (x, z, spread0.up), (x, z, spread0.down)]
    for device in greeted:
        pl.semaphore_signal(barrier, inc=1, device_id=device, device_id_type=MESH)

    for c in range(chunks):
        old[pl.ds(x, 1), :, c * width : (c + 1) * width] = m_ref[0:2, c].reshape(1, top, width)
    pick_hot = hot_of(pick_ref[...], rows)
    tile = width // NX
    for c in range(chunks):
        picked = exact(pick_hot, m_ref[:, c].reshape(rows, width))
        for xs in range(NX):
            outbox[xs * NZ : (xs + 1) * NZ, :, c * tile : (c + 1) * tile] = picked[
                :, xs * tile : (xs + 1) * tile
            ].reshape(NZ, -1, tile)
    inbox[pl.ds(me, 1)] = outbox[pl.ds(me, 1)]
    pl.semaphore_wait(barrier, len(greeted))

    def send(src, dst, send_sem, recv_sem, device):
        copy = pltpu.make_async_remote_copy(
            src_ref=src, dst_ref=dst, send_sem=send_sem, recv_sem=recv_sem, device_id=device, device_id_type=MESH
        )
        copy.start()
        started.append(copy)

    for o in others:
        send(outbox.at[o], inbox.at[me], box_sem.at[0, o], box_sem.at[1, me], (o // NZ, lax.rem(o, NZ), col))
    for d in range(1, NX):
        to = lax.rem(x + d, NX)
        send(old.at[x], old.at[x], old_sem.at[0, to], old_sem.at[1, x], (to, z, col))

    def arrive(view, sem):
        pltpu.make_async_remote_copy(
            src_ref=view, dst_ref=view, send_sem=sem, recv_sem=sem, device_id=(lax.rem(x + 1, NX), z, col),
            device_id_type=MESH,
        ).wait_recv()

    for d in range(1, NX):
        xs = lax.rem(x + d, NX)
        arrive(old.at[xs], old_sem.at[1, xs])
    pack_hot = hot_of(pack_ref[...], NX * top)
    for c in range(0, columns, width):
        packed = exact(pack_hot, old[:, :, c : c + width].reshape(NX * top, width))
        pack_box[:, :, c : c + width] = packed.reshape(NZ, -1, width)
    place_box[pl.ds(z, 1)] = pack_box[pl.ds(z, 1)]
    for o in others:
        arrive(inbox.at[o], box_sem.at[1, o])
    fold_hot = hot_of(fold_ref[...], count * CLASS_ROWS)
    for c in range(chunks):
        mine = exact(fold_hot, inbox[:, :, c * tile : (c + 1) * tile].reshape(count * CLASS_ROWS, tile))
        g[c, pl.ds(x, 1), pl.ds(z, 1)] = mine[None, None]

    pieces, work = [], []
    for c in range(chunks):
        for number, (first, low, high) in enumerate((("x", 0, X_ROWS), ("z", X_ROWS, size))):
            s = 2 * c + number
            pieces.append(Piece(g.at[c], low, high, first, x, z, col, ring_send.at[s], ring_recv.at[s]))
    flow = []
    for number, piece in enumerate(pieces):
        for place, (when, step) in enumerate(piece.steps()):
            flow.append((when + LAG * (number // 2) if when else -1.0, number, place, number // 2, step))
    flow.sort(key=lambda entry: entry[:3])
    for _ in range(2):
        flow.pop(0)[4]()
    for d in range(1, NZ):
        to = lax.rem(z + d, NZ)
        send(pack_box.at[to], place_box.at[z], move_sem.at[0, to], move_sem.at[1, z], (x, to, col))
    for _ in range(2 * chunks - 2):
        flow.pop(0)[4]()

    def prepare():
        for k in range(2):
            linv[k, 0], linv[k, 1] = split(linv_ref[k])
            uinv[k, 0], uinv[k, 1] = split(uinv_ref[k])

        def perm(r):
            hot[pl.ds(r, 128)] = hot_of(perm_ref[pl.ds(r, 128), :], 2 * width)

        blocks(2 * width, 128, perm)

    def place_moved():
        for d in range(1, NZ):
            zs = lax.rem(z + d, NZ)
            arrive(place_box.at[zs], move_sem.at[1, zs])
        column = place_ref[...]
        place_hot = hot_of(column[top:], NZ * MOVED_ROWS)
        for c in range(chunks):
            cols = slice(c * width, (c + 1) * width)
            moved = exact(place_hot, place_box[:, :, cols].reshape(NZ * MOVED_ROWS, width))
            rest[width:, cols] = jnp.where(column[top:] >= 0, moved, m_ref[2:, c].reshape(tail, width))

    def permute(c):
        whole = jnp.concatenate([g[c, n].reshape(2 * width, tile) for n in range(NX)], axis=1)
        high, middle = split(whole)

        def body(r):
            left = hot[pl.ds(r, ROWS)]
            first, second = dot(left, high), dot(left, middle)
            t[0, pl.ds(r, ROWS)] = first.astype(jnp.bfloat16)
            t[1, pl.ds(r, ROWS)] = second.astype(jnp.bfloat16)

            @pl.when(r >= width)
            def _():
                rest[pl.ds(r - width, ROWS), c * width : (c + 1) * width] = first + second

        blocks(2 * width, ROWS, body)

    def own(ref):
        return ref[pl.ds(pl.multiple_of(me * part, part), part)]

    def solve0(c):
        right = t[0, 0:width], t[1, 0:width]
        cols = slice(c * width, (c + 1) * width)

        def body(r):
            value = times((linv[0, 0, pl.ds(r, ROWS)], linv[0, 1, pl.ds(r, ROWS)]), right)
            u[0, 0, pl.ds(r, ROWS), cols], u[0, 1, pl.ds(r, ROWS), cols] = split(value)
            solved[pl.ds(r, ROWS)] = value

        blocks(width, ROWS, body)
        out_ref[0, c] = own(solved)
        if c == 0:

            @pl.when(col == 0)
            def _():
                out_ref[0, c] = own(t.at[0]).astype(jnp.float32) + own(t.at[1]).astype(jnp.float32)
                u[0, :, :, cols] = jnp.zeros((2, width, width), jnp.bfloat16)

    def find_lower0():
        @pl.when(col == 0)
        def _():
            right = uinv[0, 0], uinv[0, 1]

            def body(r):
                lower0[pl.ds(r, BODY)] = times(split(rest[pl.ds(r, BODY), 0:width]), right)

            blocks(width + tail, BODY, body)

    def split_lower(source, target):
        def body(r):
            target[0, pl.ds(r, 32)], target[1, pl.ds(r, 32)] = split(source[pl.ds(r, 32)])

        blocks(source.shape[0], 32, body)

    def reduce0(c):
        cols = slice(c * width, (c + 1) * width)
        right = u[0, 0, :, cols], u[0, 1, :, cols]

        def body(r):
            rest[pl.ds(r, BODY), cols] -= times((low0[0, pl.ds(r, BODY)], low0[1, pl.ds(r, BODY)]), right)

        blocks(width + tail, BODY, body)

    def find_lower1():
        right = uinv[1, 0], uinv[1, 1]

        def body(r):
            lower1[pl.ds(r, TAIL)] = times(split(rest[pl.ds(width + r, TAIL), 0:width]), right)

        blocks(tail, TAIL, body)

    def solve1(c):
        cols = slice(c * width, (c + 1) * width)
        right = split(rest[0:width, cols])

        def body(r):
            value = times((linv[1, 0, pl.ds(r, ROWS)], linv[1, 1, pl.ds(r, ROWS)]), right)
            u[1, 0, pl.ds(r, ROWS), cols], u[1, 1, pl.ds(r, ROWS), cols] = split(value)
            solved[pl.ds(r, ROWS)] = value

        blocks(width, ROWS, body)
        out_ref[1, c] = own(solved)
        if c == 0:

            @pl.when(col <= 1)
            def _():
                mine = jnp.where(col == 0, own(lower0), rest[pl.ds(pl.multiple_of(me * part, part), part), cols])
                out_ref[1, c] = mine
                u[1, :, :, cols] = jnp.zeros((2, width, width), jnp.bfloat16)

    def reduce1(c):
        cols = slice(c * width, (c + 1) * width)
        right = u[1, 0, :, cols], u[1, 1, :, cols]

        def body(r):
            value = rest[pl.ds(width + r, TAIL), cols] - times((low1[0, pl.ds(r, TAIL)], low1[1, pl.ds(r, TAIL)]), right)
            if c == 0:
                value = jnp.where(col == 0, lower0[pl.ds(width + r, TAIL)], jnp.where(col == 1, lower1[pl.ds(r, TAIL)], value))
            out_ref[pl.ds(2 + r // part, TAIL // part), c] = value.reshape(TAIL // part, part, width)

        blocks(tail, TAIL, body)

    def left_of(stage):
        return max([n + 1 for n, entry in enumerate(flow) if entry[3] <= stage], default=0)

    def mix(stage, actions):
        total = left_of(stage)
        done = 0
        for number, action in enumerate(actions):
            until = (number + 1) * total // (len(actions) + 1)
            for _ in range(until - done):
                flow.pop(0)[4]()
            done = until
            action()
        for _ in range(total - done):
            flow.pop(0)[4]()

    P_ = functools.partial
    def lower_arrives():
        spread0.finish()
        split_lower(lower0, low0)
        reduce0(0)

    def early():
        @pl.when(col == 1)
        def _():
            lower_arrives()
            find_lower1()

        spread1.begin()

    def late():
        pl.when(col != 1)(lower_arrives)

    mix(0, [prepare])
    place_moved()
    permute(0)
    find_lower0()
    spread0.begin()
    solve0(0)
    early()
    mix(1, [spread0.relay])
    mix(2, [P_(permute, 1), P_(solve0, 1), late, spread1.relay, P_(reduce0, 1), P_(solve1, 0)])
    permute(2)
    solve0(2)
    reduce0(2)
    solve1(1)
    solve1(2)
    spread1.finish()
    split_lower(lower1, low1)
    for c in range(chunks):
        reduce1(c)
    for copy in started:
        copy.wait_send()
    for piece in pieces:
        for copy in piece.started:
            copy.wait_send()
    spread0.close()
    spread1.close()


def two_panels(matrix, plan, lower_inv, upper_inv):
    row_blocks, part, chunks, width = matrix.shape
    rows, columns = row_blocks * part, chunks * width
    count, top, size, tile = NX * NZ, 2 * width // (NX * NZ), 2 * width // NZ, width // NX
    tail = rows - top
    vmem = pl.BlockSpec(memory_space=pltpu.VMEM)
    f32, bf16, dma = jnp.float32, jnp.bfloat16, pltpu.SemaphoreType.DMA
    result = pl.pallas_call(
        panels_kernel,
        out_shape=jax.ShapeDtypeStruct((row_blocks, chunks, part, width), f32),
        in_specs=[vmem] * 8,
        out_specs=vmem,
        scratch_shapes=[
            pltpu.VMEM((NX, top, columns), f32),
            pltpu.VMEM((NZ, MOVED_ROWS, columns), f32),
            pltpu.VMEM((NZ, MOVED_ROWS, columns), f32),
            pltpu.VMEM((count, CLASS_ROWS, columns // NX), f32),
            pltpu.VMEM((count, CLASS_ROWS, columns // NX), f32),
            pltpu.VMEM((chunks, NX, NZ, size, tile), f32),
            pltpu.VMEM((2 * width, 2 * width), bf16),
            pltpu.VMEM((2, 2, width, width), bf16),
            pltpu.VMEM((2, 2, width, width), bf16),
            pltpu.VMEM((2, 2 * width, width), bf16),
            pltpu.VMEM((2, 2, width, columns), bf16),
            pltpu.VMEM((width + tail, columns), f32),
            pltpu.VMEM((width + tail, width), f32),
            pltpu.VMEM((tail, width), f32),
            pltpu.VMEM((2, width + tail, width), bf16),
            pltpu.VMEM((2, tail, width), bf16),
            pltpu.VMEM((width, width), f32),
            dma((2, count)),
            dma((2, NZ)),
            dma((2, NX)),
            dma((2 * chunks, count, 4)),
            dma((2 * chunks, count, 2)),
            dma((2, 2, 3)),
            dma((2, 2, 3)),
        ],
        compiler_params=pltpu.CompilerParams(
            collective_id=0, has_side_effects=True, vmem_limit_bytes=62 * 2**20
        ),
        name="two_panels",
    )(matrix.transpose(0, 2, 1, 3), *plan, lower_inv, upper_inv)
    return result.transpose(0, 2, 1, 3)


def local(matrix, pivots, lower_inv, upper_inv):
    row_blocks, row_part, col_blocks, col_part = matrix.shape
    width = lower_inv.shape[1]
    *plan, most = make_plan(pivots, width, row_blocks * row_part)
    return lax.cond(
        most[0, 0] <= 0,
        lambda m, p, a, b, q: two_panels(m, q, a, b),
        lambda m, p, a, b, q: general(m, p, a, b),
        matrix, pivots, lower_inv, upper_inv, plan,
    )


def solution(mesh):
    finer = Mesh(mesh.devices.reshape(NX, NZ, mesh.shape["pcol"]), ("x", "z", "pcol"))
    in_specs = (P(None, PROW, None, "pcol"), P(), P(), P())
    out_specs = P(None, PROW, None, "pcol")
    return jax.shard_map(local, mesh=finer, in_specs=in_specs, out_specs=out_specs, check_vma=False)
```

```python
import functools

import jax
import jax.numpy as jnp
from jax import lax
from jax.experimental import pallas as pl
from jax.experimental.pallas import tpu as pltpu
from jax.sharding import Mesh
from jax.sharding import PartitionSpec as P

PROW = ("x", "z")
MESH = pl.DeviceIdType.MESH
NX, NZ = 4, 8


def in_order(parts, dim):
    shape = list(parts.shape[1:])
    shape[dim] *= parts.shape[0]
    return jnp.moveaxis(parts, 0, dim).reshape(shape)


def to_next(x, axis):
    size = lax.axis_size(axis)
    return lax.ppermute(x, axis, [(n, (n + 1) % size) for n in range(size)])


def gathered_by_axis(x, axis, dim):
    size, me = lax.axis_size(axis), lax.axis_index(axis)

    def turn(n, state):
        parts, block = state
        block = to_next(block, axis)
        return lax.dynamic_update_index_in_dim(parts, block, (me - n + size) % size, 0), block

    parts = lax.dynamic_update_index_in_dim(jnp.zeros((size, *x.shape), x.dtype), x, me, 0)
    return in_order(lax.fori_loop(1, size, turn, (parts, x))[0], dim)


def sum_by_axis(x, axis, dim):
    size, me = lax.axis_size(axis), lax.axis_index(axis)
    width = x.shape[dim] // size

    def term(n):
        return lax.dynamic_slice_in_dim(x, (me - 1 - n + size) % size * width, width, dim)

    return lax.fori_loop(1, size, lambda n, total: to_next(total, axis) + term(n), term(0))


def broadcast(x, axis, root):
    mine = lax.axis_index(axis) == root
    return lax.fori_loop(1, lax.axis_size(axis), lambda n, y: jnp.where(mine, x, to_next(y, axis)), x)


def permutation(pivot_row, offset, panel_width, full_order):
    steps = jnp.arange(panel_width, dtype=jnp.int32)
    anchors = offset + steps
    earlier = steps[None, :] < steps[:, None]
    hits_anchor = (pivot_row[None, :] == anchors[:, None]) & earlier
    chain_from = jnp.max(jnp.where(hits_anchor, steps[None, :], -1), axis=1)
    pointer = jnp.where(chain_from >= 0, chain_from, steps)
    for level in range(max(1, panel_width.bit_length())):
        pointer = pointer[pointer]
    before_value = offset + pointer
    same_target = (pivot_row[None, :] == pivot_row[:, None]) & earlier
    last_before = jnp.max(jnp.where(same_target, steps[None, :], -1), axis=1)
    anchor_value = jnp.where(
        last_before >= 0, before_value[jnp.clip(last_before, 0, panel_width - 1)], pivot_row
    )
    later = steps[None, :] > steps[:, None]
    has_later = jnp.any((pivot_row[None, :] == pivot_row[:, None]) & later, axis=1)
    outside = jnp.logical_not(has_later) & (pivot_row >= offset + panel_width)
    spots = jnp.where(outside, pivot_row, full_order)
    ordering = jnp.arange(full_order, dtype=jnp.int32).at[spots].set(before_value, mode="drop")
    return lax.dynamic_update_slice_in_dim(ordering, anchor_value, offset, 0)


def product(left, right):
    return jnp.dot(left, right, precision=lax.Precision.HIGHEST, preferred_element_type=jnp.float32)


def general(matrix, pivots, lower_inv, upper_inv):
    row_blocks, row_part, col_blocks, col_part = matrix.shape
    panel_width = lower_inv.shape[1]
    panel_count = pivots.shape[0]
    full_order = row_blocks * panel_width
    row_devices = lax.axis_size(PROW)
    col_devices = lax.axis_size("pcol")
    row_index = lax.axis_index(PROW)
    col_index = lax.axis_index("pcol")
    local_rows = row_blocks * row_part
    local_cols = col_blocks * col_part
    share_width = local_cols // row_devices
    current = matrix.reshape(local_rows, local_cols)
    global_rows = (
        jnp.arange(row_blocks, dtype=jnp.int32)[:, None] * panel_width
        + row_index * row_part
        + jnp.arange(row_part, dtype=jnp.int32)[None, :]
    ).reshape(local_rows)
    col_span = col_devices * col_part
    global_cols = (
        jnp.arange(col_blocks, dtype=jnp.int32)[:, None] * col_span
        + col_index * col_part
        + jnp.arange(col_part, dtype=jnp.int32)[None, :]
    ).reshape(local_cols)

    def panel(panel_index, current):
        offset = panel_index * panel_width
        ending = offset + panel_width
        ordering = permutation(pivots[panel_index], offset, panel_width, full_order)
        source = ordering[global_rows]
        old_top = lax.dynamic_slice_in_dim(current, panel_index * row_part, row_part, 0)
        old_panel = gathered_by_axis(old_top, PROW, 0)
        wanted = ordering[offset + jnp.arange(panel_width, dtype=jnp.int32)]
        holder = wanted % panel_width // row_part
        local_spot = wanted // panel_width * row_part + wanted % row_part
        picked = jnp.where((holder == row_index)[:, None], current[local_spot], 0.0)
        column_share = sum_by_axis(picked, PROW, 1)
        share_cols = lax.dynamic_slice_in_dim(global_cols, row_index * share_width, share_width)
        solved = product(lower_inv[panel_index], column_share)
        merged = jnp.where((share_cols >= ending)[None, :], solved, column_share)
        top_rows = gathered_by_axis(merged, PROW, 1)
        in_panel = global_rows // panel_width == panel_index
        displaced = (source != global_rows) & jnp.logical_not(in_panel)
        from_old = old_panel[jnp.clip(source - offset, 0, panel_width - 1)]
        current = jnp.where(displaced[:, None], from_old, current)
        own_rows = lax.dynamic_slice_in_dim(top_rows, row_index * row_part, row_part, 0)
        current = lax.dynamic_update_slice_in_dim(current, own_rows, panel_index * row_part, 0)
        trailing_row = global_rows >= ending
        trailing_col = global_cols >= ending
        lower_full = product(current[:, :col_part], upper_inv[panel_index])
        lower_here = jnp.where(trailing_row[:, None], lower_full, 0.0)
        lower_rows = broadcast(lower_here, "pcol", panel_index)
        upper_part = jnp.where(trailing_col[None, :], top_rows, 0.0)
        current = current - product(lower_rows, upper_part)
        own_panel = col_index == panel_index
        new_cols = jnp.where(own_panel & trailing_row[:, None], lower_rows, current[:, :col_part])
        return jnp.concatenate([new_cols, current[:, col_part:]], axis=1)

    current = lax.fori_loop(0, panel_count, panel, current)
    return current.reshape(row_blocks, row_part, col_blocks, col_part)


CLASS_ROWS = 8
MOVED_ROWS = 16


def to_column(row):
    n = row.shape[1]
    eye = lax.broadcasted_iota(jnp.int32, (n, n), 0) == lax.broadcasted_iota(jnp.int32, (n, n), 1)
    return jnp.max(jnp.where(eye, row, -1.0), axis=1, keepdims=True)


def lookup(keys, values, wanted):
    return jnp.max(jnp.where(keys == wanted, values, -1.0), axis=0, keepdims=True)


def find(size, keys, values):
    found = jnp.full((size, 1), -1.0, jnp.float32)
    for key, value in zip(keys, values):
        number = lax.broadcasted_iota(jnp.int32, (size, key.shape[1]), 0).astype(jnp.float32)
        found = jnp.maximum(found, jnp.max(jnp.where(number == key, value, -1.0), axis=1, keepdims=True))
    return found.astype(jnp.int32)


def ranks_of(keys, columns, j, i):
    ranks, smaller = [], []
    for k in range(2):
        rank = jnp.sum(jnp.where((columns[k] == keys[k]) & (j < i), 1.0, 0.0), axis=0, keepdims=True)
        if k == 1:
            rank = rank + jnp.sum(jnp.where(columns[0] == keys[1], 1.0, 0.0), axis=0, keepdims=True)
        ranks.append(rank)
        smaller.append(
            sum(jnp.sum(jnp.where(column < keys[k], 1.0, 0.0), axis=0, keepdims=True) for column in columns)
        )
    return ranks, smaller


def plan_kernel(width, piv_row_ref, pick_ref, fold_ref, perm_ref, pack_ref, place_ref, most_ref):
    me = (lax.axis_index("x") * NZ + lax.axis_index("z")).astype(jnp.float32)
    my_x, my_z = lax.axis_index("x").astype(jnp.float32), lax.axis_index("z").astype(jnp.float32)
    part = width // (NX * NZ)
    j = lax.broadcasted_iota(jnp.int32, (width, width), 0).astype(jnp.float32)
    i = lax.broadcasted_iota(jnp.int32, (width, width), 1).astype(jnp.float32)
    i_row = i[:1]
    sources, spots, spot_cols, befores, before_cols = [], [], [], [], []
    for k in range(2):
        offset = float(k * width)
        p_row = piv_row_ref[k : k + 1, :].astype(jnp.float32)
        p_col = to_column(p_row)
        chain = jnp.max(jnp.where((p_col == offset + i) & (j < i), j, -1.0), axis=0, keepdims=True)
        start = jnp.where(chain >= 0.0, chain, i_row)

        def again(state):
            return state[1] > 0.0

        def jump(state):
            pointer = state[0]
            found = lookup(j[:, :1], to_column(pointer), pointer)
            return found, jnp.max(jnp.abs(found - pointer))

        pointer, _ = lax.while_loop(again, jump, (start, jnp.float32(1.0)))
        before = offset + pointer
        before_col = to_column(before)
        same = p_col == p_row
        last = jnp.max(jnp.where(same & (j < i), j, -1.0), axis=0, keepdims=True)
        later = jnp.max(jnp.where(same & (j > i), 1.0, 0.0), axis=0, keepdims=True)
        anchor = jnp.where(last >= 0.0, lookup(j[:, :1], before_col, last), p_row)
        spot = jnp.where((later == 0.0) & (p_row >= offset + width), p_row, -5.0)
        if k == 1:
            moved = lookup(spot_cols[0], before_cols[0], anchor)
            anchor = jnp.where(moved >= 0.0, moved, anchor)
        sources.append(anchor)
        spots.append(spot)
        spot_cols.append(jnp.max(jnp.where(i == j, spot, -5.0), axis=1, keepdims=True))
        befores.append(before)
        before_cols.append(before_col)

    def divided(value, by):
        return jnp.floor(value * (1.0 / by))

    def holder_and_place(source):
        block = divided(source, width)
        within = source - block * width
        holder = divided(within, part)
        return holder, block * part + within - holder * part

    holders, places = zip(*[holder_and_place(source) for source in sources])
    ranks, smaller = ranks_of(holders, [to_column(h) for h in holders], j, i)
    most = jnp.zeros((1, 1), jnp.float32)
    picks, folds, pick_keys, fold_keys = [], [], [], []
    for k in range(2):
        number = smaller[k] + ranks[k]
        at = divided(number, NZ)
        kind = number - at * NZ
        slot = at - divided(smaller[k] - kind + (NZ - 1.0), NZ)
        most = jnp.maximum(most, jnp.max(slot, axis=1, keepdims=True) - (CLASS_ROWS - 1.0))
        good = slot < CLASS_ROWS
        pick_keys.append(jnp.where((holders[k] == me) & good, kind * CLASS_ROWS + slot, -1.0))
        picks.append(places[k])
        fold_keys.append(jnp.where((kind == my_z) & good, at, -1.0))
        folds.append(holders[k] * CLASS_ROWS + slot)
        perm_ref[k * width : (k + 1) * width, :] = to_column(kind * (2 * width // NZ) + at).astype(jnp.int32)
    pick_ref[...] = find(pick_ref.shape[0], pick_keys, picks)
    fold_ref[...] = find(fold_ref.shape[0], fold_keys, folds)

    landed = lookup(spot_cols[0], before_cols[0], befores[1])
    origins = [befores[0], jnp.where(landed >= 0.0, landed, befores[1])]
    taken = lookup(spot_cols[1], spot_cols[1], spots[0])
    targets = [
        jnp.where((spots[0] >= 2.0 * width) & (taken < 0.0), spots[0], -1.0),
        jnp.where(spots[1] >= 2.0 * width, spots[1], -1.0),
    ]
    owners, rows = zip(*[holder_and_place(origin) for origin in origins])
    ends, spot_rows = zip(*[holder_and_place(jnp.maximum(target, 0.0)) for target in targets])
    owner_x = [divided(owner, NZ) for owner in owners]
    owner_z = [owner - x * NZ for owner, x in zip(owners, owner_x)]
    keys = [
        jnp.where(targets[k] >= 0.0, owner_z[k] * (NX * NZ) + ends[k], 2000.0 + i_row + 600.0 * k) for k in range(2)
    ]
    ranks, _ = ranks_of(keys, [to_column(key) for key in keys], j, i)
    pack_keys, packs, place_keys, place_values = [], [], [], []
    for k in range(2):
        most = jnp.maximum(most, jnp.max(ranks[k], axis=1, keepdims=True) - (MOVED_ROWS - 1.0))
        good = (targets[k] >= 0.0) & (ranks[k] < MOVED_ROWS)
        end_x = divided(ends[k], NZ)
        end_z = ends[k] - end_x * NZ
        pack_keys.append(
            jnp.where(good & (owner_z[k] == my_z) & (end_x == my_x), end_z * MOVED_ROWS + ranks[k], -1.0)
        )
        packs.append(owner_x[k] * (2 * part) + rows[k])
        place_keys.append(jnp.where(good & (ends[k] == me), spot_rows[k], -1.0))
        place_values.append(owner_z[k] * MOVED_ROWS + ranks[k])
    pack_ref[...] = find(pack_ref.shape[0], pack_keys, packs)
    place_ref[...] = find(place_ref.shape[0], place_keys, place_values)
    most_ref[...] = jnp.broadcast_to(most, most_ref.shape).astype(jnp.int32)


def make_plan(pivots, width, rows):
    vmem = pl.BlockSpec(memory_space=pltpu.VMEM)
    sizes = [NZ * CLASS_ROWS, 2 * width // NZ, 2 * width, NZ * MOVED_ROWS, rows]
    shapes = [(n, 1) for n in sizes] + [(8, 128)]
    return pl.pallas_call(
        functools.partial(plan_kernel, width),
        out_shape=[jax.ShapeDtypeStruct(shape, jnp.int32) for shape in shapes],
        in_specs=[vmem],
        out_specs=[vmem] * len(shapes),
        name="row_plan",
    )(pivots)


class Piece:
    def __init__(self, buf, low, high, first, x, z, col, send_sem, recv_sem):
        self.buf, self.low, self.high, self.first = buf, low, high, first
        self.x, self.z, self.col = x, z, col
        self.send_sem, self.recv_sem = send_sem, recv_sem
        self.started = []
        self.na, self.nb = (NX, NZ) if first == "x" else (NZ, NX)
        self.a, self.b = (x, z) if first == "x" else (z, x)

    def place(self, da, db):
        a, b = lax.rem(self.a + da + self.na, self.na), lax.rem(self.b + db + self.nb, self.nb)
        return (a, b) if self.first == "x" else (b, a)

    def copy(self, da, db, to, half, k):
        bx, bz = self.place(da, db)
        middle = (self.low + self.high) // 16 * 8
        low, high = ((self.low, self.high), (self.low, middle), (middle, self.high))[0 if half is None else half + 1]
        view = self.buf.at[bx, bz, low:high]
        return pltpu.make_async_remote_copy(
            src_ref=view,
            dst_ref=view,
            send_sem=self.send_sem.at[bx * NZ + bz, k],
            recv_sem=self.recv_sem.at[bx * NZ + bz, half or 0],
            device_id=self.place(*to) + (self.col,),
            device_id_type=MESH,
        )

    def send(self, da, db, to, half, k):
        copy = self.copy(da, db, to, half, k)
        copy.start()
        self.started.append(copy)

    def receive(self, da, db, half):
        self.copy(da, db, (0, 1), half, 0).wait_recv()

    def along_first(self, d):
        for s in (1, -1):
            if d + 1 <= self.na // 2:
                half = None if d + 1 < self.na // 2 else (1 - s) // 2
                self.send(-s * d, 0, (s, 0), half, (1 - s) // 2)

    def along_second(self, da, d):
        for s in (1, -1):
            if d + 1 <= self.nb // 2:
                half = None if d + 1 < self.nb // 2 else (1 - s) // 2
                self.send(da, -s * d, (0, s), half, (1 - s) // 2 + (2 if d == 0 else 0))

    def first_step(self, d):
        if d == 0:
            self.along_first(0)
            self.along_second(0, 0)
        elif d < self.na // 2:
            for s in (1, -1):
                self.receive(-s * d, 0, None)
            self.along_first(d)
            for s in (1, -1):
                self.along_second(-s * d, 0)
        else:
            self.receive(d, 0, 0)
            self.receive(d, 0, 1)
            self.along_second(d, 0)

    def second_step(self, da, d):
        if d < self.nb // 2:
            for s in (1, -1):
                self.receive(da, -s * d, None)
            self.along_second(da, d)
        else:
            self.receive(da, d, 0)
            self.receive(da, d, 1)

    def steps(self):
        work = [(d, functools.partial(self.first_step, d)) for d in range(self.na // 2 + 1)]
        for d in range(1, self.nb // 2 + 1):
            for ad in range(self.na // 2 + 1):
                for da in [0] if ad == 0 else [ad] if ad == self.na // 2 else [-ad, ad]:
                    work.append((ad + d + 0.5, functools.partial(self.second_step, da, d)))
        return work


class Several:
    def __init__(self, copies):
        self.copies = copies

    def start(self):
        for copy in self.copies:
            copy.start()

    def wait_send(self):
        for copy in self.copies:
            copy.wait_send()

    def wait_recv(self):
        for copy in self.copies:
            copy.wait_recv()


class Spread:
    def __init__(self, buf, root, x, z, col, sems):
        self.buf, self.root, self.x, self.z, self.col, self.sems = buf, root, x, z, col, sems
        y, self.core = col // 2, lax.rem(col, 2)
        self.mate = y * 2 + 1 - self.core
        self.up = lax.rem(y + 1, 4) * 2 + self.core
        self.down = lax.rem(y + 3, 4) * 2 + self.core
        self.away = lax.rem(y - root // 2 + 4, 4)

    def copy(self, half, device, k, pair):
        return Several([self.one(half, n, device, k, pair) for n in range(QUARTERS)])

    def one(self, half, n, device, k, pair):
        rows = self.buf.shape[0] // 16 * 8
        low = half * rows
        high = self.buf.shape[0] if half else rows
        cut = [low + (high - low) * m // (8 * QUARTERS) * 8 for m in range(QUARTERS)] + [high]
        view = self.buf.at[cut[n] : cut[n + 1]]
        return pltpu.make_async_remote_copy(
            src_ref=view,
            dst_ref=view,
            send_sem=self.sems.at[0, half, k, n],
            recv_sem=self.sems.at[1, half, pair, n],
            device_id=(self.x, self.z, device),
            device_id_type=MESH,
        )

    def sends(self, hops):
        up = [self.copy(half, self.up, 0, 0) for half in ((0, 1) if hops == 0 else (0,) if hops == 1 else ())]
        down = [self.copy(half, self.down, 1, 0) for half in ((1, 0) if hops == 0 else (1,) if hops == 3 else ())]
        return up, down

    def pass_on(self, half):
        self.copy(half, self.up, 0, 0).wait_recv()
        self.copy(half, self.mate, 2, 1).start()

    def at(self, hops, action):
        pl.when((self.core == self.root % 2) & (self.away == hops))(action)

    def begin(self):
        @pl.when(self.col == self.root)
        def _():
            up, down = self.sends(0)
            for n in range(2):
                up[n].start()
                down[n].start()
                self.copy(n, self.mate, 2, 1).start()

    def relay(self):
        for hops, half in ((1, 0), (3, 1)):

            def action(hops=hops, half=half):
                self.copy(half, self.up, 0, 0).wait_recv()
                for copy in sum(self.sends(hops), []):
                    copy.start()
                self.copy(half, self.mate, 2, 1).start()

            self.at(hops, action)

    def finish(self):
        self.at(1, functools.partial(self.pass_on, 1))
        self.at(3, functools.partial(self.pass_on, 0))

        def both():
            self.pass_on(0)
            self.pass_on(1)

        self.at(2, both)

        @pl.when(self.core != self.root % 2)
        def _():
            for half in range(2):
                self.copy(half, self.mate, 2, 1).wait_recv()

    def close(self):
        for hops in range(4):

            def action(hops=hops):
                for copy in sum(self.sends(hops), []):
                    copy.wait_send()
                for half in range(2):
                    self.copy(half, self.mate, 2, 1).wait_send()

            self.at(hops, action)


def dot(left, right):
    return jnp.dot(left, right, preferred_element_type=jnp.float32)


def split(value):
    high = value.astype(jnp.bfloat16)
    return high, (value - high.astype(jnp.float32)).astype(jnp.bfloat16)


def split_three(value):
    high, rest = split(value)
    low = value - high.astype(jnp.float32) - rest.astype(jnp.float32)
    return high, rest, low.astype(jnp.bfloat16)


def exact(hot, value):
    return sum(dot(hot, term) for term in split_three(value))


def times(left, right):
    return dot(left[0], right[0]) + (dot(left[0], right[1]) + dot(left[1], right[0]))


def hot_of(column, lanes):
    number = lax.broadcasted_iota(jnp.int32, (column.shape[0], lanes), 1)
    return jnp.where(column == number, 1.0, 0.0).astype(jnp.bfloat16)


def blocks(total, step, body):
    def one(n, carry):
        body(pl.multiple_of(n * step, step))
        return carry

    lax.fori_loop(0, total // step, one, 0)


ROWS, BODY, TAIL = 256, 288, 176
LAG, X_ROWS = 3.5, 48
QUARTERS = 1


def panels_kernel(
    m_ref, pick_ref, fold_ref, perm_ref, pack_ref, place_ref, linv_ref, uinv_ref, out_ref,
    old, pack_box, place_box, outbox, inbox, g, hot, linv, uinv, t, u, rest, lower0, lower1, low0, low1, solved,
    box_sem, move_sem, old_sem, ring_send, ring_recv, spread_sem0, spread_sem1,
):
    x, z, col = lax.axis_index("x"), lax.axis_index("z"), lax.axis_index("pcol")
    me = x * NZ + z
    count = NX * NZ
    width = linv_ref.shape[1]
    part = width // count
    top = 2 * part
    row_blocks, chunks = m_ref.shape[:2]
    rows, columns = row_blocks * part, chunks * width
    size = 2 * width // NZ
    tail = rows - top
    spread0 = Spread(lower0, 0, x, z, col, spread_sem0)
    spread1 = Spread(lower1, 1, x, z, col, spread_sem1)
    started = []

    others = [lax.rem(me + n, count) for n in range(1, count)]
    barrier = pltpu.get_barrier_semaphore()
    greeted = [(o // NZ, lax.rem(o, NZ), col) for o in others]
    greeted += [(x, z, spread0.mate), (x, z, spread0.up), (x, z, spread0.down)]
    for device in greeted:
        pl.semaphore_signal(barrier, inc=1, device_id=device, device_id_type=MESH)

    for c in range(chunks):
        old[pl.ds(x, 1), :, c * width : (c + 1) * width] = m_ref[0:2, c].reshape(1, top, width)
    pick_hot = hot_of(pick_ref[...], rows)
    tile = width // NX
    for c in range(chunks):
        picked = exact(pick_hot, m_ref[:, c].reshape(rows, width))
        for xs in range(NX):
            outbox[xs * NZ : (xs + 1) * NZ, :, c * tile : (c + 1) * tile] = picked[
                :, xs * tile : (xs + 1) * tile
            ].reshape(NZ, -1, tile)
    inbox[pl.ds(me, 1)] = outbox[pl.ds(me, 1)]
    pl.semaphore_wait(barrier, len(greeted))

    def send(src, dst, send_sem, recv_sem, device):
        copy = pltpu.make_async_remote_copy(
            src_ref=src, dst_ref=dst, send_sem=send_sem, recv_sem=recv_sem, device_id=device, device_id_type=MESH
        )
        copy.start()
        started.append(copy)

    for o in others:
        send(outbox.at[o], inbox.at[me], box_sem.at[0, o], box_sem.at[1, me], (o // NZ, lax.rem(o, NZ), col))
    for d in range(1, NX):
        to = lax.rem(x + d, NX)
        send(old.at[x], old.at[x], old_sem.at[0, to], old_sem.at[1, x], (to, z, col))

    def arrive(view, sem):
        pltpu.make_async_remote_copy(
            src_ref=view, dst_ref=view, send_sem=sem, recv_sem=sem, device_id=(lax.rem(x + 1, NX), z, col),
            device_id_type=MESH,
        ).wait_recv()

    for d in range(1, NX):
        xs = lax.rem(x + d, NX)
        arrive(old.at[xs], old_sem.at[1, xs])
    pack_hot = hot_of(pack_ref[...], NX * top)
    for c in range(0, columns, width):
        packed = exact(pack_hot, old[:, :, c : c + width].reshape(NX * top, width))
        pack_box[:, :, c : c + width] = packed.reshape(NZ, -1, width)
    place_box[pl.ds(z, 1)] = pack_box[pl.ds(z, 1)]
    for o in others:
        arrive(inbox.at[o], box_sem.at[1, o])
    fold_hot = hot_of(fold_ref[...], count * CLASS_ROWS)
    for c in range(chunks):
        mine = exact(fold_hot, inbox[:, :, c * tile : (c + 1) * tile].reshape(count * CLASS_ROWS, tile))
        g[c, pl.ds(x, 1), pl.ds(z, 1)] = mine[None, None]

    pieces, work = [], []
    for c in range(chunks):
        for number, (first, low, high) in enumerate((("x", 0, X_ROWS), ("z", X_ROWS, size))):
            s = 2 * c + number
            pieces.append(Piece(g.at[c], low, high, first, x, z, col, ring_send.at[s], ring_recv.at[s]))
    flow = []
    for number, piece in enumerate(pieces):
        for place, (when, step) in enumerate(piece.steps()):
            flow.append((when + LAG * (number // 2) if when else -1.0, number, place, number // 2, step))
    flow.sort(key=lambda entry: entry[:3])
    for _ in range(2):
        flow.pop(0)[4]()
    for d in range(1, NZ):
        to = lax.rem(z + d, NZ)
        send(pack_box.at[to], place_box.at[z], move_sem.at[0, to], move_sem.at[1, z], (x, to, col))
    for _ in range(2 * chunks - 2):
        flow.pop(0)[4]()

    def prepare():
        for k in range(2):
            linv[k, 0], linv[k, 1] = split(linv_ref[k])
            uinv[k, 0], uinv[k, 1] = split(uinv_ref[k])

        def perm(r):
            hot[pl.ds(r, 128)] = hot_of(perm_ref[pl.ds(r, 128), :], 2 * width)

        blocks(2 * width, 128, perm)

    def place_moved():
        for d in range(1, NZ):
            zs = lax.rem(z + d, NZ)
            arrive(place_box.at[zs], move_sem.at[1, zs])
        column = place_ref[...]
        place_hot = hot_of(column[top:], NZ * MOVED_ROWS)
        for c in range(chunks):
            cols = slice(c * width, (c + 1) * width)
            moved = exact(place_hot, place_box[:, :, cols].reshape(NZ * MOVED_ROWS, width))
            rest[width:, cols] = jnp.where(column[top:] >= 0, moved, m_ref[2:, c].reshape(tail, width))

    def permute(c):
        whole = jnp.concatenate([g[c, n].reshape(2 * width, tile) for n in range(NX)], axis=1)
        high, middle = split(whole)

        def body(r):
            left = hot[pl.ds(r, ROWS)]
            first, second = dot(left, high), dot(left, middle)
            t[0, pl.ds(r, ROWS)] = first.astype(jnp.bfloat16)
            t[1, pl.ds(r, ROWS)] = second.astype(jnp.bfloat16)

            @pl.when(r >= width)
            def _():
                rest[pl.ds(r - width, ROWS), c * width : (c + 1) * width] = first + second

        blocks(2 * width, ROWS, body)

    def own(ref):
        return ref[pl.ds(pl.multiple_of(me * part, part), part)]

    def solve0(c):
        right = t[0, 0:width], t[1, 0:width]
        cols = slice(c * width, (c + 1) * width)

        def body(r):
            value = times((linv[0, 0, pl.ds(r, ROWS)], linv[0, 1, pl.ds(r, ROWS)]), right)
            u[0, 0, pl.ds(r, ROWS), cols], u[0, 1, pl.ds(r, ROWS), cols] = split(value)
            solved[pl.ds(r, ROWS)] = value

        blocks(width, ROWS, body)
        out_ref[0, c] = own(solved)
        if c == 0:

            @pl.when(col == 0)
            def _():
                out_ref[0, c] = own(t.at[0]).astype(jnp.float32) + own(t.at[1]).astype(jnp.float32)
                u[0, :, :, cols] = jnp.zeros((2, width, width), jnp.bfloat16)

    def find_lower0():
        @pl.when(col == 0)
        def _():
            right = uinv[0, 0], uinv[0, 1]

            def body(r):
                lower0[pl.ds(r, BODY)] = times(split(rest[pl.ds(r, BODY), 0:width]), right)

            blocks(width + tail, BODY, body)

    def split_lower(source, target):
        def body(r):
            target[0, pl.ds(r, 32)], target[1, pl.ds(r, 32)] = split(source[pl.ds(r, 32)])

        blocks(source.shape[0], 32, body)

    def reduce0(c):
        cols = slice(c * width, (c + 1) * width)
        right = u[0, 0, :, cols], u[0, 1, :, cols]

        def body(r):
            rest[pl.ds(r, BODY), cols] -= times((low0[0, pl.ds(r, BODY)], low0[1, pl.ds(r, BODY)]), right)

        blocks(width + tail, BODY, body)

    def find_lower1():
        right = uinv[1, 0], uinv[1, 1]

        def body(r):
            lower1[pl.ds(r, TAIL)] = times(split(rest[pl.ds(width + r, TAIL), 0:width]), right)

        blocks(tail, TAIL, body)

    def solve1(c):
        cols = slice(c * width, (c + 1) * width)
        right = split(rest[0:width, cols])

        def body(r):
            value = times((linv[1, 0, pl.ds(r, ROWS)], linv[1, 1, pl.ds(r, ROWS)]), right)
            u[1, 0, pl.ds(r, ROWS), cols], u[1, 1, pl.ds(r, ROWS), cols] = split(value)
            solved[pl.ds(r, ROWS)] = value

        blocks(width, ROWS, body)
        out_ref[1, c] = own(solved)
        if c == 0:

            @pl.when(col <= 1)
            def _():
                mine = jnp.where(col == 0, own(lower0), rest[pl.ds(pl.multiple_of(me * part, part), part), cols])
                out_ref[1, c] = mine
                u[1, :, :, cols] = jnp.zeros((2, width, width), jnp.bfloat16)

    def reduce1(c):
        cols = slice(c * width, (c + 1) * width)
        right = u[1, 0, :, cols], u[1, 1, :, cols]

        def body(r):
            value = rest[pl.ds(width + r, TAIL), cols] - times((low1[0, pl.ds(r, TAIL)], low1[1, pl.ds(r, TAIL)]), right)
            if c == 0:
                value = jnp.where(col == 0, lower0[pl.ds(width + r, TAIL)], jnp.where(col == 1, lower1[pl.ds(r, TAIL)], value))
            out_ref[pl.ds(2 + r // part, TAIL // part), c] = value.reshape(TAIL // part, part, width)

        blocks(tail, TAIL, body)

    def left_of(stage):
        return max([n + 1 for n, entry in enumerate(flow) if entry[3] <= stage], default=0)

    def mix(stage, actions):
        total = left_of(stage)
        done = 0
        for number, action in enumerate(actions):
            until = (number + 1) * total // (len(actions) + 1)
            for _ in range(until - done):
                flow.pop(0)[4]()
            done = until
            action()
        for _ in range(total - done):
            flow.pop(0)[4]()

    P_ = functools.partial
    def lower_arrives():
        spread0.finish()
        split_lower(lower0, low0)
        reduce0(0)

    def early():
        @pl.when(col == 1)
        def _():
            lower_arrives()
            find_lower1()

        spread1.begin()

    def late():
        pl.when(col != 1)(lower_arrives)

    mix(0, [prepare])
    place_moved()
    permute(0)
    find_lower0()
    spread0.begin()
    solve0(0)
    early()
    mix(1, [spread0.relay])
    mix(2, [P_(permute, 1), P_(solve0, 1), late, spread1.relay, P_(reduce0, 1), P_(solve1, 0)])
    permute(2)
    solve0(2)
    reduce0(2)
    solve1(1)
    solve1(2)
    spread1.finish()
    split_lower(lower1, low1)
    for c in range(chunks):
        reduce1(c)
    for copy in started:
        copy.wait_send()
    for piece in pieces:
        for copy in piece.started:
            copy.wait_send()
    spread0.close()
    spread1.close()


def two_panels(matrix, plan, lower_inv, upper_inv):
    row_blocks, part, chunks, width = matrix.shape
    rows, columns = row_blocks * part, chunks * width
    count, top, size, tile = NX * NZ, 2 * width // (NX * NZ), 2 * width // NZ, width // NX
    tail = rows - top
    vmem = pl.BlockSpec(memory_space=pltpu.VMEM)
    f32, bf16, dma = jnp.float32, jnp.bfloat16, pltpu.SemaphoreType.DMA
    result = pl.pallas_call(
        panels_kernel,
        out_shape=jax.ShapeDtypeStruct((row_blocks, chunks, part, width), f32),
        in_specs=[vmem] * 8,
        out_specs=vmem,
        scratch_shapes=[
            pltpu.VMEM((NX, top, columns), f32),
            pltpu.VMEM((NZ, MOVED_ROWS, columns), f32),
            pltpu.VMEM((NZ, MOVED_ROWS, columns), f32),
            pltpu.VMEM((count, CLASS_ROWS, columns // NX), f32),
            pltpu.VMEM((count, CLASS_ROWS, columns // NX), f32),
            pltpu.VMEM((chunks, NX, NZ, size, tile), f32),
            pltpu.VMEM((2 * width, 2 * width), bf16),
            pltpu.VMEM((2, 2, width, width), bf16),
            pltpu.VMEM((2, 2, width, width), bf16),
            pltpu.VMEM((2, 2 * width, width), bf16),
            pltpu.VMEM((2, 2, width, columns), bf16),
            pltpu.VMEM((width + tail, columns), f32),
            pltpu.VMEM((width + tail, width), f32),
            pltpu.VMEM((tail, width), f32),
            pltpu.VMEM((2, width + tail, width), bf16),
            pltpu.VMEM((2, tail, width), bf16),
            pltpu.VMEM((width, width), f32),
            dma((2, count)),
            dma((2, NZ)),
            dma((2, NX)),
            dma((2 * chunks, count, 4)),
            dma((2 * chunks, count, 2)),
            dma((2, 2, 3, QUARTERS)),
            dma((2, 2, 3, QUARTERS)),
        ],
        compiler_params=pltpu.CompilerParams(
            collective_id=0, has_side_effects=True, vmem_limit_bytes=62 * 2**20
        ),
        name="two_panels",
    )(matrix.transpose(0, 2, 1, 3), *plan, lower_inv, upper_inv)
    return result.transpose(0, 2, 1, 3)


def local(matrix, pivots, lower_inv, upper_inv):
    row_blocks, row_part, col_blocks, col_part = matrix.shape
    width = lower_inv.shape[1]
    *plan, most = make_plan(pivots, width, row_blocks * row_part)
    return lax.cond(
        most[0, 0] <= 0,
        lambda m, p, a, b, q: two_panels(m, q, a, b),
        lambda m, p, a, b, q: general(m, p, a, b),
        matrix, pivots, lower_inv, upper_inv, plan,
    )


def solution(mesh):
    finer = Mesh(mesh.devices.reshape(NX, NZ, mesh.shape["pcol"]), ("x", "z", "pcol"))
    in_specs = (P(None, PROW, None, "pcol"), P(), P(), P())
    out_specs = P(None, PROW, None, "pcol")
    return jax.shard_map(local, mesh=finer, in_specs=in_specs, out_specs=out_specs, check_vma=False)
```

```python
import functools

import jax
import jax.numpy as jnp
from jax import lax
from jax.experimental import pallas as pl
from jax.experimental.pallas import tpu as pltpu
from jax.sharding import Mesh
from jax.sharding import PartitionSpec as P

PROW = ("x", "z")
MESH = pl.DeviceIdType.MESH
NX, NZ = 4, 8


def in_order(parts, dim):
    shape = list(parts.shape[1:])
    shape[dim] *= parts.shape[0]
    return jnp.moveaxis(parts, 0, dim).reshape(shape)


def to_next(x, axis):
    size = lax.axis_size(axis)
    return lax.ppermute(x, axis, [(n, (n + 1) % size) for n in range(size)])


def gathered_by_axis(x, axis, dim):
    size, me = lax.axis_size(axis), lax.axis_index(axis)

    def turn(n, state):
        parts, block = state
        block = to_next(block, axis)
        return lax.dynamic_update_index_in_dim(parts, block, (me - n + size) % size, 0), block

    parts = lax.dynamic_update_index_in_dim(jnp.zeros((size, *x.shape), x.dtype), x, me, 0)
    return in_order(lax.fori_loop(1, size, turn, (parts, x))[0], dim)


def sum_by_axis(x, axis, dim):
    size, me = lax.axis_size(axis), lax.axis_index(axis)
    width = x.shape[dim] // size

    def term(n):
        return lax.dynamic_slice_in_dim(x, (me - 1 - n + size) % size * width, width, dim)

    return lax.fori_loop(1, size, lambda n, total: to_next(total, axis) + term(n), term(0))


def broadcast(x, axis, root):
    mine = lax.axis_index(axis) == root
    return lax.fori_loop(1, lax.axis_size(axis), lambda n, y: jnp.where(mine, x, to_next(y, axis)), x)


def permutation(pivot_row, offset, panel_width, full_order):
    steps = jnp.arange(panel_width, dtype=jnp.int32)
    anchors = offset + steps
    earlier = steps[None, :] < steps[:, None]
    hits_anchor = (pivot_row[None, :] == anchors[:, None]) & earlier
    chain_from = jnp.max(jnp.where(hits_anchor, steps[None, :], -1), axis=1)
    pointer = jnp.where(chain_from >= 0, chain_from, steps)
    for level in range(max(1, panel_width.bit_length())):
        pointer = pointer[pointer]
    before_value = offset + pointer
    same_target = (pivot_row[None, :] == pivot_row[:, None]) & earlier
    last_before = jnp.max(jnp.where(same_target, steps[None, :], -1), axis=1)
    anchor_value = jnp.where(
        last_before >= 0, before_value[jnp.clip(last_before, 0, panel_width - 1)], pivot_row
    )
    later = steps[None, :] > steps[:, None]
    has_later = jnp.any((pivot_row[None, :] == pivot_row[:, None]) & later, axis=1)
    outside = jnp.logical_not(has_later) & (pivot_row >= offset + panel_width)
    spots = jnp.where(outside, pivot_row, full_order)
    ordering = jnp.arange(full_order, dtype=jnp.int32).at[spots].set(before_value, mode="drop")
    return lax.dynamic_update_slice_in_dim(ordering, anchor_value, offset, 0)


def product(left, right):
    return jnp.dot(left, right, precision=lax.Precision.HIGHEST, preferred_element_type=jnp.float32)


def general(matrix, pivots, lower_inv, upper_inv):
    row_blocks, row_part, col_blocks, col_part = matrix.shape
    panel_width = lower_inv.shape[1]
    panel_count = pivots.shape[0]
    full_order = row_blocks * panel_width
    row_devices = lax.axis_size(PROW)
    col_devices = lax.axis_size("pcol")
    row_index = lax.axis_index(PROW)
    col_index = lax.axis_index("pcol")
    local_rows = row_blocks * row_part
    local_cols = col_blocks * col_part
    share_width = local_cols // row_devices
    current = matrix.reshape(local_rows, local_cols)
    global_rows = (
        jnp.arange(row_blocks, dtype=jnp.int32)[:, None] * panel_width
        + row_index * row_part
        + jnp.arange(row_part, dtype=jnp.int32)[None, :]
    ).reshape(local_rows)
    col_span = col_devices * col_part
    global_cols = (
        jnp.arange(col_blocks, dtype=jnp.int32)[:, None] * col_span
        + col_index * col_part
        + jnp.arange(col_part, dtype=jnp.int32)[None, :]
    ).reshape(local_cols)

    def panel(panel_index, current):
        offset = panel_index * panel_width
        ending = offset + panel_width
        ordering = permutation(pivots[panel_index], offset, panel_width, full_order)
        source = ordering[global_rows]
        old_top = lax.dynamic_slice_in_dim(current, panel_index * row_part, row_part, 0)
        old_panel = gathered_by_axis(old_top, PROW, 0)
        wanted = ordering[offset + jnp.arange(panel_width, dtype=jnp.int32)]
        holder = wanted % panel_width // row_part
        local_spot = wanted // panel_width * row_part + wanted % row_part
        picked = jnp.where((holder == row_index)[:, None], current[local_spot], 0.0)
        column_share = sum_by_axis(picked, PROW, 1)
        share_cols = lax.dynamic_slice_in_dim(global_cols, row_index * share_width, share_width)
        solved = product(lower_inv[panel_index], column_share)
        merged = jnp.where((share_cols >= ending)[None, :], solved, column_share)
        top_rows = gathered_by_axis(merged, PROW, 1)
        in_panel = global_rows // panel_width == panel_index
        displaced = (source != global_rows) & jnp.logical_not(in_panel)
        from_old = old_panel[jnp.clip(source - offset, 0, panel_width - 1)]
        current = jnp.where(displaced[:, None], from_old, current)
        own_rows = lax.dynamic_slice_in_dim(top_rows, row_index * row_part, row_part, 0)
        current = lax.dynamic_update_slice_in_dim(current, own_rows, panel_index * row_part, 0)
        trailing_row = global_rows >= ending
        trailing_col = global_cols >= ending
        lower_full = product(current[:, :col_part], upper_inv[panel_index])
        lower_here = jnp.where(trailing_row[:, None], lower_full, 0.0)
        lower_rows = broadcast(lower_here, "pcol", panel_index)
        upper_part = jnp.where(trailing_col[None, :], top_rows, 0.0)
        current = current - product(lower_rows, upper_part)
        own_panel = col_index == panel_index
        new_cols = jnp.where(own_panel & trailing_row[:, None], lower_rows, current[:, :col_part])
        return jnp.concatenate([new_cols, current[:, col_part:]], axis=1)

    current = lax.fori_loop(0, panel_count, panel, current)
    return current.reshape(row_blocks, row_part, col_blocks, col_part)


CLASS_ROWS = 8
MOVED_ROWS = 16


def to_column(row):
    n = row.shape[1]
    eye = lax.broadcasted_iota(jnp.int32, (n, n), 0) == lax.broadcasted_iota(jnp.int32, (n, n), 1)
    return jnp.max(jnp.where(eye, row, -1.0), axis=1, keepdims=True)


def lookup(keys, values, wanted):
    return jnp.max(jnp.where(keys == wanted, values, -1.0), axis=0, keepdims=True)


def find(size, keys, values):
    found = jnp.full((size, 1), -1.0, jnp.float32)
    for key, value in zip(keys, values):
        number = lax.broadcasted_iota(jnp.int32, (size, key.shape[1]), 0).astype(jnp.float32)
        found = jnp.maximum(found, jnp.max(jnp.where(number == key, value, -1.0), axis=1, keepdims=True))
    return found.astype(jnp.int32)


def ranks_of(keys, columns, j, i):
    ranks, smaller = [], []
    for k in range(2):
        rank = jnp.sum(jnp.where((columns[k] == keys[k]) & (j < i), 1.0, 0.0), axis=0, keepdims=True)
        if k == 1:
            rank = rank + jnp.sum(jnp.where(columns[0] == keys[1], 1.0, 0.0), axis=0, keepdims=True)
        ranks.append(rank)
        smaller.append(
            sum(jnp.sum(jnp.where(column < keys[k], 1.0, 0.0), axis=0, keepdims=True) for column in columns)
        )
    return ranks, smaller


def plan_kernel(width, piv_row_ref, pick_ref, fold_ref, perm_ref, pack_ref, place_ref, most_ref):
    me = (lax.axis_index("x") * NZ + lax.axis_index("z")).astype(jnp.float32)
    my_x, my_z = lax.axis_index("x").astype(jnp.float32), lax.axis_index("z").astype(jnp.float32)
    part = width // (NX * NZ)
    j = lax.broadcasted_iota(jnp.int32, (width, width), 0).astype(jnp.float32)
    i = lax.broadcasted_iota(jnp.int32, (width, width), 1).astype(jnp.float32)
    i_row = i[:1]
    sources, spots, spot_cols, befores, before_cols = [], [], [], [], []
    for k in range(2):
        offset = float(k * width)
        p_row = piv_row_ref[k : k + 1, :].astype(jnp.float32)
        p_col = to_column(p_row)
        chain = jnp.max(jnp.where((p_col == offset + i) & (j < i), j, -1.0), axis=0, keepdims=True)
        start = jnp.where(chain >= 0.0, chain, i_row)

        def again(state):
            return state[1] > 0.0

        def jump(state):
            pointer = state[0]
            found = lookup(j[:, :1], to_column(pointer), pointer)
            return found, jnp.max(jnp.abs(found - pointer))

        pointer, _ = lax.while_loop(again, jump, (start, jnp.float32(1.0)))
        before = offset + pointer
        before_col = to_column(before)
        same = p_col == p_row
        last = jnp.max(jnp.where(same & (j < i), j, -1.0), axis=0, keepdims=True)
        later = jnp.max(jnp.where(same & (j > i), 1.0, 0.0), axis=0, keepdims=True)
        anchor = jnp.where(last >= 0.0, lookup(j[:, :1], before_col, last), p_row)
        spot = jnp.where((later == 0.0) & (p_row >= offset + width), p_row, -5.0)
        if k == 1:
            moved = lookup(spot_cols[0], before_cols[0], anchor)
            anchor = jnp.where(moved >= 0.0, moved, anchor)
        sources.append(anchor)
        spots.append(spot)
        spot_cols.append(jnp.max(jnp.where(i == j, spot, -5.0), axis=1, keepdims=True))
        befores.append(before)
        before_cols.append(before_col)

    def divided(value, by):
        return jnp.floor(value * (1.0 / by))

    def holder_and_place(source):
        block = divided(source, width)
        within = source - block * width
        holder = divided(within, part)
        return holder, block * part + within - holder * part

    holders, places = zip(*[holder_and_place(source) for source in sources])
    ranks, smaller = ranks_of(holders, [to_column(h) for h in holders], j, i)
    most = jnp.zeros((1, 1), jnp.float32)
    picks, folds, pick_keys, fold_keys = [], [], [], []
    for k in range(2):
        number = smaller[k] + ranks[k]
        at = divided(number, NZ)
        kind = number - at * NZ
        slot = at - divided(smaller[k] - kind + (NZ - 1.0), NZ)
        most = jnp.maximum(most, jnp.max(slot, axis=1, keepdims=True) - (CLASS_ROWS - 1.0))
        good = slot < CLASS_ROWS
        pick_keys.append(jnp.where((holders[k] == me) & good, kind * CLASS_ROWS + slot, -1.0))
        picks.append(places[k])
        fold_keys.append(jnp.where((kind == my_z) & good, at, -1.0))
        folds.append(holders[k] * CLASS_ROWS + slot)
        perm_ref[k * width : (k + 1) * width, :] = to_column(kind * (2 * width // NZ) + at).astype(jnp.int32)
    pick_ref[...] = find(pick_ref.shape[0], pick_keys, picks)
    fold_ref[...] = find(fold_ref.shape[0], fold_keys, folds)

    landed = lookup(spot_cols[0], before_cols[0], befores[1])
    origins = [befores[0], jnp.where(landed >= 0.0, landed, befores[1])]
    taken = lookup(spot_cols[1], spot_cols[1], spots[0])
    targets = [
        jnp.where((spots[0] >= 2.0 * width) & (taken < 0.0), spots[0], -1.0),
        jnp.where(spots[1] >= 2.0 * width, spots[1], -1.0),
    ]
    owners, rows = zip(*[holder_and_place(origin) for origin in origins])
    ends, spot_rows = zip(*[holder_and_place(jnp.maximum(target, 0.0)) for target in targets])
    owner_x = [divided(owner, NZ) for owner in owners]
    owner_z = [owner - x * NZ for owner, x in zip(owners, owner_x)]
    keys = [
        jnp.where(targets[k] >= 0.0, owner_z[k] * (NX * NZ) + ends[k], 2000.0 + i_row + 600.0 * k) for k in range(2)
    ]
    ranks, _ = ranks_of(keys, [to_column(key) for key in keys], j, i)
    pack_keys, packs, place_keys, place_values = [], [], [], []
    for k in range(2):
        most = jnp.maximum(most, jnp.max(ranks[k], axis=1, keepdims=True) - (MOVED_ROWS - 1.0))
        good = (targets[k] >= 0.0) & (ranks[k] < MOVED_ROWS)
        end_x = divided(ends[k], NZ)
        end_z = ends[k] - end_x * NZ
        pack_keys.append(
            jnp.where(good & (owner_z[k] == my_z) & (end_x == my_x), end_z * MOVED_ROWS + ranks[k], -1.0)
        )
        packs.append(owner_x[k] * (2 * part) + rows[k])
        place_keys.append(jnp.where(good & (ends[k] == me), spot_rows[k], -1.0))
        place_values.append(owner_z[k] * MOVED_ROWS + ranks[k])
    pack_ref[...] = find(pack_ref.shape[0], pack_keys, packs)
    place_ref[...] = find(place_ref.shape[0], place_keys, place_values)
    most_ref[...] = jnp.broadcast_to(most, most_ref.shape).astype(jnp.int32)


def make_plan(pivots, width, rows):
    vmem = pl.BlockSpec(memory_space=pltpu.VMEM)
    sizes = [NZ * CLASS_ROWS, 2 * width // NZ, 2 * width, NZ * MOVED_ROWS, rows]
    shapes = [(n, 1) for n in sizes] + [(1, 1)]
    return pl.pallas_call(
        functools.partial(plan_kernel, width),
        out_shape=[jax.ShapeDtypeStruct(shape, jnp.int32) for shape in shapes],
        in_specs=[vmem],
        out_specs=[vmem] * len(shapes),
        name="row_plan",
    )(pivots)


class Piece:
    def __init__(self, buf, low, high, first, x, z, col, send_sem, recv_sem):
        self.buf, self.low, self.high, self.first = buf, low, high, first
        self.x, self.z, self.col = x, z, col
        self.send_sem, self.recv_sem = send_sem, recv_sem
        self.started = []
        self.na, self.nb = (NX, NZ) if first == "x" else (NZ, NX)
        self.a, self.b = (x, z) if first == "x" else (z, x)

    def place(self, da, db):
        a, b = lax.rem(self.a + da + self.na, self.na), lax.rem(self.b + db + self.nb, self.nb)
        return (a, b) if self.first == "x" else (b, a)

    def copy(self, da, db, to, half, k):
        bx, bz = self.place(da, db)
        middle = (self.low + self.high) // 16 * 8
        low, high = ((self.low, self.high), (self.low, middle), (middle, self.high))[0 if half is None else half + 1]
        view = self.buf.at[bx, bz, low:high]
        return pltpu.make_async_remote_copy(
            src_ref=view,
            dst_ref=view,
            send_sem=self.send_sem.at[bx * NZ + bz, k],
            recv_sem=self.recv_sem.at[bx * NZ + bz, half or 0],
            device_id=self.place(*to) + (self.col,),
            device_id_type=MESH,
        )

    def send(self, da, db, to, half, k):
        copy = self.copy(da, db, to, half, k)
        copy.start()
        self.started.append(copy)

    def receive(self, da, db, half):
        self.copy(da, db, (0, 1), half, 0).wait_recv()

    def along_first(self, d):
        for s in (1, -1):
            if d + 1 <= self.na // 2:
                half = None if d + 1 < self.na // 2 else (1 - s) // 2
                self.send(-s * d, 0, (s, 0), half, (1 - s) // 2)

    def along_second(self, da, d):
        for s in (1, -1):
            if d + 1 <= self.nb // 2:
                half = None if d + 1 < self.nb // 2 else (1 - s) // 2
                self.send(da, -s * d, (0, s), half, (1 - s) // 2 + (2 if d == 0 else 0))

    def first_step(self, d):
        if d == 0:
            self.along_first(0)
            self.along_second(0, 0)
        elif d < self.na // 2:
            for s in (1, -1):
                self.receive(-s * d, 0, None)
            self.along_first(d)
            for s in (1, -1):
                self.along_second(-s * d, 0)
        else:
            self.receive(d, 0, 0)
            self.receive(d, 0, 1)
            self.along_second(d, 0)

    def second_step(self, da, d):
        if d < self.nb // 2:
            for s in (1, -1):
                self.receive(da, -s * d, None)
            self.along_second(da, d)
        else:
            self.receive(da, d, 0)
            self.receive(da, d, 1)

    def steps(self):
        work = [(d, functools.partial(self.first_step, d)) for d in range(self.na // 2 + 1)]
        for d in range(1, self.nb // 2 + 1):
            for ad in range(self.na // 2 + 1):
                for da in [0] if ad == 0 else [ad] if ad == self.na // 2 else [-ad, ad]:
                    work.append((ad + d + 0.5, functools.partial(self.second_step, da, d)))
        return work


class Several:
    def __init__(self, copies):
        self.copies = copies

    def start(self):
        for copy in self.copies:
            copy.start()

    def wait_send(self):
        for copy in self.copies:
            copy.wait_send()

    def wait_recv(self):
        for copy in self.copies:
            copy.wait_recv()


class Spread:
    def __init__(self, buf, root, x, z, col, sems):
        self.buf, self.root, self.x, self.z, self.col, self.sems = buf, root, x, z, col, sems
        y, self.core = col // 2, lax.rem(col, 2)
        self.mate = y * 2 + 1 - self.core
        self.up = lax.rem(y + 1, 4) * 2 + self.core
        self.down = lax.rem(y + 3, 4) * 2 + self.core
        self.away = lax.rem(y - root // 2 + 4, 4)

    def copy(self, half, device, k, pair):
        return Several([self.one(half, n, device, k, pair) for n in range(QUARTERS)])

    def one(self, half, n, device, k, pair):
        rows = self.buf.shape[0] // 16 * 8
        low = half * rows
        high = self.buf.shape[0] if half else rows
        cut = [low + (high - low) * m // (8 * QUARTERS) * 8 for m in range(QUARTERS)] + [high]
        view = self.buf.at[cut[n] : cut[n + 1]]
        return pltpu.make_async_remote_copy(
            src_ref=view,
            dst_ref=view,
            send_sem=self.sems.at[0, half, k, n],
            recv_sem=self.sems.at[1, half, pair, n],
            device_id=(self.x, self.z, device),
            device_id_type=MESH,
        )

    def sends(self, hops):
        up = [self.copy(half, self.up, 0, 0) for half in ((0, 1) if hops == 0 else (0,) if hops == 1 else ())]
        down = [self.copy(half, self.down, 1, 0) for half in ((1, 0) if hops == 0 else (1,) if hops == 3 else ())]
        return up, down

    def pass_on(self, half):
        self.copy(half, self.up, 0, 0).wait_recv()
        self.copy(half, self.mate, 2, 1).start()

    def at(self, hops, action):
        pl.when((self.core == self.root % 2) & (self.away == hops))(action)

    def begin(self):
        @pl.when(self.col == self.root)
        def _():
            up, down = self.sends(0)
            for n in range(2):
                up[n].start()
                down[n].start()
                self.copy(n, self.mate, 2, 1).start()

    def relay(self):
        for hops, half in ((1, 0), (3, 1)):

            def action(hops=hops, half=half):
                self.copy(half, self.up, 0, 0).wait_recv()
                for copy in sum(self.sends(hops), []):
                    copy.start()
                self.copy(half, self.mate, 2, 1).start()

            self.at(hops, action)

    def finish(self):
        self.at(1, functools.partial(self.pass_on, 1))
        self.at(3, functools.partial(self.pass_on, 0))

        def both():
            self.pass_on(0)
            self.pass_on(1)

        self.at(2, both)

        @pl.when(self.core != self.root % 2)
        def _():
            for half in range(2):
                self.copy(half, self.mate, 2, 1).wait_recv()

    def close(self):
        for hops in range(4):

            def action(hops=hops):
                for copy in sum(self.sends(hops), []):
                    copy.wait_send()
                for half in range(2):
                    self.copy(half, self.mate, 2, 1).wait_send()

            self.at(hops, action)


def dot(left, right):
    return jnp.dot(left, right, preferred_element_type=jnp.float32)


def split(value):
    high = value.astype(jnp.bfloat16)
    return high, (value - high.astype(jnp.float32)).astype(jnp.bfloat16)


def split_three(value):
    high, rest = split(value)
    low = value - high.astype(jnp.float32) - rest.astype(jnp.float32)
    return high, rest, low.astype(jnp.bfloat16)


def exact(hot, value):
    return sum(dot(hot, term) for term in split_three(value))


def times(left, right):
    return dot(left[0], right[0]) + (dot(left[0], right[1]) + dot(left[1], right[0]))


def hot_of(column, lanes):
    number = lax.broadcasted_iota(jnp.int32, (column.shape[0], lanes), 1)
    return jnp.where(column == number, 1.0, 0.0).astype(jnp.bfloat16)


def blocks(total, step, body):
    def one(n, carry):
        body(pl.multiple_of(n * step, step))
        return carry

    lax.fori_loop(0, total // step, one, 0)


ROWS, BODY, TAIL = 256, 288, 176
LAG, X_ROWS = 3.5, 48
QUARTERS = 1


def panels_kernel(
    m_ref, pick_ref, fold_ref, perm_ref, pack_ref, place_ref, linv_ref, uinv_ref, out_ref,
    old, pack_box, place_box, outbox, inbox, g, hot, linv, uinv, t, u, rest, lower0, lower1, low0, low1, solved,
    box_sem, move_sem, old_sem, ring_send, ring_recv, spread_sem0, spread_sem1,
):
    x, z, col = lax.axis_index("x"), lax.axis_index("z"), lax.axis_index("pcol")
    me = x * NZ + z
    count = NX * NZ
    width = linv_ref.shape[1]
    part = width // count
    top = 2 * part
    row_blocks, chunks = m_ref.shape[:2]
    rows, columns = row_blocks * part, chunks * width
    size = 2 * width // NZ
    tail = rows - top
    spread0 = Spread(lower0, 0, x, z, col, spread_sem0)
    spread1 = Spread(lower1, 1, x, z, col, spread_sem1)
    started = []

    others = [lax.rem(me + n, count) for n in range(1, count)]
    barrier = pltpu.get_barrier_semaphore()
    greeted = [(o // NZ, lax.rem(o, NZ), col) for o in others]
    greeted += [(x, z, spread0.mate), (x, z, spread0.up), (x, z, spread0.down)]
    for device in greeted:
        pl.semaphore_signal(barrier, inc=1, device_id=device, device_id_type=MESH)

    for c in range(chunks):
        old[pl.ds(x, 1), :, c * width : (c + 1) * width] = m_ref[0:2, c].reshape(1, top, width)
    pick_hot = hot_of(pick_ref[...], rows)
    tile = width // NX
    for c in range(chunks):
        picked = exact(pick_hot, m_ref[:, c].reshape(rows, width))
        for xs in range(NX):
            outbox[xs * NZ : (xs + 1) * NZ, :, c * tile : (c + 1) * tile] = picked[
                :, xs * tile : (xs + 1) * tile
            ].reshape(NZ, -1, tile)
    inbox[pl.ds(me, 1)] = outbox[pl.ds(me, 1)]
    pl.semaphore_wait(barrier, len(greeted))

    def send(src, dst, send_sem, recv_sem, device):
        copy = pltpu.make_async_remote_copy(
            src_ref=src, dst_ref=dst, send_sem=send_sem, recv_sem=recv_sem, device_id=device, device_id_type=MESH
        )
        copy.start()
        started.append(copy)

    for o in others:
        send(outbox.at[o], inbox.at[me], box_sem.at[0, o], box_sem.at[1, me], (o // NZ, lax.rem(o, NZ), col))
    for d in range(1, NX):
        to = lax.rem(x + d, NX)
        send(old.at[x], old.at[x], old_sem.at[0, to], old_sem.at[1, x], (to, z, col))

    def arrive(view, sem):
        pltpu.make_async_remote_copy(
            src_ref=view, dst_ref=view, send_sem=sem, recv_sem=sem, device_id=(lax.rem(x + 1, NX), z, col),
            device_id_type=MESH,
        ).wait_recv()

    for d in range(1, NX):
        xs = lax.rem(x + d, NX)
        arrive(old.at[xs], old_sem.at[1, xs])
    pack_hot = hot_of(pack_ref[...], NX * top)
    for c in range(0, columns, width):
        packed = exact(pack_hot, old[:, :, c : c + width].reshape(NX * top, width))
        pack_box[:, :, c : c + width] = packed.reshape(NZ, -1, width)
    place_box[pl.ds(z, 1)] = pack_box[pl.ds(z, 1)]
    for o in others:
        arrive(inbox.at[o], box_sem.at[1, o])
    fold_hot = hot_of(fold_ref[...], count * CLASS_ROWS)
    for c in range(chunks):
        mine = exact(fold_hot, inbox[:, :, c * tile : (c + 1) * tile].reshape(count * CLASS_ROWS, tile))
        g[c, pl.ds(x, 1), pl.ds(z, 1)] = mine[None, None]

    pieces, work = [], []
    for c in range(chunks):
        for number, (first, low, high) in enumerate((("x", 0, X_ROWS), ("z", X_ROWS, size))):
            s = 2 * c + number
            pieces.append(Piece(g.at[c], low, high, first, x, z, col, ring_send.at[s], ring_recv.at[s]))
    flow = []
    for number, piece in enumerate(pieces):
        for place, (when, step) in enumerate(piece.steps()):
            flow.append((when + LAG * (number // 2) if when else -1.0, number, place, number // 2, step))
    flow.sort(key=lambda entry: entry[:3])
    for _ in range(2):
        flow.pop(0)[4]()
    for d in range(1, NZ):
        to = lax.rem(z + d, NZ)
        send(pack_box.at[to], place_box.at[z], move_sem.at[0, to], move_sem.at[1, z], (x, to, col))
    for _ in range(2 * chunks - 2):
        flow.pop(0)[4]()

    def prepare():
        for k in range(2):
            linv[k, 0], linv[k, 1] = split(linv_ref[k])
            uinv[k, 0], uinv[k, 1] = split(uinv_ref[k])

        def perm(r):
            hot[pl.ds(r, 128)] = hot_of(perm_ref[pl.ds(r, 128), :], 2 * width)

        blocks(2 * width, 128, perm)

    def place_moved():
        for d in range(1, NZ):
            zs = lax.rem(z + d, NZ)
            arrive(place_box.at[zs], move_sem.at[1, zs])
        column = place_ref[...]
        place_hot = hot_of(column[top:], NZ * MOVED_ROWS)
        for c in range(chunks):
            cols = slice(c * width, (c + 1) * width)
            moved = exact(place_hot, place_box[:, :, cols].reshape(NZ * MOVED_ROWS, width))
            rest[width:, cols] = jnp.where(column[top:] >= 0, moved, m_ref[2:, c].reshape(tail, width))

    def permute(c):
        whole = jnp.concatenate([g[c, n].reshape(2 * width, tile) for n in range(NX)], axis=1)
        high, middle = split(whole)

        def body(r):
            left = hot[pl.ds(r, ROWS)]
            first, second = dot(left, high), dot(left, middle)
            t[0, pl.ds(r, ROWS)] = first.astype(jnp.bfloat16)
            t[1, pl.ds(r, ROWS)] = second.astype(jnp.bfloat16)

            @pl.when(r >= width)
            def _():
                rest[pl.ds(r - width, ROWS), c * width : (c + 1) * width] = first + second

        blocks(2 * width, ROWS, body)

    def own(ref):
        return ref[pl.ds(pl.multiple_of(me * part, part), part)]

    def solve0(c):
        right = t[0, 0:width], t[1, 0:width]
        cols = slice(c * width, (c + 1) * width)

        def body(r):
            value = times((linv[0, 0, pl.ds(r, ROWS)], linv[0, 1, pl.ds(r, ROWS)]), right)
            u[0, 0, pl.ds(r, ROWS), cols], u[0, 1, pl.ds(r, ROWS), cols] = split(value)
            solved[pl.ds(r, ROWS)] = value

        blocks(width, ROWS, body)
        out_ref[0, c] = own(solved)
        if c == 0:

            @pl.when(col == 0)
            def _():
                out_ref[0, c] = own(t.at[0]).astype(jnp.float32) + own(t.at[1]).astype(jnp.float32)
                u[0, :, :, cols] = jnp.zeros((2, width, width), jnp.bfloat16)

    def find_lower0():
        @pl.when(col == 0)
        def _():
            right = uinv[0, 0], uinv[0, 1]

            def body(r):
                lower0[pl.ds(r, BODY)] = times(split(rest[pl.ds(r, BODY), 0:width]), right)

            blocks(width + tail, BODY, body)

    def split_lower(source, target):
        def body(r):
            target[0, pl.ds(r, 32)], target[1, pl.ds(r, 32)] = split(source[pl.ds(r, 32)])

        blocks(source.shape[0], 32, body)

    def reduce0(c):
        cols = slice(c * width, (c + 1) * width)
        right = u[0, 0, :, cols], u[0, 1, :, cols]

        def body(r):
            rest[pl.ds(r, BODY), cols] -= times((low0[0, pl.ds(r, BODY)], low0[1, pl.ds(r, BODY)]), right)

        blocks(width + tail, BODY, body)

    def find_lower1():
        right = uinv[1, 0], uinv[1, 1]

        def body(r):
            lower1[pl.ds(r, TAIL)] = times(split(rest[pl.ds(width + r, TAIL), 0:width]), right)

        blocks(tail, TAIL, body)

    def solve1(c):
        cols = slice(c * width, (c + 1) * width)
        right = split(rest[0:width, cols])

        def body(r):
            value = times((linv[1, 0, pl.ds(r, ROWS)], linv[1, 1, pl.ds(r, ROWS)]), right)
            u[1, 0, pl.ds(r, ROWS), cols], u[1, 1, pl.ds(r, ROWS), cols] = split(value)
            solved[pl.ds(r, ROWS)] = value

        blocks(width, ROWS, body)
        out_ref[1, c] = own(solved)
        if c == 0:

            @pl.when(col <= 1)
            def _():
                mine = jnp.where(col == 0, own(lower0), rest[pl.ds(pl.multiple_of(me * part, part), part), cols])
                out_ref[1, c] = mine
                u[1, :, :, cols] = jnp.zeros((2, width, width), jnp.bfloat16)

    def reduce1(c):
        cols = slice(c * width, (c + 1) * width)
        right = u[1, 0, :, cols], u[1, 1, :, cols]

        def body(r):
            value = rest[pl.ds(width + r, TAIL), cols] - times((low1[0, pl.ds(r, TAIL)], low1[1, pl.ds(r, TAIL)]), right)
            if c == 0:
                value = jnp.where(col == 0, lower0[pl.ds(width + r, TAIL)], jnp.where(col == 1, lower1[pl.ds(r, TAIL)], value))
            out_ref[pl.ds(2 + r // part, TAIL // part), c] = value.reshape(TAIL // part, part, width)

        blocks(tail, TAIL, body)

    def left_of(stage):
        return max([n + 1 for n, entry in enumerate(flow) if entry[3] <= stage], default=0)

    def mix(stage, actions):
        total = left_of(stage)
        done = 0
        for number, action in enumerate(actions):
            until = (number + 1) * total // (len(actions) + 1)
            for _ in range(until - done):
                flow.pop(0)[4]()
            done = until
            action()
        for _ in range(total - done):
            flow.pop(0)[4]()

    P_ = functools.partial
    def lower_arrives():
        spread0.finish()
        split_lower(lower0, low0)
        reduce0(0)

    def early():
        @pl.when(col == 1)
        def _():
            lower_arrives()
            find_lower1()

        spread1.begin()

    def late():
        pl.when(col != 1)(lower_arrives)

    mix(0, [prepare, place_moved])
    permute(0)
    find_lower0()
    spread0.begin()
    solve0(0)
    early()
    mix(1, [spread0.relay])
    mix(2, [P_(permute, 1), P_(solve0, 1), late, spread1.relay, P_(reduce0, 1), P_(solve1, 0)])
    permute(2)
    solve0(2)
    reduce0(2)
    solve1(1)
    solve1(2)
    spread1.finish()
    split_lower(lower1, low1)
    for c in range(chunks):
        reduce1(c)
    for copy in started:
        copy.wait_send()
    for piece in pieces:
        for copy in piece.started:
            copy.wait_send()
    spread0.close()
    spread1.close()


def two_panels(matrix, plan, lower_inv, upper_inv):
    row_blocks, part, chunks, width = matrix.shape
    rows, columns = row_blocks * part, chunks * width
    count, top, size, tile = NX * NZ, 2 * width // (NX * NZ), 2 * width // NZ, width // NX
    tail = rows - top
    vmem = pl.BlockSpec(memory_space=pltpu.VMEM)
    f32, bf16, dma = jnp.float32, jnp.bfloat16, pltpu.SemaphoreType.DMA
    result = pl.pallas_call(
        panels_kernel,
        out_shape=jax.ShapeDtypeStruct((row_blocks, chunks, part, width), f32),
        in_specs=[vmem] * 8,
        out_specs=vmem,
        scratch_shapes=[
            pltpu.VMEM((NX, top, columns), f32),
            pltpu.VMEM((NZ, MOVED_ROWS, columns), f32),
            pltpu.VMEM((NZ, MOVED_ROWS, columns), f32),
            pltpu.VMEM((count, CLASS_ROWS, columns // NX), f32),
            pltpu.VMEM((count, CLASS_ROWS, columns // NX), f32),
            pltpu.VMEM((chunks, NX, NZ, size, tile), f32),
            pltpu.VMEM((2 * width, 2 * width), bf16),
            pltpu.VMEM((2, 2, width, width), bf16),
            pltpu.VMEM((2, 2, width, width), bf16),
            pltpu.VMEM((2, 2 * width, width), bf16),
            pltpu.VMEM((2, 2, width, columns), bf16),
            pltpu.VMEM((width + tail, columns), f32),
            pltpu.VMEM((width + tail, width), f32),
            pltpu.VMEM((tail, width), f32),
            pltpu.VMEM((2, width + tail, width), bf16),
            pltpu.VMEM((2, tail, width), bf16),
            pltpu.VMEM((width, width), f32),
            dma((2, count)),
            dma((2, NZ)),
            dma((2, NX)),
            dma((2 * chunks, count, 4)),
            dma((2 * chunks, count, 2)),
            dma((2, 2, 3, QUARTERS)),
            dma((2, 2, 3, QUARTERS)),
        ],
        compiler_params=pltpu.CompilerParams(
            collective_id=0, has_side_effects=True, vmem_limit_bytes=62 * 2**20
        ),
        name="two_panels",
    )(matrix.transpose(0, 2, 1, 3), *plan, lower_inv, upper_inv)
    return result.transpose(0, 2, 1, 3)


def local(matrix, pivots, lower_inv, upper_inv):
    row_blocks, row_part, col_blocks, col_part = matrix.shape
    width = lower_inv.shape[1]
    *plan, most = make_plan(pivots, width, row_blocks * row_part)
    return lax.cond(
        most[0, 0] <= 0,
        lambda m, p, a, b, q: two_panels(m, q, a, b),
        lambda m, p, a, b, q: general(m, p, a, b),
        matrix, pivots, lower_inv, upper_inv, plan,
    )


def solution(mesh):
    finer = Mesh(mesh.devices.reshape(NX, NZ, mesh.shape["pcol"]), ("x", "z", "pcol"))
    in_specs = (P(None, PROW, None, "pcol"), P(), P(), P())
    out_specs = P(None, PROW, None, "pcol")
    return jax.shard_map(local, mesh=finer, in_specs=in_specs, out_specs=out_specs, check_vma=False)
```

```python
import functools

import jax
import jax.numpy as jnp
from jax import lax
from jax.experimental import pallas as pl
from jax.experimental.pallas import tpu as pltpu
from jax.sharding import Mesh
from jax.sharding import PartitionSpec as P

PROW = ("x", "z")
MESH = pl.DeviceIdType.MESH
NX, NZ = 4, 8


def in_order(parts, dim):
    shape = list(parts.shape[1:])
    shape[dim] *= parts.shape[0]
    return jnp.moveaxis(parts, 0, dim).reshape(shape)


def to_next(x, axis):
    size = lax.axis_size(axis)
    return lax.ppermute(x, axis, [(n, (n + 1) % size) for n in range(size)])


def gathered_by_axis(x, axis, dim):
    size, me = lax.axis_size(axis), lax.axis_index(axis)

    def turn(n, state):
        parts, block = state
        block = to_next(block, axis)
        return lax.dynamic_update_index_in_dim(parts, block, (me - n + size) % size, 0), block

    parts = lax.dynamic_update_index_in_dim(jnp.zeros((size, *x.shape), x.dtype), x, me, 0)
    return in_order(lax.fori_loop(1, size, turn, (parts, x))[0], dim)


def sum_by_axis(x, axis, dim):
    size, me = lax.axis_size(axis), lax.axis_index(axis)
    width = x.shape[dim] // size

    def term(n):
        return lax.dynamic_slice_in_dim(x, (me - 1 - n + size) % size * width, width, dim)

    return lax.fori_loop(1, size, lambda n, total: to_next(total, axis) + term(n), term(0))


def broadcast(x, axis, root):
    mine = lax.axis_index(axis) == root
    return lax.fori_loop(1, lax.axis_size(axis), lambda n, y: jnp.where(mine, x, to_next(y, axis)), x)


def permutation(pivot_row, offset, panel_width, full_order):
    steps = jnp.arange(panel_width, dtype=jnp.int32)
    anchors = offset + steps
    earlier = steps[None, :] < steps[:, None]
    hits_anchor = (pivot_row[None, :] == anchors[:, None]) & earlier
    chain_from = jnp.max(jnp.where(hits_anchor, steps[None, :], -1), axis=1)
    pointer = jnp.where(chain_from >= 0, chain_from, steps)
    for level in range(max(1, panel_width.bit_length())):
        pointer = pointer[pointer]
    before_value = offset + pointer
    same_target = (pivot_row[None, :] == pivot_row[:, None]) & earlier
    last_before = jnp.max(jnp.where(same_target, steps[None, :], -1), axis=1)
    anchor_value = jnp.where(
        last_before >= 0, before_value[jnp.clip(last_before, 0, panel_width - 1)], pivot_row
    )
    later = steps[None, :] > steps[:, None]
    has_later = jnp.any((pivot_row[None, :] == pivot_row[:, None]) & later, axis=1)
    outside = jnp.logical_not(has_later) & (pivot_row >= offset + panel_width)
    spots = jnp.where(outside, pivot_row, full_order)
    ordering = jnp.arange(full_order, dtype=jnp.int32).at[spots].set(before_value, mode="drop")
    return lax.dynamic_update_slice_in_dim(ordering, anchor_value, offset, 0)


def product(left, right):
    return jnp.dot(left, right, precision=lax.Precision.HIGHEST, preferred_element_type=jnp.float32)


def general(matrix, pivots, lower_inv, upper_inv):
    row_blocks, row_part, col_blocks, col_part = matrix.shape
    panel_width = lower_inv.shape[1]
    panel_count = pivots.shape[0]
    full_order = row_blocks * panel_width
    row_devices = lax.axis_size(PROW)
    col_devices = lax.axis_size("pcol")
    row_index = lax.axis_index(PROW)
    col_index = lax.axis_index("pcol")
    local_rows = row_blocks * row_part
    local_cols = col_blocks * col_part
    share_width = local_cols // row_devices
    current = matrix.reshape(local_rows, local_cols)
    global_rows = (
        jnp.arange(row_blocks, dtype=jnp.int32)[:, None] * panel_width
        + row_index * row_part
        + jnp.arange(row_part, dtype=jnp.int32)[None, :]
    ).reshape(local_rows)
    col_span = col_devices * col_part
    global_cols = (
        jnp.arange(col_blocks, dtype=jnp.int32)[:, None] * col_span
        + col_index * col_part
        + jnp.arange(col_part, dtype=jnp.int32)[None, :]
    ).reshape(local_cols)

    def panel(panel_index, current):
        offset = panel_index * panel_width
        ending = offset + panel_width
        ordering = permutation(pivots[panel_index], offset, panel_width, full_order)
        source = ordering[global_rows]
        old_top = lax.dynamic_slice_in_dim(current, panel_index * row_part, row_part, 0)
        old_panel = gathered_by_axis(old_top, PROW, 0)
        wanted = ordering[offset + jnp.arange(panel_width, dtype=jnp.int32)]
        holder = wanted % panel_width // row_part
        local_spot = wanted // panel_width * row_part + wanted % row_part
        picked = jnp.where((holder == row_index)[:, None], current[local_spot], 0.0)
        column_share = sum_by_axis(picked, PROW, 1)
        share_cols = lax.dynamic_slice_in_dim(global_cols, row_index * share_width, share_width)
        solved = product(lower_inv[panel_index], column_share)
        merged = jnp.where((share_cols >= ending)[None, :], solved, column_share)
        top_rows = gathered_by_axis(merged, PROW, 1)
        in_panel = global_rows // panel_width == panel_index
        displaced = (source != global_rows) & jnp.logical_not(in_panel)
        from_old = old_panel[jnp.clip(source - offset, 0, panel_width - 1)]
        current = jnp.where(displaced[:, None], from_old, current)
        own_rows = lax.dynamic_slice_in_dim(top_rows, row_index * row_part, row_part, 0)
        current = lax.dynamic_update_slice_in_dim(current, own_rows, panel_index * row_part, 0)
        trailing_row = global_rows >= ending
        trailing_col = global_cols >= ending
        lower_full = product(current[:, :col_part], upper_inv[panel_index])
        lower_here = jnp.where(trailing_row[:, None], lower_full, 0.0)
        lower_rows = broadcast(lower_here, "pcol", panel_index)
        upper_part = jnp.where(trailing_col[None, :], top_rows, 0.0)
        current = current - product(lower_rows, upper_part)
        own_panel = col_index == panel_index
        new_cols = jnp.where(own_panel & trailing_row[:, None], lower_rows, current[:, :col_part])
        return jnp.concatenate([new_cols, current[:, col_part:]], axis=1)

    current = lax.fori_loop(0, panel_count, panel, current)
    return current.reshape(row_blocks, row_part, col_blocks, col_part)


CLASS_ROWS = 8
MOVED_ROWS = 16


def to_column(row):
    n = row.shape[1]
    eye = lax.broadcasted_iota(jnp.int32, (n, n), 0) == lax.broadcasted_iota(jnp.int32, (n, n), 1)
    return jnp.max(jnp.where(eye, row, -1.0), axis=1, keepdims=True)


def lookup(keys, values, wanted):
    return jnp.max(jnp.where(keys == wanted, values, -1.0), axis=0, keepdims=True)


def find(size, keys, values):
    found = jnp.full((size, 1), -1.0, jnp.float32)
    for key, value in zip(keys, values):
        number = lax.broadcasted_iota(jnp.int32, (size, key.shape[1]), 0).astype(jnp.float32)
        found = jnp.maximum(found, jnp.max(jnp.where(number == key, value, -1.0), axis=1, keepdims=True))
    return found.astype(jnp.int32)


def ranks_of(keys, columns, j, i):
    ranks, smaller = [], []
    for k in range(2):
        rank = jnp.sum(jnp.where((columns[k] == keys[k]) & (j < i), 1.0, 0.0), axis=0, keepdims=True)
        if k == 1:
            rank = rank + jnp.sum(jnp.where(columns[0] == keys[1], 1.0, 0.0), axis=0, keepdims=True)
        ranks.append(rank)
        smaller.append(
            sum(jnp.sum(jnp.where(column < keys[k], 1.0, 0.0), axis=0, keepdims=True) for column in columns)
        )
    return ranks, smaller


def plan_kernel(width, piv_row_ref, pick_ref, fold_ref, perm_ref, pack_ref, place_ref, most_ref):
    me = (lax.axis_index("x") * NZ + lax.axis_index("z")).astype(jnp.float32)
    my_x, my_z = lax.axis_index("x").astype(jnp.float32), lax.axis_index("z").astype(jnp.float32)
    part = width // (NX * NZ)
    j = lax.broadcasted_iota(jnp.int32, (width, width), 0).astype(jnp.float32)
    i = lax.broadcasted_iota(jnp.int32, (width, width), 1).astype(jnp.float32)
    i_row = i[:1]
    sources, spots, spot_cols, befores, before_cols = [], [], [], [], []
    for k in range(2):
        offset = float(k * width)
        p_row = piv_row_ref[k : k + 1, :].astype(jnp.float32)
        p_col = to_column(p_row)
        chain = jnp.max(jnp.where((p_col == offset + i) & (j < i), j, -1.0), axis=0, keepdims=True)
        start = jnp.where(chain >= 0.0, chain, i_row)

        def again(state):
            return state[1] > 0.0

        def jump(state):
            pointer = state[0]
            found = lookup(j[:, :1], to_column(pointer), pointer)
            return found, jnp.max(jnp.abs(found - pointer))

        pointer, _ = lax.while_loop(again, jump, (start, jnp.float32(1.0)))
        before = offset + pointer
        before_col = to_column(before)
        same = p_col == p_row
        last = jnp.max(jnp.where(same & (j < i), j, -1.0), axis=0, keepdims=True)
        later = jnp.max(jnp.where(same & (j > i), 1.0, 0.0), axis=0, keepdims=True)
        anchor = jnp.where(last >= 0.0, lookup(j[:, :1], before_col, last), p_row)
        spot = jnp.where((later == 0.0) & (p_row >= offset + width), p_row, -5.0)
        if k == 1:
            moved = lookup(spot_cols[0], before_cols[0], anchor)
            anchor = jnp.where(moved >= 0.0, moved, anchor)
        sources.append(anchor)
        spots.append(spot)
        spot_cols.append(jnp.max(jnp.where(i == j, spot, -5.0), axis=1, keepdims=True))
        befores.append(before)
        before_cols.append(before_col)

    def divided(value, by):
        return jnp.floor(value * (1.0 / by))

    def holder_and_place(source):
        block = divided(source, width)
        within = source - block * width
        holder = divided(within, part)
        return holder, block * part + within - holder * part

    holders, places = zip(*[holder_and_place(source) for source in sources])
    ranks, smaller = ranks_of(holders, [to_column(h) for h in holders], j, i)
    most = jnp.zeros((1, 1), jnp.float32)
    picks, folds, pick_keys, fold_keys = [], [], [], []
    for k in range(2):
        number = smaller[k] + ranks[k]
        at = divided(number, NZ)
        kind = number - at * NZ
        slot = at - divided(smaller[k] - kind + (NZ - 1.0), NZ)
        most = jnp.maximum(most, jnp.max(slot, axis=1, keepdims=True) - (CLASS_ROWS - 1.0))
        good = slot < CLASS_ROWS
        pick_keys.append(jnp.where((holders[k] == me) & good, kind * CLASS_ROWS + slot, -1.0))
        picks.append(places[k])
        fold_keys.append(jnp.where((kind == my_z) & good, at, -1.0))
        folds.append(holders[k] * CLASS_ROWS + slot)
        perm_ref[k * width : (k + 1) * width, :] = to_column(kind * (2 * width // NZ) + at).astype(jnp.int32)
    pick_ref[...] = find(pick_ref.shape[0], pick_keys, picks)
    fold_ref[...] = find(fold_ref.shape[0], fold_keys, folds)

    landed = lookup(spot_cols[0], before_cols[0], befores[1])
    origins = [befores[0], jnp.where(landed >= 0.0, landed, befores[1])]
    taken = lookup(spot_cols[1], spot_cols[1], spots[0])
    targets = [
        jnp.where((spots[0] >= 2.0 * width) & (taken < 0.0), spots[0], -1.0),
        jnp.where(spots[1] >= 2.0 * width, spots[1], -1.0),
    ]
    owners, rows = zip(*[holder_and_place(origin) for origin in origins])
    ends, spot_rows = zip(*[holder_and_place(jnp.maximum(target, 0.0)) for target in targets])
    owner_x = [divided(owner, NZ) for owner in owners]
    owner_z = [owner - x * NZ for owner, x in zip(owners, owner_x)]
    keys = [
        jnp.where(targets[k] >= 0.0, owner_z[k] * (NX * NZ) + ends[k], 2000.0 + i_row + 600.0 * k) for k in range(2)
    ]
    ranks, _ = ranks_of(keys, [to_column(key) for key in keys], j, i)
    pack_keys, packs, place_keys, place_values = [], [], [], []
    for k in range(2):
        most = jnp.maximum(most, jnp.max(ranks[k], axis=1, keepdims=True) - (MOVED_ROWS - 1.0))
        good = (targets[k] >= 0.0) & (ranks[k] < MOVED_ROWS)
        end_x = divided(ends[k], NZ)
        end_z = ends[k] - end_x * NZ
        pack_keys.append(
            jnp.where(good & (owner_z[k] == my_z) & (end_x == my_x), end_z * MOVED_ROWS + ranks[k], -1.0)
        )
        packs.append(owner_x[k] * (2 * part) + rows[k])
        place_keys.append(jnp.where(good & (ends[k] == me), spot_rows[k], -1.0))
        place_values.append(owner_z[k] * MOVED_ROWS + ranks[k])
    pack_ref[...] = find(pack_ref.shape[0], pack_keys, packs)
    place_ref[...] = find(place_ref.shape[0], place_keys, place_values)
    most_ref[...] = jnp.broadcast_to(most, most_ref.shape).astype(jnp.int32)


def make_plan(pivots, width, rows):
    vmem = pl.BlockSpec(memory_space=pltpu.VMEM)
    sizes = [NZ * CLASS_ROWS, 2 * width // NZ, 2 * width, NZ * MOVED_ROWS, rows]
    shapes = [(n, 1) for n in sizes] + [(1, 1)]
    return pl.pallas_call(
        functools.partial(plan_kernel, width),
        out_shape=[jax.ShapeDtypeStruct(shape, jnp.int32) for shape in shapes],
        in_specs=[vmem],
        out_specs=[vmem] * len(shapes),
        name="row_plan",
    )(pivots)


class Piece:
    def __init__(self, buf, low, high, first, x, z, col, send_sem, recv_sem):
        self.buf, self.low, self.high, self.first = buf, low, high, first
        self.x, self.z, self.col = x, z, col
        self.send_sem, self.recv_sem = send_sem, recv_sem
        self.started = []
        self.na, self.nb = (NX, NZ) if first == "x" else (NZ, NX)
        self.a, self.b = (x, z) if first == "x" else (z, x)

    def place(self, da, db):
        a, b = lax.rem(self.a + da + self.na, self.na), lax.rem(self.b + db + self.nb, self.nb)
        return (a, b) if self.first == "x" else (b, a)

    def copy(self, da, db, to, half, k):
        bx, bz = self.place(da, db)
        middle = (self.low + self.high) // 16 * 8
        low, high = ((self.low, self.high), (self.low, middle), (middle, self.high))[0 if half is None else half + 1]
        view = self.buf.at[bx, bz, low:high]
        return pltpu.make_async_remote_copy(
            src_ref=view,
            dst_ref=view,
            send_sem=self.send_sem.at[bx * NZ + bz, k],
            recv_sem=self.recv_sem.at[bx * NZ + bz, half or 0],
            device_id=self.place(*to) + (self.col,),
            device_id_type=MESH,
        )

    def send(self, da, db, to, half, k):
        copy = self.copy(da, db, to, half, k)
        copy.start()
        self.started.append(copy)

    def receive(self, da, db, half):
        self.copy(da, db, (0, 1), half, 0).wait_recv()

    def along_first(self, d):
        for s in (1, -1):
            if d + 1 <= self.na // 2:
                half = None if d + 1 < self.na // 2 else (1 - s) // 2
                self.send(-s * d, 0, (s, 0), half, (1 - s) // 2)

    def along_second(self, da, d):
        for s in (1, -1):
            if d + 1 <= self.nb // 2:
                half = None if d + 1 < self.nb // 2 else (1 - s) // 2
                self.send(da, -s * d, (0, s), half, (1 - s) // 2 + (2 if d == 0 else 0))

    def first_step(self, d):
        if d == 0:
            self.along_first(0)
            self.along_second(0, 0)
        elif d < self.na // 2:
            for s in (1, -1):
                self.receive(-s * d, 0, None)
            self.along_first(d)
            for s in (1, -1):
                self.along_second(-s * d, 0)
        else:
            self.receive(d, 0, 0)
            self.receive(d, 0, 1)
            self.along_second(d, 0)

    def second_step(self, da, d):
        if d < self.nb // 2:
            for s in (1, -1):
                self.receive(da, -s * d, None)
            self.along_second(da, d)
        else:
            self.receive(da, d, 0)
            self.receive(da, d, 1)

    def steps(self):
        work = [(d, functools.partial(self.first_step, d)) for d in range(self.na // 2 + 1)]
        for d in range(1, self.nb // 2 + 1):
            for ad in range(self.na // 2 + 1):
                for da in [0] if ad == 0 else [ad] if ad == self.na // 2 else [-ad, ad]:
                    work.append((ad + d + 0.5, functools.partial(self.second_step, da, d)))
        return work


class Several:
    def __init__(self, copies):
        self.copies = copies

    def start(self):
        for copy in self.copies:
            copy.start()

    def wait_send(self):
        for copy in self.copies:
            copy.wait_send()

    def wait_recv(self):
        for copy in self.copies:
            copy.wait_recv()


class Spread:
    def __init__(self, buf, root, x, z, col, sems):
        self.buf, self.root, self.x, self.z, self.col, self.sems = buf, root, x, z, col, sems
        y, self.core = col // 2, lax.rem(col, 2)
        self.mate = y * 2 + 1 - self.core
        self.up = lax.rem(y + 1, 4) * 2 + self.core
        self.down = lax.rem(y + 3, 4) * 2 + self.core
        self.away = lax.rem(y - root // 2 + 4, 4)

    def copy(self, half, device, k, pair):
        return Several([self.one(half, n, device, k, pair) for n in range(QUARTERS)])

    def one(self, half, n, device, k, pair):
        rows = self.buf.shape[0] // 16 * 8
        low = half * rows
        high = self.buf.shape[0] if half else rows
        cut = [low + (high - low) * m // (8 * QUARTERS) * 8 for m in range(QUARTERS)] + [high]
        view = self.buf.at[cut[n] : cut[n + 1]]
        return pltpu.make_async_remote_copy(
            src_ref=view,
            dst_ref=view,
            send_sem=self.sems.at[0, half, k, n],
            recv_sem=self.sems.at[1, half, pair, n],
            device_id=(self.x, self.z, device),
            device_id_type=MESH,
        )

    def sends(self, hops):
        up = [self.copy(half, self.up, 0, 0) for half in ((0, 1) if hops == 0 else (0,) if hops == 1 else ())]
        down = [self.copy(half, self.down, 1, 0) for half in ((1, 0) if hops == 0 else (1,) if hops == 3 else ())]
        return up, down

    def pass_on(self, half):
        self.copy(half, self.up, 0, 0).wait_recv()
        self.copy(half, self.mate, 2, 1).start()

    def at(self, hops, action):
        pl.when((self.core == self.root % 2) & (self.away == hops))(action)

    def begin(self):
        @pl.when(self.col == self.root)
        def _():
            up, down = self.sends(0)
            for n in range(2):
                self.copy(n, self.mate, 2, 1).start()
                up[n].start()
                down[n].start()

    def relay(self):
        for hops, half in ((1, 0), (3, 1)):

            def action(hops=hops, half=half):
                self.copy(half, self.up, 0, 0).wait_recv()
                for copy in sum(self.sends(hops), []):
                    copy.start()
                self.copy(half, self.mate, 2, 1).start()

            self.at(hops, action)

    def finish(self):
        self.at(1, functools.partial(self.pass_on, 1))
        self.at(3, functools.partial(self.pass_on, 0))

        def both():
            self.pass_on(0)
            self.pass_on(1)

        self.at(2, both)

        @pl.when(self.core != self.root % 2)
        def _():
            for half in range(2):
                self.copy(half, self.mate, 2, 1).wait_recv()

    def close(self):
        for hops in range(4):

            def action(hops=hops):
                for copy in sum(self.sends(hops), []):
                    copy.wait_send()
                for half in range(2):
                    self.copy(half, self.mate, 2, 1).wait_send()

            self.at(hops, action)


def dot(left, right):
    return jnp.dot(left, right, preferred_element_type=jnp.float32)


def split(value):
    high = value.astype(jnp.bfloat16)
    return high, (value - high.astype(jnp.float32)).astype(jnp.bfloat16)


def split_three(value):
    high, rest = split(value)
    low = value - high.astype(jnp.float32) - rest.astype(jnp.float32)
    return high, rest, low.astype(jnp.bfloat16)


def exact(hot, value):
    return sum(dot(hot, term) for term in split_three(value))


def times(left, right):
    return dot(left[0], right[0]) + (dot(left[0], right[1]) + dot(left[1], right[0]))


def hot_of(column, lanes):
    number = lax.broadcasted_iota(jnp.int32, (column.shape[0], lanes), 1)
    return jnp.where(column == number, 1.0, 0.0).astype(jnp.bfloat16)


def blocks(total, step, body):
    def one(n, carry):
        body(pl.multiple_of(n * step, step))
        return carry

    lax.fori_loop(0, total // step, one, 0)


ROWS, BODY, TAIL = 256, 288, 176
LAG, X_ROWS = 3.5, 48
QUARTERS = 1


def panels_kernel(
    m_ref, pick_ref, fold_ref, perm_ref, pack_ref, place_ref, linv_ref, uinv_ref, out_ref,
    old, pack_box, place_box, outbox, inbox, g, hot, linv, uinv, t, u, rest, lower0, lower1, low0, low1, solved,
    box_sem, move_sem, old_sem, ring_send, ring_recv, spread_sem0, spread_sem1,
):
    x, z, col = lax.axis_index("x"), lax.axis_index("z"), lax.axis_index("pcol")
    me = x * NZ + z
    count = NX * NZ
    width = linv_ref.shape[1]
    part = width // count
    top = 2 * part
    row_blocks, chunks = m_ref.shape[:2]
    rows, columns = row_blocks * part, chunks * width
    size = 2 * width // NZ
    tail = rows - top
    spread0 = Spread(lower0, 0, x, z, col, spread_sem0)
    spread1 = Spread(lower1, 1, x, z, col, spread_sem1)
    started = []

    others = [lax.rem(me + n, count) for n in range(1, count)]
    barrier = pltpu.get_barrier_semaphore()
    greeted = [(o // NZ, lax.rem(o, NZ), col) for o in others]
    greeted += [(x, z, spread0.mate), (x, z, spread0.up), (x, z, spread0.down)]
    for device in greeted:
        pl.semaphore_signal(barrier, inc=1, device_id=device, device_id_type=MESH)

    for c in range(chunks):
        old[pl.ds(x, 1), :, c * width : (c + 1) * width] = m_ref[0:2, c].reshape(1, top, width)
    pick_hot = hot_of(pick_ref[...], rows)
    tile = width // NX
    for c in range(chunks):
        picked = exact(pick_hot, m_ref[:, c].reshape(rows, width))
        for xs in range(NX):
            outbox[xs * NZ : (xs + 1) * NZ, :, c * tile : (c + 1) * tile] = picked[
                :, xs * tile : (xs + 1) * tile
            ].reshape(NZ, -1, tile)
    inbox[pl.ds(me, 1)] = outbox[pl.ds(me, 1)]
    pl.semaphore_wait(barrier, len(greeted))

    def send(src, dst, send_sem, recv_sem, device):
        copy = pltpu.make_async_remote_copy(
            src_ref=src, dst_ref=dst, send_sem=send_sem, recv_sem=recv_sem, device_id=device, device_id_type=MESH
        )
        copy.start()
        started.append(copy)

    for o in others:
        send(outbox.at[o], inbox.at[me], box_sem.at[0, o], box_sem.at[1, me], (o // NZ, lax.rem(o, NZ), col))
    for d in range(1, NX):
        to = lax.rem(x + d, NX)
        send(old.at[x], old.at[x], old_sem.at[0, to], old_sem.at[1, x], (to, z, col))

    def arrive(view, sem):
        pltpu.make_async_remote_copy(
            src_ref=view, dst_ref=view, send_sem=sem, recv_sem=sem, device_id=(lax.rem(x + 1, NX), z, col),
            device_id_type=MESH,
        ).wait_recv()

    for d in range(1, NX):
        xs = lax.rem(x + d, NX)
        arrive(old.at[xs], old_sem.at[1, xs])
    pack_hot = hot_of(pack_ref[...], NX * top)
    for c in range(0, columns, width):
        packed = exact(pack_hot, old[:, :, c : c + width].reshape(NX * top, width))
        pack_box[:, :, c : c + width] = packed.reshape(NZ, -1, width)
    place_box[pl.ds(z, 1)] = pack_box[pl.ds(z, 1)]
    for o in others:
        arrive(inbox.at[o], box_sem.at[1, o])
    fold_hot = hot_of(fold_ref[...], count * CLASS_ROWS)
    for c in range(chunks):
        mine = exact(fold_hot, inbox[:, :, c * tile : (c + 1) * tile].reshape(count * CLASS_ROWS, tile))
        g[c, pl.ds(x, 1), pl.ds(z, 1)] = mine[None, None]

    pieces, work = [], []
    for c in range(chunks):
        for number, (first, low, high) in enumerate((("x", 0, X_ROWS), ("z", X_ROWS, size))):
            s = 2 * c + number
            pieces.append(Piece(g.at[c], low, high, first, x, z, col, ring_send.at[s], ring_recv.at[s]))
    flow = []
    for number, piece in enumerate(pieces):
        for place, (when, step) in enumerate(piece.steps()):
            flow.append((when + LAG * (number // 2) if when else -1.0, number, place, number // 2, step))
    flow.sort(key=lambda entry: entry[:3])
    for _ in range(2):
        flow.pop(0)[4]()
    for d in range(1, NZ):
        to = lax.rem(z + d, NZ)
        send(pack_box.at[to], place_box.at[z], move_sem.at[0, to], move_sem.at[1, z], (x, to, col))
    for _ in range(2 * chunks - 2):
        flow.pop(0)[4]()

    def prepare():
        for k in range(2):
            linv[k, 0], linv[k, 1] = split(linv_ref[k])
            uinv[k, 0], uinv[k, 1] = split(uinv_ref[k])

        def perm(r):
            hot[pl.ds(r, 128)] = hot_of(perm_ref[pl.ds(r, 128), :], 2 * width)

        blocks(2 * width, 128, perm)

    def place_moved():
        for d in range(1, NZ):
            zs = lax.rem(z + d, NZ)
            arrive(place_box.at[zs], move_sem.at[1, zs])
        column = place_ref[...]
        place_hot = hot_of(column[top:], NZ * MOVED_ROWS)
        for c in range(chunks):
            cols = slice(c * width, (c + 1) * width)
            moved = exact(place_hot, place_box[:, :, cols].reshape(NZ * MOVED_ROWS, width))
            rest[width:, cols] = jnp.where(column[top:] >= 0, moved, m_ref[2:, c].reshape(tail, width))

    def permute(c, begin=0, end=2 * width):
        whole = jnp.concatenate([g[c, n].reshape(2 * width, tile) for n in range(NX)], axis=1)
        high, middle = split(whole)

        def body(n):
            r = pl.multiple_of(begin + n, ROWS)
            left = hot[pl.ds(r, ROWS)]
            first, second = dot(left, high), dot(left, middle)
            t[0, pl.ds(r, ROWS)] = first.astype(jnp.bfloat16)
            t[1, pl.ds(r, ROWS)] = second.astype(jnp.bfloat16)

            @pl.when(r >= width)
            def _():
                rest[pl.ds(r - width, ROWS), c * width : (c + 1) * width] = first + second

        blocks(end - begin, ROWS, body)

    def own(ref):
        return ref[pl.ds(pl.multiple_of(me * part, part), part)]

    def solve0(c):
        right = t[0, 0:width], t[1, 0:width]
        cols = slice(c * width, (c + 1) * width)

        def body(r):
            value = times((linv[0, 0, pl.ds(r, ROWS)], linv[0, 1, pl.ds(r, ROWS)]), right)
            u[0, 0, pl.ds(r, ROWS), cols], u[0, 1, pl.ds(r, ROWS), cols] = split(value)
            solved[pl.ds(r, ROWS)] = value

        blocks(width, ROWS, body)
        out_ref[0, c] = own(solved)
        if c == 0:

            @pl.when(col == 0)
            def _():
                out_ref[0, c] = own(t.at[0]).astype(jnp.float32) + own(t.at[1]).astype(jnp.float32)
                u[0, :, :, cols] = jnp.zeros((2, width, width), jnp.bfloat16)

    def find_lower0():
        @pl.when(col == 0)
        def _():
            right = uinv[0, 0], uinv[0, 1]

            def body(r):
                lower0[pl.ds(r, BODY)] = times(split(rest[pl.ds(r, BODY), 0:width]), right)

            blocks(width + tail, BODY, body)

    def split_lower(source, target):
        def body(r):
            target[0, pl.ds(r, 32)], target[1, pl.ds(r, 32)] = split(source[pl.ds(r, 32)])

        blocks(source.shape[0], 32, body)

    def reduce0(c):
        cols = slice(c * width, (c + 1) * width)
        right = u[0, 0, :, cols], u[0, 1, :, cols]

        def body(r):
            rest[pl.ds(r, BODY), cols] -= times((low0[0, pl.ds(r, BODY)], low0[1, pl.ds(r, BODY)]), right)

        blocks(width + tail, BODY, body)

    def find_lower1():
        right = uinv[1, 0], uinv[1, 1]

        def body(r):
            lower1[pl.ds(r, TAIL)] = times(split(rest[pl.ds(width + r, TAIL), 0:width]), right)

        blocks(tail, TAIL, body)

    def solve1(c):
        cols = slice(c * width, (c + 1) * width)
        right = split(rest[0:width, cols])

        def body(r):
            value = times((linv[1, 0, pl.ds(r, ROWS)], linv[1, 1, pl.ds(r, ROWS)]), right)
            u[1, 0, pl.ds(r, ROWS), cols], u[1, 1, pl.ds(r, ROWS), cols] = split(value)
            solved[pl.ds(r, ROWS)] = value

        blocks(width, ROWS, body)
        out_ref[1, c] = own(solved)
        if c == 0:

            @pl.when(col <= 1)
            def _():
                mine = jnp.where(col == 0, own(lower0), rest[pl.ds(pl.multiple_of(me * part, part), part), cols])
                out_ref[1, c] = mine
                u[1, :, :, cols] = jnp.zeros((2, width, width), jnp.bfloat16)

    def reduce1(c):
        cols = slice(c * width, (c + 1) * width)
        right = u[1, 0, :, cols], u[1, 1, :, cols]

        def body(r):
            value = rest[pl.ds(width + r, TAIL), cols] - times((low1[0, pl.ds(r, TAIL)], low1[1, pl.ds(r, TAIL)]), right)
            if c == 0:
                value = jnp.where(col == 0, lower0[pl.ds(width + r, TAIL)], jnp.where(col == 1, lower1[pl.ds(r, TAIL)], value))
            out_ref[pl.ds(2 + r // part, TAIL // part), c] = value.reshape(TAIL // part, part, width)

        blocks(tail, TAIL, body)

    def left_of(stage):
        return max([n + 1 for n, entry in enumerate(flow) if entry[3] <= stage], default=0)

    def mix(stage, actions):
        total = left_of(stage)
        done = 0
        for number, action in enumerate(actions):
            until = (number + 1) * total // (len(actions) + 1)
            for _ in range(until - done):
                flow.pop(0)[4]()
            done = until
            action()
        for _ in range(total - done):
            flow.pop(0)[4]()

    P_ = functools.partial
    def lower_arrives():
        spread0.finish()
        split_lower(lower0, low0)
        reduce0(0)

    def early():
        @pl.when(col == 1)
        def _():
            lower_arrives()
            find_lower1()

        spread1.begin()

    def late():
        pl.when(col != 1)(lower_arrives)

    mix(0, [prepare, place_moved])
    permute(0, width, 2 * width)
    find_lower0()
    spread0.begin()
    permute(0, 0, width)
    solve0(0)
    early()
    mix(1, [spread0.relay])
    mix(2, [P_(permute, 1), P_(solve0, 1), late, spread1.relay, P_(reduce0, 1), P_(solve1, 0)])
    permute(2)
    solve0(2)
    reduce0(2)
    solve1(1)
    solve1(2)
    spread1.finish()
    split_lower(lower1, low1)
    for c in range(chunks):
        reduce1(c)
    for copy in started:
        copy.wait_send()
    for piece in pieces:
        for copy in piece.started:
            copy.wait_send()
    spread0.close()
    spread1.close()


def two_panels(matrix, plan, lower_inv, upper_inv):
    row_blocks, part, chunks, width = matrix.shape
    rows, columns = row_blocks * part, chunks * width
    count, top, size, tile = NX * NZ, 2 * width // (NX * NZ), 2 * width // NZ, width // NX
    tail = rows - top
    vmem = pl.BlockSpec(memory_space=pltpu.VMEM)
    f32, bf16, dma = jnp.float32, jnp.bfloat16, pltpu.SemaphoreType.DMA
    result = pl.pallas_call(
        panels_kernel,
        out_shape=jax.ShapeDtypeStruct((row_blocks, chunks, part, width), f32),
        in_specs=[vmem] * 8,
        out_specs=vmem,
        scratch_shapes=[
            pltpu.VMEM((NX, top, columns), f32),
            pltpu.VMEM((NZ, MOVED_ROWS, columns), f32),
            pltpu.VMEM((NZ, MOVED_ROWS, columns), f32),
            pltpu.VMEM((count, CLASS_ROWS, columns // NX), f32),
            pltpu.VMEM((count, CLASS_ROWS, columns // NX), f32),
            pltpu.VMEM((chunks, NX, NZ, size, tile), f32),
            pltpu.VMEM((2 * width, 2 * width), bf16),
            pltpu.VMEM((2, 2, width, width), bf16),
            pltpu.VMEM((2, 2, width, width), bf16),
            pltpu.VMEM((2, 2 * width, width), bf16),
            pltpu.VMEM((2, 2, width, columns), bf16),
            pltpu.VMEM((width + tail, columns), f32),
            pltpu.VMEM((width + tail, width), f32),
            pltpu.VMEM((tail, width), f32),
            pltpu.VMEM((2, width + tail, width), bf16),
            pltpu.VMEM((2, tail, width), bf16),
            pltpu.VMEM((width, width), f32),
            dma((2, count)),
            dma((2, NZ)),
            dma((2, NX)),
            dma((2 * chunks, count, 4)),
            dma((2 * chunks, count, 2)),
            dma((2, 2, 3, QUARTERS)),
            dma((2, 2, 3, QUARTERS)),
        ],
        compiler_params=pltpu.CompilerParams(
            collective_id=0, has_side_effects=True, vmem_limit_bytes=62 * 2**20
        ),
        name="two_panels",
    )(matrix.transpose(0, 2, 1, 3), *plan, lower_inv, upper_inv)
    return result.transpose(0, 2, 1, 3)


def local(matrix, pivots, lower_inv, upper_inv):
    row_blocks, row_part, col_blocks, col_part = matrix.shape
    width = lower_inv.shape[1]
    *plan, most = make_plan(pivots, width, row_blocks * row_part)
    return lax.cond(
        most[0, 0] <= 0,
        lambda m, p, a, b, q: two_panels(m, q, a, b),
        lambda m, p, a, b, q: general(m, p, a, b),
        matrix, pivots, lower_inv, upper_inv, plan,
    )


def solution(mesh):
    finer = Mesh(mesh.devices.reshape(NX, NZ, mesh.shape["pcol"]), ("x", "z", "pcol"))
    in_specs = (P(None, PROW, None, "pcol"), P(), P(), P())
    out_specs = P(None, PROW, None, "pcol")
    return jax.shard_map(local, mesh=finer, in_specs=in_specs, out_specs=out_specs, check_vma=False)
```
